256 devices in a mesh: gs: 64 (over x, z, core), view: 4 (over y).
Axes of the slice: x: 4, y: 4, z: 8, core: 2. Of those that a mesh axis runs over, the one named last changes fastest.
Arguments:
- sh_coef: float32 [48, 65536], P(None, 'gs'), may hold values from -4 to 4
- opacity_logit: float32 [65536], P('gs'), may hold values from -6 to -1
- view_angle: float32 [4, 2, 65536], P('view', None, 'gs'), may hold values from -3.140625 to 3.140625
- mean_pos: float32 [4, 2, 65536], P('view', None, 'gs'), may hold values from 0.15 to 0.85
- conic: float32 [4, 3, 65536], P('view', None, 'gs'), may hold values from -60 to 100, as said below
- send_slot: int32 [4, 65536], P('view', 'gs'), may hold values from 0 to 2047, as said below
- depth_rank: int32 [4, 65536], P('view', 'gs'), may hold values from 0 to 65535, each once within a row
- target: float32 [4, 256, 3, 1024], P('view', 'gs'), may hold values from 0 to 1
Outputs:
- sh_grad: float32 [48, 65536], P(None, 'gs')
- opacity_grad: float32 [65536], P('gs')
- mean_grad: float32 [4, 2, 65536], P('view', None, 'gs')
- rendered: float32 [4, 256, 3, 1024], P('view', 'gs')
The draws below stay inside these ranges and needn't reach their ends.
Inputs may be any that keep to these rules, and one draw needn't show every extreme that they name: `send_slot`: in each view the 1024 values of one device's Gaussians are distinct, so no block holds more than 8 Gaussians of one device. In every view one block holds 8 Gaussians of every device, and every device fills some block's 8 places. `conic`: xx and yy lie in 8 to 100, and |xy| <= 0.6 sqrt(xx yy).
All inputs are finite; a program needn't handle non-finite values.
Results may differ from the reference program's by a relative error of at most 0.0003.
Values sent between devices are 32-bit elements; how exact they have to be, the bound alone decides.
A program may use at most 64 MiB of HBM per device.

```python
import math
import jax
import jax.numpy as jnp
from jax import lax

SH_TERMS = 16
TILE_PX = 16
QUADS_DEV = 4
G_DEV = 1024
VIEWS = 4
GAUSS = 65536
QUADS = 256
CAPQ = 8
QROWS = 512
QPIX = 1024
N_GS = 64


def draw_conic(key, part):
    key = jax.random.fold_in(key, 7)
    key_first, key_third, key_tilt = jax.random.split(key, 3)
    shape = (VIEWS, GAUSS)
    first = jnp.exp(jax.random.uniform(key_first, shape, jnp.float32, math.log(8.0), math.log(100.0)))
    third = jnp.exp(jax.random.uniform(key_third, shape, jnp.float32, math.log(8.0), math.log(100.0)))
    tilt = jax.random.uniform(key_tilt, shape, jnp.float32, -0.6, 0.6)
    return jnp.stack([first, tilt * jnp.sqrt(first * third), third], axis=1)


def draw_send_slot(key, part):
    key = jax.random.fold_in(key, 13)
    total = 2 * G_DEV
    buckets = total // CAPQ
    slot_ids = jnp.arange(total, dtype=jnp.int32)
    bucket_of = slot_ids // CAPQ

    def one_device(device_key, shared):
        key_own, key_score, key_order = jax.random.split(device_key, 3)
        own_bucket = jax.random.randint(key_own, (), 0, buckets)
        scores = jax.random.randint(key_score, (total,), 0, 2 ** 17) * 4096 + slot_ids
        boosted = jnp.where((bucket_of == own_bucket) | (bucket_of == shared), scores + 2 ** 29, scores)
        chosen = lax.top_k(boosted, G_DEV)[1]
        return jax.random.permutation(key_order, chosen).astype(jnp.int32)

    def one_view(view_key):
        key_shared, key_devices = jax.random.split(view_key)
        shared = jax.random.randint(key_shared, (), 0, buckets)
        device_keys = jax.random.split(key_devices, N_GS)
        picked = jax.vmap(one_device, in_axes=(0, None))(device_keys, shared)
        return picked.reshape(GAUSS)
    return jax.vmap(one_view)(jax.random.split(key, VIEWS))


def shard_levels(key, dims, pieces, smallest, high):
    factor_of = 1.0
    for axis_at, parts in pieces:
        heights = jax.random.uniform(jax.random.fold_in(jax.random.fold_in(key, 6), axis_at), (parts,), jnp.float32, smallest / len(pieces), high / len(pieces))
        factor_of = factor_of * jnp.repeat(jnp.exp(heights), dims[axis_at] // parts).reshape((-1,) + (1,) * (len(dims) - 1 - axis_at))
    return factor_of


def noise(rng, dims, deviation, limit, cuts=(), kind=jnp.bfloat16):
    drawn = deviation * jax.random.normal(rng, dims, jnp.float32)
    if cuts:
        drawn = drawn * shard_levels(rng, dims, cuts, -0.22, 0.18)
    return jnp.clip(drawn, -limit, limit).astype(kind)


def setup_inputs(seed: int = 0) -> dict:
    key_of = jax.random.split(jax.random.key(seed), 9)
    sh_coef = noise(key_of[0], (3 * SH_TERMS, GAUSS), 0.3, 4.0, ((1, 64),), jnp.float32)
    opacity_logit = jnp.clip(-6.0 + 5.0 * jax.random.uniform(key_of[1], (GAUSS,), jnp.float32) ** shard_levels(key_of[1], (GAUSS,), ((0, 64),), -0.2, 0.2), -6.0, -1.0)
    view_angle = jnp.clip(jax.random.uniform(key_of[2], (VIEWS, 2, GAUSS), jnp.float32, -3.140625, 3.140625), -3.140625, 3.140625)
    mean_pos = jnp.clip(0.15 + 0.70000002 * jax.random.uniform(key_of[3], (VIEWS, 2, GAUSS), jnp.float32) ** shard_levels(key_of[3], (VIEWS, 2, GAUSS), ((0, 4), (2, 64)), -0.2, 0.2), 0.15, 0.85)
    conic = draw_conic(jax.random.fold_in(key_of[8], 71), 0)
    send_slot = draw_send_slot(jax.random.fold_in(key_of[8], 71), 0)
    depth_rank = jax.vmap(lambda own: jax.random.permutation(own, GAUSS))(jax.random.split(key_of[6], VIEWS)).reshape((VIEWS, GAUSS)).astype(jnp.int32)
    target = jnp.clip(1.0 * jax.random.uniform(key_of[7], (VIEWS, QUADS, 3, QPIX), jnp.float32) ** shard_levels(key_of[7], (VIEWS, QUADS, 3, QPIX), ((0, 4), (1, 64)), -0.2, 0.2), 0.0, 1.0)
    return dict(sh_coef=sh_coef, opacity_logit=opacity_logit, view_angle=view_angle, mean_pos=mean_pos, conic=conic, send_slot=send_slot, depth_rank=depth_rank, target=target)


SH_ZERO = 0.28209479177387814
SH_ONE = 0.4886025119029199
SH_TWO = (1.0925484305920792, -1.0925484305920792, 0.31539156525252005, -1.0925484305920792, 0.5462742152960396)
SH_THREE = (-0.5900435899266435, 2.890611442640554, -0.4570457994644658, 0.3731763325901154, -0.4570457994644658, 1.445305721320277, -0.5900435899266435)
SSIM_MEAN = 0.0001
SSIM_SPREAD = 0.0009
HIGHEST = lax.Precision.HIGHEST

def unit_dirs(angles):
    polar = angles[0]
    azimuth = angles[1]
    return jnp.stack([jnp.sin(polar) * jnp.cos(azimuth), jnp.sin(polar) * jnp.sin(azimuth), jnp.cos(polar)])

def sh_basis(direction):
    coord_x, coord_y, coord_z = (direction[0], direction[1], direction[2])
    square_x = coord_x * coord_x
    square_y = coord_y * coord_y
    square_z = coord_z * coord_z
    terms = [SH_ZERO * jnp.ones_like(coord_x), -SH_ONE * coord_y, SH_ONE * coord_z, -SH_ONE * coord_x, SH_TWO[0] * coord_x * coord_y, SH_TWO[1] * coord_y * coord_z, SH_TWO[2] * (2.0 * square_z - square_x - square_y), SH_TWO[3] * coord_x * coord_z, SH_TWO[4] * (square_x - square_y), SH_THREE[0] * coord_y * (3.0 * square_x - square_y), SH_THREE[1] * coord_x * coord_y * coord_z, SH_THREE[2] * coord_y * (4.0 * square_z - square_x - square_y), SH_THREE[3] * coord_z * (2.0 * square_z - 3.0 * square_x - 3.0 * square_y), SH_THREE[4] * coord_x * (4.0 * square_z - square_x - square_y), SH_THREE[5] * coord_z * (square_x - square_y), SH_THREE[6] * coord_x * (square_x - 3.0 * square_y)]
    return jnp.stack(terms)

def shade(coeffs, harmonics):
    return 0.5 + lax.optimization_barrier(jnp.sum(coeffs.reshape(harmonics.shape[0], 3, -1) * harmonics[:, None, :], axis=0))

def pixel_grid(quad_side):
    pixels = jnp.arange(quad_side * quad_side, dtype=jnp.int32)
    across = ((pixels % quad_side).astype(jnp.float32) + 0.5) / quad_side
    downward = ((pixels // quad_side).astype(jnp.float32) + 0.5) / quad_side
    return (across, downward)

def render(colors, centers, conics, opacity, depth_order, across, downward):
    offset_u = across[None, :] - centers[0][:, None]
    offset_w = downward[None, :] - centers[1][:, None]
    quadratic = 0.5 * (conics[0][:, None] * offset_u * offset_u + 2.0 * conics[1][:, None] * offset_u * offset_w + conics[2][:, None] * offset_w * offset_w)
    alphas = opacity[:, None] * jnp.exp(-quadratic)
    before = (depth_order[None, :] < depth_order[:, None]).astype(jnp.float32)
    log_pass = jnp.dot(before, jnp.log1p(-alphas), precision=HIGHEST)
    weights = jnp.exp(log_pass) * alphas
    return jnp.dot(colors, weights, precision=HIGHEST)

def quad_loss(picture, target, quad_side):

    def block_mean(values):
        return values.reshape(3, quad_side // 4, 4, quad_side // 4, 4).mean(axis=(2, 4))
    difference = picture - target
    squared = jnp.sum(difference * difference) * (0.8 / 16.0)
    mean_x = block_mean(picture)
    mean_y = block_mean(target)
    spread_x = block_mean(picture * picture) - mean_x * mean_x
    spread_y = block_mean(target * target) - mean_y * mean_y
    joint = block_mean(picture * target) - mean_x * mean_y
    ssim_value = (2.0 * mean_x * mean_y + SSIM_MEAN) * (2.0 * joint + SSIM_SPREAD) / ((mean_x * mean_x + mean_y * mean_y + SSIM_MEAN) * (spread_x + spread_y + SSIM_SPREAD))
    return squared + 0.2 * jnp.sum(1.0 - ssim_value)

def quad_grads(colorize, coeffs, geometry, depth_order, target, across, downward, quad_side):

    def forward(coef_in, center_in, opacity_in):
        picture = render(colorize(coef_in), center_in, geometry[2:5], opacity_in, depth_order, across, downward)
        return (picture, quad_loss(picture, target, quad_side))
    (picture, loss_value), pullback = jax.vjp(forward, coeffs, geometry[0:2], geometry[5])
    grad_coef, grad_center, grad_opacity = pullback((jnp.zeros_like(picture), jnp.ones_like(loss_value)))
    return (picture, jnp.concatenate([grad_coef, grad_center, grad_opacity[None]], axis=0))

def keep_colors(values):
    return values

def reference(sh_coef, opacity_logit, view_angle, mean_pos, conic, send_slot, depth_rank, target):
    quad_side = 2 * TILE_PX
    across, downward = pixel_grid(quad_side)
    sigmoid_value = jax.nn.sigmoid(opacity_logit)
    opacity = 0.99 * sigmoid_value
    source = jnp.arange(GAUSS, dtype=jnp.int32) // G_DEV

    def quad_step(inputs):
        payload, order_row, target_quad = inputs
        return quad_grads(keep_colors, payload[0:3], payload[3:9], order_row[0], target_quad, across, downward, quad_side)
    sh_total = jnp.zeros(sh_coef.shape, jnp.float32)
    logit_total = jnp.zeros(opacity_logit.shape, jnp.float32)
    mean_grads = []
    pictures = []
    for view_index in range(VIEWS):
        harmonics = sh_basis(unit_dirs(view_angle[view_index]))
        payload = jnp.concatenate([shade(sh_coef, harmonics), mean_pos[view_index], conic[view_index], opacity[None]], axis=0)
        slot_index = send_slot[view_index]
        owner = slot_index // (QUADS_DEV * CAPQ)
        block_index = owner * QUADS_DEV + slot_index // CAPQ % QUADS_DEV
        row_index = source * CAPQ + slot_index % CAPQ
        buffer = jnp.zeros((QUADS, 9, QROWS), jnp.float32).at[block_index, :, row_index].set(payload.T)
        orders = jnp.full((QUADS, 1, QROWS), -1, jnp.int32).at[block_index, 0, row_index].set(depth_rank[view_index].astype(jnp.int32))
        images, grads = lax.map(quad_step, (buffer, orders, target[view_index]))
        returned = grads[block_index, :, row_index].T
        grad_color = returned[0:3]
        sh_total = sh_total + (harmonics[:, None, :] * grad_color[None, :, :]).reshape(sh_coef.shape)
        logit_total = logit_total + returned[5] * 0.99 * sigmoid_value * (1.0 - sigmoid_value)
        mean_grads.append(returned[3:5])
        pictures.append(images)
    return (sh_total, logit_total, jnp.stack(mean_grads), jnp.stack(pictures))
```

```python
import jax
import jax.numpy as jnp
from jax import lax
from jax.experimental import pallas as pl
from jax.experimental.pallas import tpu as pltpu
from jax.sharding import PartitionSpec as P

F32 = jnp.float32
BF16 = jnp.bfloat16

SH_ZERO = 0.28209479177387814
SH_ONE = 0.4886025119029199
SH_TWO = (
    1.0925484305920792,
    -1.0925484305920792,
    0.31539156525252005,
    -1.0925484305920792,
    0.5462742152960396,
)
SH_THREE = (
    -0.5900435899266435,
    2.890611442640554,
    -0.4570457994644658,
    0.3731763325901154,
    -0.4570457994644658,
    1.445305721320277,
    -0.5900435899266435,
)
SSIM_MEAN = 0.0001
SSIM_SPREAD = 0.0009

GS = 64
VIEWS = 4
QUADS = 4
CAP = 8
G = 1024
PLACES = GS * CAP
PIX = 1024
TILES = PIX // 128
WIDE = 16
OPA, COL, KEY = 6, 7, 10
BACK = 8
HIGHEST = lax.Precision.HIGHEST


def iota(shape, axis):
    return lax.broadcasted_iota(jnp.int32, shape, axis)


def sh_basis(polar, azimuth):
    across = jnp.sin(polar)
    x = across * jnp.cos(azimuth)
    y = across * jnp.sin(azimuth)
    z = jnp.cos(polar)
    xx, yy, zz = x * x, y * y, z * z
    return [
        jnp.full_like(x, SH_ZERO),
        -SH_ONE * y,
        SH_ONE * z,
        -SH_ONE * x,
        SH_TWO[0] * x * y,
        SH_TWO[1] * y * z,
        SH_TWO[2] * (2.0 * zz - xx - yy),
        SH_TWO[3] * x * z,
        SH_TWO[4] * (xx - yy),
        SH_THREE[0] * y * (3.0 * xx - yy),
        SH_THREE[1] * x * y * z,
        SH_THREE[2] * y * (4.0 * zz - xx - yy),
        SH_THREE[3] * z * (2.0 * zz - 3.0 * xx - 3.0 * yy),
        SH_THREE[4] * x * (4.0 * zz - xx - yy),
        SH_THREE[5] * z * (xx - yy),
        SH_THREE[6] * x * (xx - 3.0 * yy),
    ]


def three_parts(values):
    high = values.astype(BF16).astype(F32)
    rest = values - high
    middle = rest.astype(BF16).astype(F32)
    return high, middle, rest - middle


def centre(mean):
    return mean * 32.0 - 16.5


def pack_kernel(sh_ref, logit_ref, angle_ref, mean_ref, conic_ref, slot_ref, rank_ref, out_ref, pay):
    basis = sh_basis(angle_ref[0:1, :], angle_ref[1:2, :])
    colour = jnp.full((3, G), 0.5, F32)
    for k in range(16):
        colour = colour + sh_ref[3 * k : 3 * k + 3, :] * basis[k]
    m, n = centre(mean_ref[0:1, :]), centre(mean_ref[1:2, :])
    scale = 1.0 / 1024.0
    a, b, c = (conic_ref[k : k + 1, :] * scale for k in range(3))
    pay[...] = jnp.zeros((WIDE, G), F32)
    pay[0:1, :] = -0.5 * (a * m * m + 2.0 * b * m * n + c * n * n)
    pay[1:2, :] = a * m + b * n
    pay[2:3, :] = b * m + c * n
    pay[3:4, :] = -0.5 * a
    pay[4:5, :] = -b
    pay[5:6, :] = -0.5 * c
    pay[OPA : OPA + 1, :] = 0.99 * jax.nn.sigmoid(logit_ref[...])
    pay[COL : COL + 3, :] = colour
    pay[KEY : KEY + 1, :] = (rank_ref[...] + 1).astype(F32)
    parts = three_parts(pay[...])
    slot = slot_ref[...]
    owner = jnp.where(iota((GS, G), 0) == (slot >> 5), 1.0, 0.0).astype(BF16)
    place = slot & 31
    for q in range(QUADS):
        total = jnp.zeros((GS, 128), F32)
        for part in parts[::-1]:
            spread = jnp.concatenate(
                [jnp.where(place == q * CAP + cap, part, 0.0) for cap in range(CAP)], axis=0
            ).astype(BF16)
            total = total + lax.dot_general(
                owner, spread, (((1,), (1,)), ((), ())), preferred_element_type=F32
            )
        out_ref[:, q, :] = total


def monomials():
    lane = iota((WIDE, 128), 1)
    row = iota((WIDE, 128), 0)
    u = ((lane & 31) - 16).astype(F32)
    w = ((lane >> 5) - 16).astype(F32)

    def rows(entries):
        out = jnp.zeros((WIDE, 128), F32)
        for k, value in entries.items():
            out = jnp.where(row == k, value, out)
        return out

    tiles = [
        rows({0: 1.0, 1: u, 2: w, 3: u * u, 4: u * w, 5: w * w}),
        rows({2: 4.0, 4: 4.0 * u, 5: 8.0 * w + 16.0}),
        rows({5: 32.0}),
        rows({OPA: 1.0}),
        rows({COL: 1.0}),
        rows({COL + 1: 1.0}),
        rows({COL + 2: 1.0}),
    ]
    base = jnp.concatenate(tiles, axis=1)
    pad = jnp.zeros((128 - 3 * WIDE, base.shape[1]), F32)
    return jnp.concatenate([base, base, base, pad], axis=0).astype(BF16)


def loss_slope(x, y):
    lane = iota((128, 128), 1)
    other = iota((128, 128), 0)
    same = ((lane & 31) >> 2) == ((other & 31) >> 2)
    pool = jnp.where(same, 1.0 / 16.0, 0.0)
    rows = x.shape[0]
    means = jnp.dot(
        jnp.concatenate([x, y, x * x, y * y, x * y], axis=0),
        pool,
        precision=HIGHEST,
        preferred_element_type=F32,
    )
    mx, my, exx, eyy, exy = (means[k * rows : (k + 1) * rows] for k in range(5))
    n1 = 2.0 * mx * my + SSIM_MEAN
    n2 = 2.0 * (exy - mx * my) + SSIM_SPREAD
    d1 = mx * mx + my * my + SSIM_MEAN
    d2 = (exx - mx * mx) + (eyy - my * my) + SSIM_SPREAD
    i1, i2 = 1.0 / d1, 1.0 / d2
    both = i1 * i2
    ratio = n1 * n2 * both
    by_mean = 2.0 * my * (n2 - n1) * both + 2.0 * mx * ratio * (i2 - i1)
    by_square = -ratio * i2
    by_cross = 2.0 * n1 * both
    return 0.1 * (x - y) - (0.2 / 16.0) * (by_mean + 2.0 * x * by_square + y * by_cross)


def render_kernel(arr_ref, tgt_ref, img_ref, ret_ref, xq, rq, perm, bc, a_s, w_s, tg, gr, pic, tgt, slope, mono):
    mono[...] = monomials()
    for q in range(QUADS):
        xq[q] = arr_ref[:, q, :]
    sub = iota((8, PIX), 0)

    def shifted(values, by, fill):
        keep = (sub >= by) if by > 0 else (sub < 8 + by)
        return jnp.where(keep, pltpu.roll(values, by % 8, 0), fill)

    def block(q, carry):
        x = xq[q]
        turned = x.T
        keys = jnp.concatenate(
            [turned[c * WIDE + KEY : c * WIDE + KEY + 1, :] for c in range(CAP)], axis=1
        )
        count = jnp.zeros((8, PLACES), F32)
        for c in range(CAP):
            column = x[:, c * WIDE + KEY : c * WIDE + KEY + 1]
            less = jnp.where(column < keys, 1.0, 0.0)
            count = count + jnp.sum(less.reshape(8, 8, PLACES), axis=0)
        rank = jnp.sum(count, axis=0, keepdims=True)
        filled = jnp.sum(jnp.where(keys > 0.0, 1.0, 0.0)).astype(jnp.int32)
        run = ((filled + 15) // 16) * 2
        at = iota((PLACES, 128), 0)
        step = at >> 3
        wanted = (at & 7) * run + step + (PLACES - filled)
        wanted = jnp.where(step < run, wanted, -1).astype(F32)
        for t in range(PLACES // 128):
            here = rank[:, t * 128 : (t + 1) * 128]
            perm[:, t * 128 : (t + 1) * 128] = jnp.where(here == wanted, 1.0, 0.0).astype(BF16)
        parts = three_parts(x)
        lane = iota((GS, 128), 1)
        gathered = []
        for c in range(CAP):
            turn = [pltpu.roll(parts[k], (WIDE * (k - c)) % 128, 1) for k in range(3)]
            gathered.append(
                jnp.where(
                    lane < WIDE,
                    turn[0],
                    jnp.where(lane < 2 * WIDE, turn[1], jnp.where(lane < 3 * WIDE, turn[2], 0.0)),
                )
            )
        payload = jnp.concatenate(gathered, axis=0).astype(BF16)
        ordered = jnp.dot(perm[...], payload, preferred_element_type=F32).astype(BF16)
        bc[...] = jnp.dot(ordered, mono[...], preferred_element_type=F32)

        def ahead(i, carry):
            passing, seen = list(carry[0]), [list(s) for s in carry[1]]
            rows = pl.ds(pl.multiple_of(i * 8, 8), 8)
            power, first, second, opacity, c0, c1, c2 = (
                bc[rows, k * 128 : (k + 1) * 128] for k in range(7)
            )
            for t in range(TILES):
                alpha = opacity * jnp.exp(power)
                weight = passing[t] * alpha
                passing[t] = passing[t] - weight
                a_s[rows, t * 128 : (t + 1) * 128] = alpha
                w_s[rows, t * 128 : (t + 1) * 128] = weight
                for k, colour in enumerate((c0, c1, c2)):
                    seen[k][t] = seen[k][t] + colour * weight
                power = power + first
                first = first + second
            return tuple(passing), tuple(tuple(s) for s in seen)

        one = jnp.ones((8, 128), F32)
        zero = jnp.zeros((8, 128), F32)
        start = ((one,) * TILES, ((zero,) * TILES,) * 3)
        passing, seen = lax.fori_loop(
            0, run // 2, lambda i, s: ahead(2 * i + 1, ahead(2 * i, s)), start
        )
        left = jnp.concatenate(passing, axis=1)
        seen = [jnp.concatenate(s, axis=1) for s in seen]
        before = shifted(left, 1, 1.0)
        for by in (1, 2, 4):
            before = before * shifted(before, by, 1.0)
        for k in range(3):
            image = jnp.sum(before * seen[k], axis=0, keepdims=True)
            img_ref[q, k : k + 1, :] = image
            for t in range(TILES):
                pic[k * 8 + t : k * 8 + t + 1, :] = image[:, t * 128 : (t + 1) * 128]
                tgt[k * 8 + t : k * 8 + t + 1, :] = tgt_ref[q, k : k + 1, t * 128 : (t + 1) * 128]
        slope[...] = loss_slope(pic[...], tgt[...])
        behind = jnp.zeros((8, PIX), F32)
        for k in range(3):
            row = jnp.concatenate([slope[k * 8 + t : k * 8 + t + 1, :] for t in range(TILES)], axis=1)
            behind = behind + row * seen[k]
            tg[k] = before * row
        value, factor = shifted(behind, -1, 0.0), shifted(left, -1, 0.0)
        for by in (1, 2, 4):
            value = value + factor * shifted(value, -by, 0.0)
            factor = factor * shifted(factor, -by, 0.0)
        value = before * value
        gr[...] = jnp.zeros((PLACES, 128), F32)
        lane8 = iota((8, 128), 1)
        across = ((lane8 & 31) - 16).astype(F32)
        down = ((lane8 >> 5) - 16).astype(F32)
        slot = lane8 & 7

        def back(i, later):
            later = list(later)
            rows = pl.ds(pl.multiple_of(i * 8, 8), 8)
            c0, c1, c2 = (bc[rows, k * 128 : (k + 1) * 128] for k in (4, 5, 6))
            plain, graded = zero, zero
            colours = [zero, zero, zero]
            for t in range(TILES - 1, -1, -1):
                cols = slice(t * 128, (t + 1) * 128)
                alpha, weight = a_s[rows, cols], w_s[rows, cols]
                g0, g1, g2 = (tg[k, :, cols] for k in range(3))
                gap = c0 * g0 + c1 * g1 + c2 * g2 - later[t]
                later[t] = later[t] + alpha * gap
                plain = plain + weight * gap
                if t:
                    graded = graded + plain
                colours = [colours[0] + weight * g0, colours[1] + weight * g1, colours[2] + weight * g2]
            sums = colours + [plain * across, plain * down + 4.0 * graded, plain]
            out = zero
            for k, value in enumerate(sums):
                out = jnp.where(slot == k, jnp.sum(value, axis=1, keepdims=True), out)
            gr[rows, :] = out
            return tuple(later)

        lax.fori_loop(
            0,
            run // 2,
            lambda i, s: back(run - 2 - 2 * i, back(run - 1 - 2 * i, s)),
            tuple(value[:, t * 128 : (t + 1) * 128] for t in range(TILES)),
        )
        grads = gr[...]
        high = grads.astype(BF16)
        low = (grads - high.astype(F32)).astype(BF16)
        placed = lax.dot_general(
            perm[...],
            jnp.concatenate([high, low], axis=1),
            (((0,), (0,)), ((), ())),
            preferred_element_type=F32,
        )
        placed = placed[:, 0:128] + placed[:, 128:256]
        group = iota((GS, 128), 1) >> 3
        total = jnp.zeros((GS, 128), F32)
        for c in range(CAP):
            total = jnp.where(group == (q & 1) * 8 + c, placed[c * GS : (c + 1) * GS, :], total)
        rq[q] = total
        return carry

    lax.fori_loop(0, QUADS, block, 0)
    for j in range(QUADS // 2):
        ret_ref[:, j, :] = rq[2 * j] + rq[2 * j + 1]


def unpack_kernel(ret_ref, slot_ref, mean_ref, conic_ref, part_ref, mean_grad_ref):
    slot = slot_ref[...]
    owner = jnp.where(iota((GS, G), 0) == (slot >> 5), 1.0, 0.0).astype(BF16)
    owner = jnp.concatenate([owner] * 3, axis=0)
    place = slot & 31
    total = jnp.zeros((BACK, G), F32)
    for j in range(QUADS // 2):
        parts = jnp.concatenate(three_parts(ret_ref[:, j, :]), axis=0).astype(BF16)
        spread = lax.dot_general(
            parts, owner, (((0,), (0,)), ((), ())), preferred_element_type=F32
        )
        for i in range(16):
            total = jnp.where(place == j * 16 + i, spread[i * BACK : (i + 1) * BACK, :], total)
    m, n = centre(mean_ref[0:1, :]), centre(mean_ref[1:2, :])
    a, b, c = (conic_ref[k : k + 1, :] * (1.0 / 32.0) for k in range(3))
    plain = total[5:6, :]
    du = total[3:4, :] - m * plain
    dw = total[4:5, :] - n * plain
    part_ref[0:3, :] = total[0:3, :]
    part_ref[3:4, :] = plain
    mean_grad_ref[0:1, :] = a * du + b * dw
    mean_grad_ref[1:2, :] = b * du + c * dw


def final_kernel(part_ref, angle_ref, logit_ref, sh_ref, logit_grad_ref):
    plain = part_ref[0, 3:4, :]
    for v in range(1, VIEWS):
        plain = plain + part_ref[v, 3:4, :]
    logit_grad_ref[...] = plain * (1.0 - jax.nn.sigmoid(logit_ref[...]))
    polar = jnp.concatenate([angle_ref[v, 0:1, :] for v in range(VIEWS)], axis=0)
    azimuth = jnp.concatenate([angle_ref[v, 1:2, :] for v in range(VIEWS)], axis=0)
    basis = sh_basis(polar, azimuth)
    for k in range(16):
        total = part_ref[0, 0:3, :] * basis[k][0:1, :]
        for v in range(1, VIEWS):
            total = total + part_ref[v, 0:3, :] * basis[k][v : v + 1, :]
        sh_ref[3 * k : 3 * k + 3, :] = total


VM = pl.BlockSpec(memory_space=pltpu.VMEM)


def call(kernel, ins, outs, scratch=(), limit=48):
    single = not isinstance(outs, list)
    shapes = [outs] if single else outs
    got = pl.pallas_call(
        kernel,
        out_shape=[jax.ShapeDtypeStruct(s, F32) for s in shapes],
        in_specs=[VM] * len(ins),
        out_specs=[VM] * len(shapes),
        scratch_shapes=list(scratch),
        compiler_params=pltpu.CompilerParams(vmem_limit_bytes=limit * 2**20),
    )(*ins)
    return got[0] if single else got


def pack(sh_coef, logit, angle, mean, conic, slot, rank):
    return call(
        pack_kernel,
        [sh_coef, logit, angle, mean, conic, slot, rank],
        (GS, QUADS, 128),
        [pltpu.VMEM((WIDE, G), F32)],
    )


def render(arrived, target):
    return call(
        render_kernel,
        [arrived, target],
        [(QUADS, 3, PIX), (GS, QUADS // 2, 128)],
        [
            pltpu.VMEM((QUADS, GS, 128), F32),
            pltpu.VMEM((QUADS, GS, 128), F32),
            pltpu.VMEM((PLACES, PLACES), BF16),
            pltpu.VMEM((PLACES, 7 * 128), F32),
            pltpu.VMEM((PLACES, PIX), F32),
            pltpu.VMEM((PLACES, PIX), F32),
            pltpu.VMEM((3, 8, PIX), F32),
            pltpu.VMEM((PLACES, 128), F32),
            pltpu.VMEM((24, 128), F32),
            pltpu.VMEM((24, 128), F32),
            pltpu.VMEM((24, 128), F32),
            pltpu.VMEM((128, 7 * 128), BF16),
        ],
    )


def unpack(back, slot, mean, conic):
    return call(unpack_kernel, [back, slot, mean, conic], [(4, G), (2, G)])


def final(parts, angles, logit):
    return call(final_kernel, [parts, angles, logit], [(48, G), (1, G)])


def local(sh_coef, opacity_logit, view_angle, mean_pos, conic, send_slot, depth_rank, target):
    logit = opacity_logit.reshape(1, G)
    sent = pack(sh_coef, logit, view_angle[0], mean_pos[0], conic[0], send_slot, depth_rank)
    arrived = lax.all_to_all(sent, "gs", split_axis=0, concat_axis=0, tiled=True)
    angles = lax.all_gather(view_angle[0], "view")
    images, back = render(arrived, target[0])
    returned = lax.all_to_all(back, "gs", split_axis=0, concat_axis=0, tiled=True)
    part, mean_grad = unpack(returned, send_slot, mean_pos[0], conic[0])
    parts = lax.all_gather(part, "view")
    sh_grad, logit_grad = final(parts, angles, logit)
    return (sh_grad, logit_grad.reshape(G), mean_grad[None], images[None])


def solution(mesh):
    return jax.shard_map(
        local,
        mesh=mesh,
        in_specs=(
            P(None, "gs"),
            P("gs"),
            P("view", None, "gs"),
            P("view", None, "gs"),
            P("view", None, "gs"),
            P("view", "gs"),
            P("view", "gs"),
            P("view", "gs", None, None),
        ),
        out_specs=(P(None, "gs"), P("gs"), P("view", None, "gs"), P("view", "gs", None, None)),
        check_vma=False,
    )
```

```python
import jax
import jax.numpy as jnp
from jax import lax
from jax.experimental import pallas as pl
from jax.experimental.pallas import tpu as pltpu
from jax.sharding import PartitionSpec as P

F32 = jnp.float32
BF16 = jnp.bfloat16

SH_ZERO = 0.28209479177387814
SH_ONE = 0.4886025119029199
SH_TWO = (
    1.0925484305920792,
    -1.0925484305920792,
    0.31539156525252005,
    -1.0925484305920792,
    0.5462742152960396,
)
SH_THREE = (
    -0.5900435899266435,
    2.890611442640554,
    -0.4570457994644658,
    0.3731763325901154,
    -0.4570457994644658,
    1.445305721320277,
    -0.5900435899266435,
)
SSIM_MEAN = 0.0001
SSIM_SPREAD = 0.0009

GS = 64
VIEWS = 4
QUADS = 4
CAP = 8
G = 1024
PLACES = GS * CAP
PIX = 1024
TILES = PIX // 128
WIDE = 16
OPA, COL, KEY = 6, 7, 10
BACK = 8
HIGHEST = lax.Precision.HIGHEST


def iota(shape, axis):
    return lax.broadcasted_iota(jnp.int32, shape, axis)


def sh_basis(polar, azimuth):
    across = jnp.sin(polar)
    x = across * jnp.cos(azimuth)
    y = across * jnp.sin(azimuth)
    z = jnp.cos(polar)
    xx, yy, zz = x * x, y * y, z * z
    return [
        jnp.full_like(x, SH_ZERO),
        -SH_ONE * y,
        SH_ONE * z,
        -SH_ONE * x,
        SH_TWO[0] * x * y,
        SH_TWO[1] * y * z,
        SH_TWO[2] * (2.0 * zz - xx - yy),
        SH_TWO[3] * x * z,
        SH_TWO[4] * (xx - yy),
        SH_THREE[0] * y * (3.0 * xx - yy),
        SH_THREE[1] * x * y * z,
        SH_THREE[2] * y * (4.0 * zz - xx - yy),
        SH_THREE[3] * z * (2.0 * zz - 3.0 * xx - 3.0 * yy),
        SH_THREE[4] * x * (4.0 * zz - xx - yy),
        SH_THREE[5] * z * (xx - yy),
        SH_THREE[6] * x * (xx - 3.0 * yy),
    ]


def three_parts(values):
    high = values.astype(BF16).astype(F32)
    rest = values - high
    middle = rest.astype(BF16).astype(F32)
    return high, middle, rest - middle


def centre(mean):
    return mean * 32.0 - 16.5


def peers():
    return lax.axis_index("gs"), lax.axis_index("view")


def greet():
    me, view = peers()
    barrier = pltpu.get_barrier_semaphore()

    def one(d, carry):
        pl.semaphore_signal(barrier, inc=1, device_id=(lax.rem(me + d, GS), view), device_id_type=MESH)
        return carry

    lax.fori_loop(1, GS, one, 0)
    for d in range(1, VIEWS):
        pl.semaphore_signal(barrier, inc=1, device_id=(me, lax.rem(view + d, VIEWS)), device_id_type=MESH)


def greeted():
    pl.semaphore_wait(pltpu.get_barrier_semaphore(), GS - 1 + VIEWS - 1)


def deal(sent, got, send_sem, recv_sem):
    me, view = peers()

    def one(d, carry):
        other = lax.rem(me + d, GS)
        pltpu.make_async_remote_copy(
            src_ref=sent.at[other],
            dst_ref=got.at[me],
            send_sem=send_sem,
            recv_sem=recv_sem,
            device_id=(other, view),
            device_id_type=MESH,
        ).start()
        return carry

    lax.fori_loop(1, GS, one, 0)


def spread_views(mine, got, send_sem, recv_sem):
    me, view = peers()
    for d in range(1, VIEWS):
        pltpu.make_async_remote_copy(
            src_ref=mine,
            dst_ref=got.at[view],
            send_sem=send_sem,
            recv_sem=recv_sem,
            device_id=(me, lax.rem(view + d, VIEWS)),
            device_id_type=MESH,
        ).start()


def settle(whole, count, sem):
    part = whole.at[pl.ds(0, count)]
    pltpu.make_async_copy(part, part, sem).wait()


def pack_kernel(
    sh_ref, logit_ref, angle_ref, mean_ref, conic_ref, slot_ref, rank_ref, arr_ref, angles_ref, out_ref, pay, sems
):
    greet()
    me, view = peers()
    angles_ref[view] = angle_ref[...]
    basis = sh_basis(angle_ref[0:1, :], angle_ref[1:2, :])
    colour = jnp.full((3, G), 0.5, F32)
    for k in range(16):
        colour = colour + sh_ref[3 * k : 3 * k + 3, :] * basis[k]
    m, n = centre(mean_ref[0:1, :]), centre(mean_ref[1:2, :])
    scale = 1.0 / 1024.0
    a, b, c = (conic_ref[k : k + 1, :] * scale for k in range(3))
    pay[...] = jnp.zeros((WIDE, G), F32)
    pay[0:1, :] = -0.5 * (a * m * m + 2.0 * b * m * n + c * n * n)
    pay[1:2, :] = a * m + b * n
    pay[2:3, :] = b * m + c * n
    pay[3:4, :] = -0.5 * a
    pay[4:5, :] = -b
    pay[5:6, :] = -0.5 * c
    pay[OPA : OPA + 1, :] = 0.99 * jax.nn.sigmoid(logit_ref[...])
    pay[COL : COL + 3, :] = colour
    pay[KEY : KEY + 1, :] = (rank_ref[...] + 1).astype(F32)
    parts = three_parts(pay[...])
    slot = slot_ref[...]
    owner = jnp.where(iota((GS, G), 0) == (slot >> 5), 1.0, 0.0).astype(BF16)
    place = slot & 31
    for q in range(QUADS):
        total = jnp.zeros((GS, 128), F32)
        for part in parts[::-1]:
            spread = jnp.concatenate(
                [jnp.where(place == q * CAP + cap, part, 0.0) for cap in range(CAP)], axis=0
            ).astype(BF16)
            total = total + lax.dot_general(
                owner, spread, (((1,), (1,)), ((), ())), preferred_element_type=F32
            )
        out_ref[:, q, :] = total
    arr_ref[me] = out_ref[me]
    greeted()
    deal(out_ref, arr_ref, sems.at[0], sems.at[1])
    spread_views(angle_ref, angles_ref, sems.at[2], sems.at[3])
    settle(arr_ref, GS - 1, sems.at[1])
    settle(angles_ref, VIEWS - 1, sems.at[3])
    settle(arr_ref, GS - 1, sems.at[0])
    settle(angles_ref, VIEWS - 1, sems.at[2])


def monomials():
    lane = iota((WIDE, 128), 1)
    row = iota((WIDE, 128), 0)
    u = ((lane & 31) - 16).astype(F32)
    w = ((lane >> 5) - 16).astype(F32)

    def rows(entries):
        out = jnp.zeros((WIDE, 128), F32)
        for k, value in entries.items():
            out = jnp.where(row == k, value, out)
        return out

    tiles = [
        rows({0: 1.0, 1: u, 2: w, 3: u * u, 4: u * w, 5: w * w}),
        rows({2: 4.0, 4: 4.0 * u, 5: 8.0 * w + 16.0}),
        rows({5: 32.0}),
        rows({OPA: 1.0}),
        rows({COL: 1.0}),
        rows({COL + 1: 1.0}),
        rows({COL + 2: 1.0}),
    ]
    base = jnp.concatenate(tiles, axis=1)
    pad = jnp.zeros((128 - 3 * WIDE, base.shape[1]), F32)
    return jnp.concatenate([base, base, base, pad], axis=0).astype(BF16)


def loss_slope(x, y):
    lane = iota((128, 128), 1)
    other = iota((128, 128), 0)
    same = ((lane & 31) >> 2) == ((other & 31) >> 2)
    pool = jnp.where(same, 1.0 / 16.0, 0.0)
    rows = x.shape[0]
    means = jnp.dot(
        jnp.concatenate([x, y, x * x, y * y, x * y], axis=0),
        pool,
        precision=HIGHEST,
        preferred_element_type=F32,
    )
    mx, my, exx, eyy, exy = (means[k * rows : (k + 1) * rows] for k in range(5))
    n1 = 2.0 * mx * my + SSIM_MEAN
    n2 = 2.0 * (exy - mx * my) + SSIM_SPREAD
    d1 = mx * mx + my * my + SSIM_MEAN
    d2 = (exx - mx * mx) + (eyy - my * my) + SSIM_SPREAD
    i1, i2 = 1.0 / d1, 1.0 / d2
    both = i1 * i2
    ratio = n1 * n2 * both
    by_mean = 2.0 * my * (n2 - n1) * both + 2.0 * mx * ratio * (i2 - i1)
    by_square = -ratio * i2
    by_cross = 2.0 * n1 * both
    return 0.1 * (x - y) - (0.2 / 16.0) * (by_mean + 2.0 * x * by_square + y * by_cross)


def render_kernel(arr_ref, tgt_ref, img_ref, ret_ref, xq, rq, perm, bc, a_s, w_s, tg, gr, pic, tgt, slope, mono):
    mono[...] = monomials()
    for q in range(QUADS):
        xq[q] = arr_ref[:, q, :]
    sub = iota((8, PIX), 0)

    def shifted(values, by, fill):
        keep = (sub >= by) if by > 0 else (sub < 8 + by)
        return jnp.where(keep, pltpu.roll(values, by % 8, 0), fill)

    def block(q, carry):
        x = xq[q]
        turned = x.T
        keys = jnp.concatenate(
            [turned[c * WIDE + KEY : c * WIDE + KEY + 1, :] for c in range(CAP)], axis=1
        )
        count = jnp.zeros((8, PLACES), F32)
        for c in range(CAP):
            column = x[:, c * WIDE + KEY : c * WIDE + KEY + 1]
            less = jnp.where(column < keys, 1.0, 0.0)
            count = count + jnp.sum(less.reshape(8, 8, PLACES), axis=0)
        rank = jnp.sum(count, axis=0, keepdims=True)
        filled = jnp.sum(jnp.where(keys > 0.0, 1.0, 0.0)).astype(jnp.int32)
        run = ((filled + 15) // 16) * 2
        at = iota((PLACES, 128), 0)
        step = at >> 3
        wanted = (at & 7) * run + step + (PLACES - filled)
        wanted = jnp.where(step < run, wanted, -1).astype(F32)
        for t in range(PLACES // 128):
            here = rank[:, t * 128 : (t + 1) * 128]
            perm[:, t * 128 : (t + 1) * 128] = jnp.where(here == wanted, 1.0, 0.0).astype(BF16)
        parts = three_parts(x)
        lane = iota((GS, 128), 1)
        gathered = []
        for c in range(CAP):
            turn = [pltpu.roll(parts[k], (WIDE * (k - c)) % 128, 1) for k in range(3)]
            gathered.append(
                jnp.where(
                    lane < WIDE,
                    turn[0],
                    jnp.where(lane < 2 * WIDE, turn[1], jnp.where(lane < 3 * WIDE, turn[2], 0.0)),
                )
            )
        payload = jnp.concatenate(gathered, axis=0).astype(BF16)
        ordered = jnp.dot(perm[...], payload, preferred_element_type=F32).astype(BF16)
        bc[...] = jnp.dot(ordered, mono[...], preferred_element_type=F32)

        def ahead(i, carry):
            passing, seen = list(carry[0]), [list(s) for s in carry[1]]
            rows = pl.ds(pl.multiple_of(i * 8, 8), 8)
            power, first, second, opacity, c0, c1, c2 = (
                bc[rows, k * 128 : (k + 1) * 128] for k in range(7)
            )
            for t in range(TILES):
                alpha = opacity * jnp.exp(power)
                weight = passing[t] * alpha
                passing[t] = passing[t] - weight
                a_s[rows, t * 128 : (t + 1) * 128] = alpha
                w_s[rows, t * 128 : (t + 1) * 128] = weight
                for k, colour in enumerate((c0, c1, c2)):
                    seen[k][t] = seen[k][t] + colour * weight
                power = power + first
                first = first + second
            return tuple(passing), tuple(tuple(s) for s in seen)

        one = jnp.ones((8, 128), F32)
        zero = jnp.zeros((8, 128), F32)
        start = ((one,) * TILES, ((zero,) * TILES,) * 3)
        passing, seen = lax.fori_loop(
            0, run // 2, lambda i, s: ahead(2 * i + 1, ahead(2 * i, s)), start
        )
        left = jnp.concatenate(passing, axis=1)
        seen = [jnp.concatenate(s, axis=1) for s in seen]
        before = shifted(left, 1, 1.0)
        for by in (1, 2, 4):
            before = before * shifted(before, by, 1.0)
        for k in range(3):
            image = jnp.sum(before * seen[k], axis=0, keepdims=True)
            img_ref[q, k : k + 1, :] = image
            for t in range(TILES):
                pic[k * 8 + t : k * 8 + t + 1, :] = image[:, t * 128 : (t + 1) * 128]
                tgt[k * 8 + t : k * 8 + t + 1, :] = tgt_ref[q, k : k + 1, t * 128 : (t + 1) * 128]
        slope[...] = loss_slope(pic[...], tgt[...])
        behind = jnp.zeros((8, PIX), F32)
        for k in range(3):
            row = jnp.concatenate([slope[k * 8 + t : k * 8 + t + 1, :] for t in range(TILES)], axis=1)
            behind = behind + row * seen[k]
            tg[k] = before * row
        value, factor = shifted(behind, -1, 0.0), shifted(left, -1, 0.0)
        for by in (1, 2, 4):
            value = value + factor * shifted(value, -by, 0.0)
            factor = factor * shifted(factor, -by, 0.0)
        value = before * value
        gr[...] = jnp.zeros((PLACES, 128), F32)
        lane8 = iota((8, 128), 1)
        across = ((lane8 & 31) - 16).astype(F32)
        down = ((lane8 >> 5) - 16).astype(F32)
        slot = lane8 & 7

        def back(i, later):
            later = list(later)
            rows = pl.ds(pl.multiple_of(i * 8, 8), 8)
            c0, c1, c2 = (bc[rows, k * 128 : (k + 1) * 128] for k in (4, 5, 6))
            plain, graded = zero, zero
            colours = [zero, zero, zero]
            for t in range(TILES - 1, -1, -1):
                cols = slice(t * 128, (t + 1) * 128)
                alpha, weight = a_s[rows, cols], w_s[rows, cols]
                g0, g1, g2 = (tg[k, :, cols] for k in range(3))
                gap = c0 * g0 + c1 * g1 + c2 * g2 - later[t]
                later[t] = later[t] + alpha * gap
                plain = plain + weight * gap
                if t:
                    graded = graded + plain
                colours = [colours[0] + weight * g0, colours[1] + weight * g1, colours[2] + weight * g2]
            sums = colours + [plain * across, plain * down + 4.0 * graded, plain]
            out = zero
            for k, value in enumerate(sums):
                out = jnp.where(slot == k, jnp.sum(value, axis=1, keepdims=True), out)
            gr[rows, :] = out
            return tuple(later)

        lax.fori_loop(
            0,
            run // 2,
            lambda i, s: back(run - 2 - 2 * i, back(run - 1 - 2 * i, s)),
            tuple(value[:, t * 128 : (t + 1) * 128] for t in range(TILES)),
        )
        grads = gr[...]
        high = grads.astype(BF16)
        low = (grads - high.astype(F32)).astype(BF16)
        placed = lax.dot_general(
            perm[...],
            jnp.concatenate([high, low], axis=1),
            (((0,), (0,)), ((), ())),
            preferred_element_type=F32,
        )
        placed = placed[:, 0:128] + placed[:, 128:256]
        group = iota((GS, 128), 1) >> 3
        total = jnp.zeros((GS, 128), F32)
        for c in range(CAP):
            total = jnp.where(group == (q & 1) * 8 + c, placed[c * GS : (c + 1) * GS, :], total)
        rq[q] = total
        return carry

    lax.fori_loop(0, QUADS, block, 0)
    for j in range(QUADS // 2):
        ret_ref[:, j, :] = rq[2 * j] + rq[2 * j + 1]


def unpack_kernel(sent_ref, slot_ref, mean_ref, conic_ref, parts_ref, mean_grad_ref, ret_ref, part_ref, sems):
    greet()
    me, view = peers()
    ret_ref[me] = sent_ref[me]
    slot = slot_ref[...]
    owner = jnp.where(iota((GS, G), 0) == (slot >> 5), 1.0, 0.0).astype(BF16)
    owner = jnp.concatenate([owner] * 3, axis=0)
    place = slot & 31
    total = jnp.zeros((BACK, G), F32)
    greeted()
    deal(sent_ref, ret_ref, sems.at[0], sems.at[1])
    settle(ret_ref, GS - 1, sems.at[1])
    for j in range(QUADS // 2):
        parts = jnp.concatenate(three_parts(ret_ref[:, j, :]), axis=0).astype(BF16)
        spread = lax.dot_general(
            parts, owner, (((0,), (0,)), ((), ())), preferred_element_type=F32
        )
        for i in range(16):
            total = jnp.where(place == j * 16 + i, spread[i * BACK : (i + 1) * BACK, :], total)
    m, n = centre(mean_ref[0:1, :]), centre(mean_ref[1:2, :])
    a, b, c = (conic_ref[k : k + 1, :] * (1.0 / 32.0) for k in range(3))
    plain = total[5:6, :]
    du = total[3:4, :] - m * plain
    dw = total[4:5, :] - n * plain
    part_ref[0:3, :] = total[0:3, :]
    part_ref[3:4, :] = plain
    spread_views(part_ref, parts_ref, sems.at[2], sems.at[3])
    parts_ref[view] = part_ref[...]
    mean_grad_ref[0:1, :] = a * du + b * dw
    mean_grad_ref[1:2, :] = b * du + c * dw
    settle(parts_ref, VIEWS - 1, sems.at[3])
    settle(ret_ref, GS - 1, sems.at[0])
    settle(parts_ref, VIEWS - 1, sems.at[2])


def final_kernel(part_ref, angle_ref, logit_ref, sh_ref, logit_grad_ref):
    plain = part_ref[0, 3:4, :]
    for v in range(1, VIEWS):
        plain = plain + part_ref[v, 3:4, :]
    logit_grad_ref[...] = plain * (1.0 - jax.nn.sigmoid(logit_ref[...]))
    polar = jnp.concatenate([angle_ref[v, 0:1, :] for v in range(VIEWS)], axis=0)
    azimuth = jnp.concatenate([angle_ref[v, 1:2, :] for v in range(VIEWS)], axis=0)
    basis = sh_basis(polar, azimuth)
    for k in range(16):
        total = part_ref[0, 0:3, :] * basis[k][0:1, :]
        for v in range(1, VIEWS):
            total = total + part_ref[v, 0:3, :] * basis[k][v : v + 1, :]
        sh_ref[3 * k : 3 * k + 3, :] = total


MESH = pl.DeviceIdType.MESH
VM = pl.BlockSpec(memory_space=pltpu.VMEM)


def call(kernel, ins, outs, scratch=(), limit=48, remote=None):
    extra = {} if remote is None else dict(collective_id=remote, has_side_effects=True)
    single = not isinstance(outs, list)
    shapes = [outs] if single else outs
    got = pl.pallas_call(
        kernel,
        out_shape=[jax.ShapeDtypeStruct(s, F32) for s in shapes],
        in_specs=[VM] * len(ins),
        out_specs=[VM] * len(shapes),
        scratch_shapes=list(scratch),
        compiler_params=pltpu.CompilerParams(vmem_limit_bytes=limit * 2**20, **extra),
    )(*ins)
    return got[0] if single else got


def pack(sh_coef, logit, angle, mean, conic, slot, rank):
    return call(
        pack_kernel,
        [sh_coef, logit, angle, mean, conic, slot, rank],
        [(GS, QUADS, 128), (VIEWS, 2, G)],
        [
            pltpu.VMEM((GS, QUADS, 128), F32),
            pltpu.VMEM((WIDE, G), F32),
            pltpu.SemaphoreType.DMA((4,)),
        ],
        remote=0,
    )


def render(arrived, target):
    return call(
        render_kernel,
        [arrived, target],
        [(QUADS, 3, PIX), (GS, QUADS // 2, 128)],
        [
            pltpu.VMEM((QUADS, GS, 128), F32),
            pltpu.VMEM((QUADS, GS, 128), F32),
            pltpu.VMEM((PLACES, PLACES), BF16),
            pltpu.VMEM((PLACES, 7 * 128), F32),
            pltpu.VMEM((PLACES, PIX), F32),
            pltpu.VMEM((PLACES, PIX), F32),
            pltpu.VMEM((3, 8, PIX), F32),
            pltpu.VMEM((PLACES, 128), F32),
            pltpu.VMEM((24, 128), F32),
            pltpu.VMEM((24, 128), F32),
            pltpu.VMEM((24, 128), F32),
            pltpu.VMEM((128, 7 * 128), BF16),
        ],
    )


def unpack(back, slot, mean, conic):
    return call(
        unpack_kernel,
        [back, slot, mean, conic],
        [(VIEWS, 4, G), (2, G)],
        [
            pltpu.VMEM((GS, QUADS // 2, 128), F32),
            pltpu.VMEM((4, G), F32),
            pltpu.SemaphoreType.DMA((4,)),
        ],
        remote=1,
    )


def final(parts, angles, logit):
    return call(final_kernel, [parts, angles, logit], [(48, G), (1, G)])


def local(sh_coef, opacity_logit, view_angle, mean_pos, conic, send_slot, depth_rank, target):
    logit = opacity_logit.reshape(1, G)
    arrived, angles = pack(sh_coef, logit, view_angle[0], mean_pos[0], conic[0], send_slot, depth_rank)
    images, back = render(arrived, target[0])
    parts, mean_grad = unpack(back, send_slot, mean_pos[0], conic[0])
    sh_grad, logit_grad = final(parts, angles, logit)
    return (sh_grad, logit_grad.reshape(G), mean_grad[None], images[None])


def solution(mesh):
    return jax.shard_map(
        local,
        mesh=mesh,
        in_specs=(
            P(None, "gs"),
            P("gs"),
            P("view", None, "gs"),
            P("view", None, "gs"),
            P("view", None, "gs"),
            P("view", "gs"),
            P("view", "gs"),
            P("view", "gs", None, None),
        ),
        out_specs=(P(None, "gs"), P("gs"), P("view", None, "gs"), P("view", "gs", None, None)),
        check_vma=False,
    )
```

```python
import jax
import jax.numpy as jnp
from jax import lax
from jax.experimental import pallas as pl
from jax.experimental.pallas import tpu as pltpu
from jax.sharding import PartitionSpec as P

F32 = jnp.float32
BF16 = jnp.bfloat16

SH_ZERO = 0.28209479177387814
SH_ONE = 0.4886025119029199
SH_TWO = (
    1.0925484305920792,
    -1.0925484305920792,
    0.31539156525252005,
    -1.0925484305920792,
    0.5462742152960396,
)
SH_THREE = (
    -0.5900435899266435,
    2.890611442640554,
    -0.4570457994644658,
    0.3731763325901154,
    -0.4570457994644658,
    1.445305721320277,
    -0.5900435899266435,
)
SSIM_MEAN = 0.0001
SSIM_SPREAD = 0.0009

GS = 64
VIEWS = 4
QUADS = 4
CAP = 8
G = 1024
PLACES = GS * CAP
PIX = 1024
TILES = PIX // 128
WIDE = 16
COL, KEY = 6, 9
BACK = 8
OWN = 7
SHIFT = 64.0
LOG2E = 1.4426950408889634
HALF = 8
PASSES = 8 // HALF
UNROLL = 8
FORMS = 2 * PASSES + 4


def iota(shape, axis):
    return lax.broadcasted_iota(jnp.int32, shape, axis)


def sh_basis(polar, azimuth):
    across = jnp.sin(polar)
    x = across * jnp.cos(azimuth)
    y = across * jnp.sin(azimuth)
    z = jnp.cos(polar)
    xx, yy, zz = x * x, y * y, z * z
    return [
        jnp.full_like(x, SH_ZERO),
        -SH_ONE * y,
        SH_ONE * z,
        -SH_ONE * x,
        SH_TWO[0] * x * y,
        SH_TWO[1] * y * z,
        SH_TWO[2] * (2.0 * zz - xx - yy),
        SH_TWO[3] * x * z,
        SH_TWO[4] * (xx - yy),
        SH_THREE[0] * y * (3.0 * xx - yy),
        SH_THREE[1] * x * y * z,
        SH_THREE[2] * y * (4.0 * zz - xx - yy),
        SH_THREE[3] * z * (2.0 * zz - 3.0 * xx - 3.0 * yy),
        SH_THREE[4] * x * (4.0 * zz - xx - yy),
        SH_THREE[5] * z * (xx - yy),
        SH_THREE[6] * x * (xx - 3.0 * yy),
    ]


def three_parts(values):
    high = values.astype(BF16).astype(F32)
    rest = values - high
    middle = rest.astype(BF16).astype(F32)
    return high, middle, rest - middle


def centre(mean):
    return mean * 32.0 - 16.5


def peers():
    return lax.axis_index("gs"), lax.axis_index("view")


def far_first(me):
    across = [((me // 16 + d) % 4) * 16 for d in range(4)]
    along = [((me // 2 + d) % 8) * 2 for d in range(8)]
    core = [me % 2, 1 - me % 2]
    steps = [(x, z, c) for x in range(4) for z in range(8) for c in range(2)]
    steps.sort(key=lambda s: (-min(s[0], 4 - s[0]) - min(s[1], 8 - s[1]), -s[2]))
    return [across[x] + along[z] + core[c] for x, z, c in steps if (x, z, c) != (0, 0, 0)]


def greet():
    me, view = peers()
    barrier = pltpu.get_barrier_semaphore()
    for other in far_first(me):
        pl.semaphore_signal(barrier, inc=1, device_id=(other, view), device_id_type=MESH)
    for d in range(1, VIEWS):
        pl.semaphore_signal(barrier, inc=1, device_id=(me, lax.rem(view + d, VIEWS)), device_id_type=MESH)


def greeted():
    pl.semaphore_wait(pltpu.get_barrier_semaphore(), GS - 1 + VIEWS - 1)


def deal(sent, got, send_sem, recv_sem):
    me, view = peers()
    for other in far_first(me):
        pltpu.make_async_remote_copy(
            src_ref=sent.at[other],
            dst_ref=got.at[me],
            send_sem=send_sem,
            recv_sem=recv_sem,
            device_id=(other, view),
            device_id_type=MESH,
        ).start()


def spread_views(mine, got, send_sem, recv_sem):
    me, view = peers()
    for d in range(1, VIEWS):
        pltpu.make_async_remote_copy(
            src_ref=mine,
            dst_ref=got.at[view],
            send_sem=send_sem,
            recv_sem=recv_sem,
            device_id=(me, lax.rem(view + d, VIEWS)),
            device_id_type=MESH,
        ).start()


def settle(whole, count, sem):
    part = whole.at[pl.ds(0, count)]
    pltpu.make_async_copy(part, part, sem).wait()


def pack_kernel(*refs):
    far, (arr_ref, angles_ref, own_ref, aim_ref), rest = refs[:8], refs[8:12], refs[12:]
    near, (out_ref, pay, sems, load_sems) = rest[:7], rest[7:]
    loads = [
        pltpu.make_async_copy(src, dst, load_sems.at[k])
        for k, (src, dst) in enumerate(zip(far, (*near, aim_ref)))
    ]
    for load in loads:
        load.start()
    greet()
    for load in loads:
        load.wait()
    sh_ref, logit_ref, angle_ref, mean_ref, conic_ref, slot_ref, rank_ref = near
    me, view = peers()
    angles_ref[view] = angle_ref[...]
    basis = sh_basis(angle_ref[0:1, :], angle_ref[1:2, :])
    colour = jnp.full((3, G), 0.5, F32)
    for k in range(16):
        colour = colour + sh_ref[3 * k : 3 * k + 3, :] * basis[k]
    m, n = centre(mean_ref[0:1, :]), centre(mean_ref[1:2, :])
    kept = [slot_ref[...].astype(F32), m, n] + [conic_ref[k] * (1.0 / 32.0) for k in range(3)]
    for k, row in enumerate(kept + [logit_ref[...]]):
        own_ref[k : k + 1, :] = row
    scale = LOG2E / 1024.0
    opacity = 0.99 * jax.nn.sigmoid(logit_ref[...])
    a, b, c = (conic_ref[k] * scale for k in range(3))
    pay[...] = jnp.zeros((WIDE, G), F32)
    away = 0.5 * (a * m * m + 2.0 * b * m * n + c * n * n)
    pay[0:1, :] = (jnp.log(opacity) * LOG2E + SHIFT) - away
    pay[1:2, :] = a * m + b * n
    pay[2:3, :] = b * m + c * n
    pay[3:4, :] = -0.5 * a
    pay[4:5, :] = -b
    pay[5:6, :] = -0.5 * c
    pay[COL : COL + 3, :] = colour
    pay[KEY : KEY + 1, :] = (rank_ref[...] + 1).astype(F32)
    parts = three_parts(pay[...])
    slot = slot_ref[...]
    owner = jnp.where(iota((GS, G), 0) == (slot >> 5), 1.0, 0.0).astype(BF16)
    place = slot & 31
    for q in range(QUADS):
        total = jnp.zeros((GS, 128), F32)
        for part in parts[::-1]:
            spread = jnp.concatenate(
                [jnp.where(place == q * CAP + cap, part, 0.0) for cap in range(CAP)], axis=0
            ).astype(BF16)
            total = total + lax.dot_general(
                owner, spread, (((1,), (1,)), ((), ())), preferred_element_type=F32
            )
        out_ref[:, q, :] = total
    arr_ref[me] = out_ref[me]
    greeted()
    deal(out_ref, arr_ref, sems.at[0], sems.at[1])
    spread_views(angle_ref, angles_ref, sems.at[2], sems.at[3])
    settle(arr_ref, GS - 1, sems.at[1])
    settle(angles_ref, VIEWS - 1, sems.at[3])
    settle(arr_ref, GS - 1, sems.at[0])
    settle(angles_ref, VIEWS - 1, sems.at[2])


def monomials():
    lane = iota((WIDE, 128), 1)
    row = iota((WIDE, 128), 0)
    u = ((lane & 31) - 16).astype(F32)
    top = ((lane >> 5) - 16).astype(F32)

    def rows(entries):
        out = jnp.zeros((WIDE, 128), F32)
        for k, value in entries.items():
            out = jnp.where(row == k, value, out)
        return out

    def power(w):
        return rows({0: 1.0, 1: u, 2: w, 3: u * u, 4: u * w, 5: w * w})

    def first(w):
        return rows({2: 4.0, 4: 4.0 * u, 5: 8.0 * w + 16.0})

    tiles = []
    for h in range(PASSES):
        tiles += [power(top + 4.0 * HALF * h), first(top + 4.0 * HALF * h)]
    tiles.append(rows({5: 32.0}))
    tiles += [rows({COL + c: 1.0}) for c in range(3)]
    base = jnp.concatenate(tiles, axis=1)
    shift = jnp.where(
        (iota((WIDE, 128), 0) == 0) & (iota((WIDE, 128), 1) >= 0), -SHIFT, 0.0
    )
    none = jnp.zeros((WIDE, 128), F32)
    shift = jnp.concatenate([shift, none] * PASSES + [none] * 4, axis=1)
    return jnp.concatenate([base, base, base, shift], axis=0).astype(BF16)


def loss_slope(x, y):
    lane = iota((128, 128), 1)
    other = iota((128, 128), 0)
    same = ((lane & 31) >> 2) == ((other & 31) >> 2)
    pool = jnp.where(same, 1.0 / 16.0, 0.0).astype(BF16)
    rows = x.shape[0]
    parts = three_parts(jnp.concatenate([x, y, x * x, y * y, x * y], axis=0))
    sums = jnp.dot(
        jnp.concatenate(parts, axis=0).astype(BF16), pool, preferred_element_type=F32
    )
    means = (sums[10 * rows : 15 * rows] + sums[5 * rows : 10 * rows]) + sums[0 : 5 * rows]
    mx, my, exx, eyy, exy = (means[k * rows : (k + 1) * rows] for k in range(5))
    n1 = 2.0 * mx * my + SSIM_MEAN
    n2 = 2.0 * (exy - mx * my) + SSIM_SPREAD
    d1 = mx * mx + my * my + SSIM_MEAN
    d2 = (exx - mx * mx) + (eyy - my * my) + SSIM_SPREAD
    i1, i2 = 1.0 / d1, 1.0 / d2
    both = i1 * i2
    ratio = n1 * n2 * both
    by_mean = 2.0 * my * (n2 - n1) * both + 2.0 * mx * ratio * (i2 - i1)
    by_square = -ratio * i2
    by_cross = 2.0 * n1 * both
    return 0.1 * (x - y) - (0.2 / 16.0) * (by_mean + 2.0 * x * by_square + y * by_cross)


def shifted(values, by, fill):
    sub = iota(values.shape, 0)
    keep = (sub >= by) if by > 0 else (sub < 8 + by)
    return jnp.where(keep, pltpu.roll(values, by % 8, 0), fill)


def order(x, perm, bc, mono, step_s, sub_s):
    turned = x.T
    packed = jnp.concatenate([turned[c * WIDE : (c + 1) * WIDE, :] for c in range(CAP)], axis=1)
    parts = jnp.concatenate(three_parts(packed), axis=0).astype(BF16)
    keys = packed[KEY : KEY + 1, :]
    pick = jnp.where((iota((3 * WIDE, 128), 0) & 15) == KEY, 1.0, 0.0).astype(BF16)
    column = lax.dot_general(parts, pick, (((0,), (0,)), ((), ())), preferred_element_type=F32)
    filled = jnp.sum(jnp.where(keys > 0.0, 1.0, 0.0))
    run = ((filled.astype(jnp.int32) + 8 * UNROLL - 1) // (8 * UNROLL)) * UNROLL
    span = run.astype(F32)
    step = step_s[...]
    wanted = jnp.where(step < span, sub_s[...] * span + step + (PLACES - filled), -1.0)
    for t in range(PLACES // 128):
        less = jnp.where(column < keys[:, tile(t)], 1.0, 0.0)
        rank = jnp.sum(less, axis=0, keepdims=True)
        perm[:, tile(t)] = jnp.where(rank == wanted, 1.0, 0.0).astype(BF16)
    ordered = lax.dot_general(
        parts, perm[...], (((1,), (1,)), ((), ())), preferred_element_type=F32
    )
    ordered = jnp.concatenate([ordered, jnp.ones((WIDE, PLACES), F32)], axis=0).astype(BF16)
    bc[...] = lax.dot_general(
        ordered, mono[...], (((0,), (0,)), ((), ())), preferred_element_type=F32
    )
    return run


def unroll_loop(run, body, start):
    def several(i, state):
        for k in range(UNROLL):
            state = body(i * UNROLL + k, state)
        return state

    return lax.fori_loop(0, run // UNROLL, several, start)


def tile(t):
    return slice(t * 128, (t + 1) * 128)


def blend(run, bc, a_s, w_s, left, seen):
    one = jnp.ones((8, 128), F32)
    zero = jnp.zeros((8, 128), F32)
    for h in range(PASSES):

        def ahead(i, state, h=h):
            passing, got = list(state[0]), [list(s) for s in state[1]]
            rows = pl.ds(pl.multiple_of(i * 8, 8), 8)
            power, first = bc[rows, tile(2 * h)], bc[rows, tile(2 * h + 1)]
            second = bc[rows, tile(2 * PASSES)]
            colours = [bc[rows, tile(2 * PASSES + 1 + c)] for c in range(3)]
            for t in range(HALF):
                alpha = jnp.exp2(power)
                weight = passing[t] * alpha
                passing[t] = passing[t] - weight
                a_s[rows, tile(h * HALF + t)] = alpha
                w_s[rows, tile(h * HALF + t)] = weight
                for c in range(3):
                    got[c][t] = got[c][t] + colours[c] * weight
                if t < HALF - 1:
                    power = power + first
                    first = first + second
            return tuple(passing), tuple(tuple(s) for s in got)

        passing, got = unroll_loop(run, ahead, ((one,) * HALF, ((zero,) * HALF,) * 3))
        for t in range(HALF):
            left[:, tile(h * HALF + t)] = passing[t]
            for c in range(3):
                seen[c, :, tile(h * HALF + t)] = got[c][t]


def backward(run, bc, a_s, w_s, tg, later_s, red):
    zero = jnp.zeros((8, 128), F32)
    for h in range(PASSES - 1, -1, -1):

        def back(i, later, h=h):
            later = list(later)
            rows = pl.ds(pl.multiple_of((run - 1 - i) * 8, 8), 8)
            c0, c1, c2 = (bc[rows, tile(2 * PASSES + 1 + c)] for c in range(3))
            plain, graded = zero, zero
            sums = [zero, zero, zero]
            for t in range(HALF - 1, -1, -1):
                cols = tile(h * HALF + t)
                alpha, weight = a_s[rows, cols], w_s[rows, cols]
                g0, g1, g2 = (tg[c, :, cols] for c in range(3))
                gap = c0 * g0 + c1 * g1 + c2 * g2 - later[t]
                later[t] = later[t] + alpha * gap
                plain = plain + weight * gap
                if t:
                    graded = graded + plain
                sums = [sums[0] + weight * g0, sums[1] + weight * g1, sums[2] + weight * g2]
            if h:
                graded = graded + HALF * h * plain
            sums = sums + [plain, graded]
            for k in range(5):
                if h < PASSES - 1:
                    sums[k] = sums[k] + red[rows, tile(k)]
                red[rows, tile(k)] = sums[k]
            return tuple(later)

        unroll_loop(run, back, tuple(later_s[:, tile(h * HALF + t)] for t in range(HALF)))


def join(left, seen, pic, slope, tgt, tg, later, image):
    before = shifted(left[...], 1, 1.0)
    for by in (1, 2, 4):
        before = before * shifted(before, by, 1.0)
    for c in range(3):
        row = jnp.sum(before * seen[c], axis=0, keepdims=True)
        image[c : c + 1, :] = row
        for t in range(TILES):
            pic[c * 8 + t : c * 8 + t + 1, :] = row[:, tile(t)]
    slope[...] = loss_slope(pic[...], tgt[...])
    behind = jnp.zeros((8, PIX), F32)
    for c in range(3):
        row = jnp.concatenate([slope[c * 8 + t : c * 8 + t + 1, :] for t in range(TILES)], axis=1)
        behind = behind + row * seen[c]
        tg[c] = before * row
    value, factor = shifted(behind, -1, 0.0), shifted(left[...], -1, 0.0)
    for by in (1, 2, 4):
        value = value + factor * shifted(value, -by, 0.0)
        factor = factor * shifted(factor, -by, 0.0)
    later[...] = before * value


def render_kernel(
    arr_ref, tgt_ref, img_ref, red, perm, runs,
    bc, a_s, w_s, left, seen, tg, later, pic, tgt, slope, mono, xq, image, step_s, sub_s
):
    mono[...] = monomials()
    at = iota((PLACES, 128), 0)
    step_s[...] = (at >> 3).astype(F32)
    sub_s[...] = (at & 7).astype(F32)
    for q in range(QUADS):
        xq[q] = arr_ref[:, q, :]
        for c in range(3):
            for t in range(TILES):
                tgt[q, c * 8 + t : c * 8 + t + 1, :] = tgt_ref[c, q : q + 1, tile(t)]

    def block(q, carry):
        run = order(xq[q], perm.at[q], bc, mono, step_s, sub_s)
        blend(run, bc, a_s, w_s, left, seen)
        join(left, seen, pic, slope, tgt.at[q], tg, later, image.at[q])
        backward(run, bc, a_s, w_s, tg, later, red.at[q])
        runs[q] = jnp.full((8, 128), 8 * run, jnp.int32).astype(F32)
        return carry

    lax.fori_loop(0, QUADS, block, 0)
    for q in range(QUADS):
        for c in range(3):
            img_ref[c, q : q + 1, :] = image[q, c : c + 1, :]


def send_back(red_ref, perm_ref, runs_ref, sent, back):
    pixel = iota((128, 128), 0)
    across = ((pixel & 31) - 16).astype(F32)
    down = ((pixel >> 5) - 16).astype(F32)
    row = iota((BACK, 128), 1).astype(F32)

    def block(q, carry):
        groups = []
        for n in range(PLACES // 128):
            g0, g1, g2, plain, graded = (red_ref[q, tile(n), tile(k)].T for k in range(5))
            sums = (g0, g1, g2, plain * across, plain * down + 4.0 * graded, plain)
            sums = [jnp.sum(value, axis=0, keepdims=True) for value in sums]
            sums = jnp.concatenate(sums + [jnp.zeros((BACK - 6, 128), F32)], axis=0)
            groups.append(jnp.where(row + n * 128.0 < runs_ref[q], sums, 0.0))
        parts = jnp.concatenate(three_parts(jnp.concatenate(groups, axis=1)), axis=0)
        placed = jnp.dot(parts.astype(BF16), perm_ref[q], preferred_element_type=F32)
        placed = (placed[2 * BACK :] + placed[BACK : 2 * BACK]) + placed[0:BACK]
        rows = [placed[:, c * GS : (c + 1) * GS] for c in range(CAP)]
        back[q] = jnp.concatenate(rows, axis=0).T
        return carry

    lax.fori_loop(0, QUADS, block, 0)
    for j in range(QUADS // 2):
        sent[:, j, :] = jnp.concatenate([back[2 * j], back[2 * j + 1]], axis=1)


def unpack_kernel(
    red_ref, perm_ref, runs_ref, own_ref, angles_ref, parts_ref, mean_grad_ref, basis_ref,
    sent_ref, back, ret_ref, part_ref, sems
):
    greet()
    me, view = peers()
    send_back(red_ref, perm_ref, runs_ref, sent_ref, back)
    ret_ref[me] = sent_ref[me]
    slot = own_ref[0:1, :].astype(jnp.int32)
    owner = jnp.where(iota((GS, G), 0) == (slot >> 5), 1.0, 0.0).astype(BF16)
    owner = jnp.concatenate([owner] * 3, axis=0)
    place = slot & 31
    total = jnp.zeros((BACK, G), F32)
    greeted()
    deal(sent_ref, ret_ref, sems.at[0], sems.at[1])
    polar = jnp.concatenate([angles_ref[v, 0:1, :] for v in range(VIEWS)], axis=0)
    azimuth = jnp.concatenate([angles_ref[v, 1:2, :] for v in range(VIEWS)], axis=0)
    for k, values in enumerate(sh_basis(polar, azimuth)):
        basis_ref[k] = values
    settle(ret_ref, GS - 1, sems.at[1])
    for j in range(QUADS // 2):
        parts = jnp.concatenate(three_parts(ret_ref[:, j, :]), axis=0).astype(BF16)
        spread = lax.dot_general(
            parts, owner, (((0,), (0,)), ((), ())), preferred_element_type=F32
        )
        for i in range(16):
            total = jnp.where(place == j * 16 + i, spread[i * BACK : (i + 1) * BACK, :], total)
    m, n, a, b, c = (own_ref[k : k + 1, :] for k in range(1, 6))
    plain = total[5:6, :]
    du = total[3:4, :] - m * plain
    dw = total[4:5, :] - n * plain
    part_ref[0:3, :] = total[0:3, :]
    part_ref[3:4, :] = plain
    spread_views(part_ref, parts_ref, sems.at[2], sems.at[3])
    parts_ref[view] = part_ref[...]
    mean_grad_ref[0:1, :] = a * du + b * dw
    mean_grad_ref[1:2, :] = b * du + c * dw
    settle(parts_ref, VIEWS - 1, sems.at[3])
    settle(ret_ref, GS - 1, sems.at[0])
    settle(parts_ref, VIEWS - 1, sems.at[2])


def final_kernel(part_ref, basis_ref, own_ref, sh_ref, logit_grad_ref):
    plain = part_ref[0, 3:4, :]
    for v in range(1, VIEWS):
        plain = plain + part_ref[v, 3:4, :]
    logit_grad_ref[...] = plain * (1.0 - jax.nn.sigmoid(own_ref[6:7, :]))
    for k in range(16):
        total = part_ref[0, 0:3, :] * basis_ref[k, 0:1, :]
        for v in range(1, VIEWS):
            total = total + part_ref[v, 0:3, :] * basis_ref[k, v : v + 1, :]
        sh_ref[3 * k : 3 * k + 3, :] = total


MESH = pl.DeviceIdType.MESH
VM = pl.BlockSpec(memory_space=pltpu.VMEM)


def call(kernel, ins, outs, scratch=(), limit=16, remote=None, far=False):
    extra = {} if remote is None else dict(collective_id=remote, has_side_effects=True)
    shapes = [o if isinstance(o, jax.ShapeDtypeStruct) else jax.ShapeDtypeStruct(o, F32) for o in outs]
    return pl.pallas_call(
        kernel,
        out_shape=shapes,
        in_specs=[pl.BlockSpec(memory_space=pltpu.HBM) if far else VM] * len(ins),
        out_specs=[VM] * len(shapes),
        scratch_shapes=list(scratch),
        compiler_params=pltpu.CompilerParams(vmem_limit_bytes=limit * 2**20, **extra),
    )(*ins)


def pack(*ins):
    return call(
        pack_kernel,
        [pltpu.with_memory_space_constraint(i, pltpu.HBM) for i in ins],
        [(GS, QUADS, 128), (VIEWS, 2, G), (OWN, G), (3, QUADS, PIX)],
        [pltpu.VMEM(i.shape, i.dtype) for i in ins[:7]]
        + [
            pltpu.VMEM((GS, QUADS, 128), F32),
            pltpu.VMEM((WIDE, G), F32),
            pltpu.SemaphoreType.DMA((4,)),
            pltpu.SemaphoreType.DMA((len(ins),)),
        ],
        remote=0,
        far=True,
    )


def render(arrived, target):
    return call(
        render_kernel,
        [arrived, target],
        [
            (3, QUADS, PIX),
            (QUADS, PLACES, 5 * 128),
            jax.ShapeDtypeStruct((QUADS, PLACES, PLACES), BF16),
            (QUADS, 8, 128),
        ],
        [
            pltpu.VMEM((PLACES, FORMS * 128), F32),
            pltpu.VMEM((PLACES, PIX), F32),
            pltpu.VMEM((PLACES, PIX), F32),
            pltpu.VMEM((8, PIX), F32),
            pltpu.VMEM((3, 8, PIX), F32),
            pltpu.VMEM((3, 8, PIX), F32),
            pltpu.VMEM((8, PIX), F32),
            pltpu.VMEM((24, 128), F32),
            pltpu.VMEM((QUADS, 24, 128), F32),
            pltpu.VMEM((24, 128), F32),
            pltpu.VMEM((4 * WIDE, FORMS * 128), BF16),
            pltpu.VMEM((QUADS, GS, 128), F32),
            pltpu.VMEM((QUADS, 3, PIX), F32),
            pltpu.VMEM((PLACES, 128), F32),
            pltpu.VMEM((PLACES, 128), F32),
        ],
        limit=24,
    )


def unpack(sums, perm, runs, own, angles):
    return call(
        unpack_kernel,
        [sums, perm, runs, own, angles],
        [(VIEWS, 4, G), (2, G), (16, VIEWS, G)],
        [
            pltpu.VMEM((GS, QUADS // 2, 128), F32),
            pltpu.VMEM((QUADS, GS, GS), F32),
            pltpu.VMEM((GS, QUADS // 2, 128), F32),
            pltpu.VMEM((4, G), F32),
            pltpu.SemaphoreType.DMA((4,)),
        ],
        limit=24,
        remote=1,
    )


def final(parts, basis, own):
    return call(final_kernel, [parts, basis, own], [(48, G), (1, G)])


def local(sh_coef, opacity_logit, view_angle, mean_pos, conic, send_slot, depth_rank, target):
    arrived, angles, own, aim = pack(
        sh_coef,
        opacity_logit.reshape(1, G),
        view_angle[0],
        mean_pos[0],
        jnp.transpose(conic, (1, 0, 2)),
        send_slot,
        depth_rank,
        jnp.transpose(target[0], (1, 0, 2)),
    )
    images, sums, perm, runs = render(arrived, aim)
    parts, mean_grad, basis = unpack(sums, perm, runs, own, angles)
    sh_grad, logit_grad = final(parts, basis, own)
    return (sh_grad, logit_grad.reshape(G), mean_grad[None], jnp.transpose(images, (1, 0, 2))[None])


def solution(mesh):
    return jax.shard_map(
        local,
        mesh=mesh,
        in_specs=(
            P(None, "gs"),
            P("gs"),
            P("view", None, "gs"),
            P("view", None, "gs"),
            P("view", None, "gs"),
            P("view", "gs"),
            P("view", "gs"),
            P("view", "gs", None, None),
        ),
        out_specs=(P(None, "gs"), P("gs"), P("view", None, "gs"), P("view", "gs", None, None)),
        check_vma=False,
    )
```

```python
import jax
import jax.numpy as jnp
from jax import lax
from jax.experimental import pallas as pl
from jax.experimental.pallas import tpu as pltpu
from jax.sharding import PartitionSpec as P

F32 = jnp.float32
BF16 = jnp.bfloat16

SH_ZERO = 0.28209479177387814
SH_ONE = 0.4886025119029199
SH_TWO = (
    1.0925484305920792,
    -1.0925484305920792,
    0.31539156525252005,
    -1.0925484305920792,
    0.5462742152960396,
)
SH_THREE = (
    -0.5900435899266435,
    2.890611442640554,
    -0.4570457994644658,
    0.3731763325901154,
    -0.4570457994644658,
    1.445305721320277,
    -0.5900435899266435,
)
SSIM_MEAN = 0.0001
SSIM_SPREAD = 0.0009

GS = 64
VIEWS = 4
QUADS = 4
CAP = 8
G = 1024
PLACES = GS * CAP
PIX = 1024
TILES = PIX // 128
WIDE = 16
COL, KEY = 6, 9
BACK = 8
OWN = 7
SHIFT = 64.0
LOG2E = 1.4426950408889634
HALF = 8
PASSES = 8 // HALF
UNROLL = 8
TOGETHER = 4
FORMS = 2 * PASSES + 4


def iota(shape, axis):
    return lax.broadcasted_iota(jnp.int32, shape, axis)


def sh_basis(polar, azimuth):
    across = jnp.sin(polar)
    x = across * jnp.cos(azimuth)
    y = across * jnp.sin(azimuth)
    z = jnp.cos(polar)
    xx, yy, zz = x * x, y * y, z * z
    return [
        jnp.full_like(x, SH_ZERO),
        -SH_ONE * y,
        SH_ONE * z,
        -SH_ONE * x,
        SH_TWO[0] * x * y,
        SH_TWO[1] * y * z,
        SH_TWO[2] * (2.0 * zz - xx - yy),
        SH_TWO[3] * x * z,
        SH_TWO[4] * (xx - yy),
        SH_THREE[0] * y * (3.0 * xx - yy),
        SH_THREE[1] * x * y * z,
        SH_THREE[2] * y * (4.0 * zz - xx - yy),
        SH_THREE[3] * z * (2.0 * zz - 3.0 * xx - 3.0 * yy),
        SH_THREE[4] * x * (4.0 * zz - xx - yy),
        SH_THREE[5] * z * (xx - yy),
        SH_THREE[6] * x * (xx - 3.0 * yy),
    ]


def three_parts(values):
    high = values.astype(BF16).astype(F32)
    rest = values - high
    middle = rest.astype(BF16).astype(F32)
    return high, middle, rest - middle


def centre(mean):
    return mean * 32.0 - 16.5


def peers():
    return lax.axis_index("gs"), lax.axis_index("view")


def far_first(me):
    across = [((me // 16 + d) % 4) * 16 for d in range(4)]
    along = [((me // 2 + d) % 8) * 2 for d in range(8)]
    core = [me % 2, 1 - me % 2]
    steps = [(x, z, c) for x in range(4) for z in range(8) for c in range(2)]
    steps.sort(key=lambda s: (-min(s[0], 4 - s[0]) - min(s[1], 8 - s[1]), -s[2]))
    return [across[x] + along[z] + core[c] for x, z, c in steps if (x, z, c) != (0, 0, 0)]


def greet():
    me, view = peers()
    barrier = pltpu.get_barrier_semaphore()
    for other in far_first(me):
        pl.semaphore_signal(barrier, inc=1, device_id=(other, view), device_id_type=MESH)
    for d in range(1, VIEWS):
        pl.semaphore_signal(barrier, inc=1, device_id=(me, lax.rem(view + d, VIEWS)), device_id_type=MESH)


def greeted():
    pl.semaphore_wait(pltpu.get_barrier_semaphore(), GS - 1 + VIEWS - 1)


def deal(sent, got, send_sem, recv_sem):
    me, view = peers()
    for other in far_first(me):
        pltpu.make_async_remote_copy(
            src_ref=sent.at[other],
            dst_ref=got.at[me],
            send_sem=send_sem,
            recv_sem=recv_sem,
            device_id=(other, view),
            device_id_type=MESH,
        ).start()


def spread_views(mine, got, send_sem, recv_sem):
    me, view = peers()
    for d in range(1, VIEWS):
        pltpu.make_async_remote_copy(
            src_ref=mine,
            dst_ref=got.at[view],
            send_sem=send_sem,
            recv_sem=recv_sem,
            device_id=(me, lax.rem(view + d, VIEWS)),
            device_id_type=MESH,
        ).start()


def settle(whole, count, sem):
    part = whole.at[pl.ds(0, count)]
    pltpu.make_async_copy(part, part, sem).wait()


def pack_kernel(*refs):
    far, outs, rest = refs[:8], refs[8:15], refs[15:]
    arr_ref, angles_ref, own_ref, tgt, mono, step_s, sub_s = outs
    near, (out_ref, pay, sems, load_sems) = rest[:8], rest[8:]
    loads = [
        pltpu.make_async_copy(src, dst, load_sems.at[k]) for k, (src, dst) in enumerate(zip(far, near))
    ]
    for load in loads:
        load.start()
    greet()
    for load in loads:
        load.wait()
    sh_ref, logit_ref, angle_ref, mean_ref, conic_ref, slot_ref, rank_ref, tgt_ref = near
    me, view = peers()
    angles_ref[view] = angle_ref[...]
    basis = sh_basis(angle_ref[0:1, :], angle_ref[1:2, :])
    colour = jnp.full((3, G), 0.5, F32)
    for k in range(16):
        colour = colour + sh_ref[3 * k : 3 * k + 3, :] * basis[k]
    m, n = centre(mean_ref[0:1, :]), centre(mean_ref[1:2, :])
    kept = [slot_ref[...].astype(F32), m, n] + [conic_ref[k] * (1.0 / 32.0) for k in range(3)]
    for k, row in enumerate(kept + [logit_ref[...]]):
        own_ref[k : k + 1, :] = row
    scale = LOG2E / 1024.0
    opacity = 0.99 * jax.nn.sigmoid(logit_ref[...])
    a, b, c = (conic_ref[k] * scale for k in range(3))
    pay[...] = jnp.zeros((WIDE, G), F32)
    away = 0.5 * (a * m * m + 2.0 * b * m * n + c * n * n)
    pay[0:1, :] = (jnp.log(opacity) * LOG2E + SHIFT) - away
    pay[1:2, :] = a * m + b * n
    pay[2:3, :] = b * m + c * n
    pay[3:4, :] = -0.5 * a
    pay[4:5, :] = -b
    pay[5:6, :] = -0.5 * c
    pay[COL : COL + 3, :] = colour
    pay[KEY : KEY + 1, :] = (rank_ref[...] + 1).astype(F32)
    parts = three_parts(pay[...])
    slot = slot_ref[...]
    owner = jnp.where(iota((GS, G), 0) == (slot >> 5), 1.0, 0.0).astype(BF16)
    place = slot & 31
    for q in range(QUADS):
        total = jnp.zeros((GS, 128), F32)
        for part in parts[::-1]:
            spread = jnp.concatenate(
                [jnp.where(place == q * CAP + cap, part, 0.0) for cap in range(CAP)], axis=0
            ).astype(BF16)
            total = total + lax.dot_general(
                owner, spread, (((1,), (1,)), ((), ())), preferred_element_type=F32
            )
        out_ref[:, q, :] = total
    arr_ref[me] = out_ref[me]
    mono[...] = monomials()
    at = iota((PLACES, 128), 0)
    step_s[...] = (at >> 3).astype(F32)
    sub_s[...] = (at & 7).astype(F32)
    for q in range(QUADS):
        for c in range(3):
            for t in range(TILES):
                tgt[q, c * 8 + t : c * 8 + t + 1, :] = tgt_ref[c, q : q + 1, tile(t)]
    greeted()
    deal(out_ref, arr_ref, sems.at[0], sems.at[1])
    spread_views(angle_ref, angles_ref, sems.at[2], sems.at[3])
    settle(arr_ref, GS - 1, sems.at[1])
    settle(angles_ref, VIEWS - 1, sems.at[3])
    settle(arr_ref, GS - 1, sems.at[0])
    settle(angles_ref, VIEWS - 1, sems.at[2])


def monomials():
    lane = iota((WIDE, 128), 1)
    row = iota((WIDE, 128), 0)
    u = ((lane & 31) - 16).astype(F32)
    top = ((lane >> 5) - 16).astype(F32)

    def rows(entries):
        out = jnp.zeros((WIDE, 128), F32)
        for k, value in entries.items():
            out = jnp.where(row == k, value, out)
        return out

    def power(w):
        return rows({0: 1.0, 1: u, 2: w, 3: u * u, 4: u * w, 5: w * w})

    def first(w):
        return rows({2: 4.0, 4: 4.0 * u, 5: 8.0 * w + 16.0})

    tiles = []
    for h in range(PASSES):
        tiles += [power(top + 4.0 * HALF * h), first(top + 4.0 * HALF * h)]
    tiles.append(rows({5: 32.0}))
    tiles += [rows({COL + c: 1.0}) for c in range(3)]
    base = jnp.concatenate(tiles, axis=1)
    shift = jnp.where(
        (iota((WIDE, 128), 0) == 0) & (iota((WIDE, 128), 1) >= 0), -SHIFT, 0.0
    )
    none = jnp.zeros((WIDE, 128), F32)
    shift = jnp.concatenate([shift, none] * PASSES + [none] * 4, axis=1)
    return jnp.concatenate([base, base, base, shift], axis=0).astype(BF16)


def loss_slope(x, y):
    lane = iota((128, 128), 1)
    other = iota((128, 128), 0)
    same = ((lane & 31) >> 2) == ((other & 31) >> 2)
    pool = jnp.where(same, 1.0 / 16.0, 0.0).astype(BF16)
    rows = x.shape[0]
    parts = three_parts(jnp.concatenate([x, y, x * x, y * y, x * y], axis=0))
    sums = jnp.dot(
        jnp.concatenate(parts, axis=0).astype(BF16), pool, preferred_element_type=F32
    )
    means = (sums[10 * rows : 15 * rows] + sums[5 * rows : 10 * rows]) + sums[0 : 5 * rows]
    mx, my, exx, eyy, exy = (means[k * rows : (k + 1) * rows] for k in range(5))
    n1 = 2.0 * mx * my + SSIM_MEAN
    n2 = 2.0 * (exy - mx * my) + SSIM_SPREAD
    d1 = mx * mx + my * my + SSIM_MEAN
    d2 = (exx - mx * mx) + (eyy - my * my) + SSIM_SPREAD
    i1, i2 = 1.0 / d1, 1.0 / d2
    both = i1 * i2
    ratio = n1 * n2 * both
    by_mean = 2.0 * my * (n2 - n1) * both + 2.0 * mx * ratio * (i2 - i1)
    by_square = -ratio * i2
    by_cross = 2.0 * n1 * both
    return 0.1 * (x - y) - (0.2 / 16.0) * (by_mean + 2.0 * x * by_square + y * by_cross)


def shifted(values, by, fill):
    sub = iota(values.shape, 0)
    keep = (sub >= by) if by > 0 else (sub < 8 + by)
    return jnp.where(keep, pltpu.roll(values, by % 8, 0), fill)


def order(blocks, xs, perm, bc, mono, step_s, sub_s):
    pick = jnp.where((iota((3 * WIDE, 128), 0) & 15) == KEY, 1.0, 0.0).astype(BF16)
    turned = [x.T for x in xs]
    packed = [
        jnp.concatenate([t[c * WIDE : (c + 1) * WIDE, :] for c in range(CAP)], axis=1) for t in turned
    ]
    parts = [jnp.concatenate(three_parts(p), axis=0).astype(BF16) for p in packed]
    keys = [p[KEY : KEY + 1, :] for p in packed]
    columns = [
        lax.dot_general(p, pick, (((0,), (0,)), ((), ())), preferred_element_type=F32) for p in parts
    ]
    filled = [jnp.sum(jnp.where(k > 0.0, 1.0, 0.0), axis=1, keepdims=True) for k in keys]
    turns = [jnp.floor((f + (8 * UNROLL - 1.0)) * (1.0 / (8 * UNROLL))) for f in filled]
    step, sub = step_s[...], sub_s[...]
    for q, key, column, turn, full in zip(blocks, keys, columns, turns, filled):
        span = turn * UNROLL
        wanted = jnp.where(step < span, sub * span + step + (PLACES - full), -1.0)
        for t in range(PLACES // 128):
            less = jnp.where(column < key[:, tile(t)], 1.0, 0.0)
            rank = jnp.sum(less, axis=0, keepdims=True)
            perm[q, :, tile(t)] = jnp.where(rank == wanted, 1.0, 0.0).astype(BF16)
    ordered = [
        lax.dot_general(p, perm[q], (((1,), (1,)), ((), ())), preferred_element_type=F32)
        for q, p in zip(blocks, parts)
    ]
    ones = jnp.ones((WIDE, PLACES), F32)
    ordered = [jnp.concatenate([o, ones], axis=0).astype(BF16) for o in ordered]
    for q, o in zip(blocks, ordered):
        bc[q] = lax.dot_general(o, mono[...], (((0,), (0,)), ((), ())), preferred_element_type=F32)
    return turns


def unroll_loop(run, body, start):
    def several(i, state):
        for k in range(UNROLL):
            state = body(i * UNROLL + k, state)
        return state

    return lax.fori_loop(0, run // UNROLL, several, start)


def tile(t):
    return slice(t * 128, (t + 1) * 128)


def blend(run, bc, a_s, w_s, left, seen):
    one = jnp.ones((8, 128), F32)
    zero = jnp.zeros((8, 128), F32)
    for h in range(PASSES):

        def ahead(i, state, h=h):
            passing, got = list(state[0]), [list(s) for s in state[1]]
            rows = pl.ds(pl.multiple_of(i * 8, 8), 8)
            power, first = bc[rows, tile(2 * h)], bc[rows, tile(2 * h + 1)]
            second = bc[rows, tile(2 * PASSES)]
            colours = [bc[rows, tile(2 * PASSES + 1 + c)] for c in range(3)]
            for t in range(HALF):
                alpha = jnp.exp2(power)
                weight = passing[t] * alpha
                passing[t] = passing[t] - weight
                a_s[rows, tile(h * HALF + t)] = alpha
                w_s[rows, tile(h * HALF + t)] = weight
                for c in range(3):
                    got[c][t] = got[c][t] + colours[c] * weight
                if t < HALF - 1:
                    power = power + first
                    first = first + second
            return tuple(passing), tuple(tuple(s) for s in got)

        passing, got = unroll_loop(run, ahead, ((one,) * HALF, ((zero,) * HALF,) * 3))
        for t in range(HALF):
            left[:, tile(h * HALF + t)] = passing[t]
            for c in range(3):
                seen[c, :, tile(h * HALF + t)] = got[c][t]


def backward(run, bc, a_s, w_s, tg, later_s, red):
    zero = jnp.zeros((8, 128), F32)
    for h in range(PASSES - 1, -1, -1):

        def back(i, later, h=h):
            later = list(later)
            rows = pl.ds(pl.multiple_of((run - 1 - i) * 8, 8), 8)
            c0, c1, c2 = (bc[rows, tile(2 * PASSES + 1 + c)] for c in range(3))
            plain, graded = zero, zero
            sums = [zero, zero, zero]
            for t in range(HALF - 1, -1, -1):
                cols = tile(h * HALF + t)
                alpha, weight = a_s[rows, cols], w_s[rows, cols]
                g0, g1, g2 = (tg[c, :, cols] for c in range(3))
                gap = c0 * g0 + c1 * g1 + c2 * g2 - later[t]
                later[t] = later[t] + alpha * gap
                plain = plain + weight * gap
                if t:
                    graded = graded + plain
                sums = [sums[0] + weight * g0, sums[1] + weight * g1, sums[2] + weight * g2]
            if h:
                graded = graded + HALF * h * plain
            sums = sums + [plain, graded]
            for k in range(5):
                if h < PASSES - 1:
                    sums[k] = sums[k] + red[rows, tile(k)]
                red[rows, tile(k)] = sums[k]
            return tuple(later)

        unroll_loop(run, back, tuple(later_s[:, tile(h * HALF + t)] for t in range(HALF)))


def join(left, seen, pic, slope, tgt, tg, later, image):
    before = shifted(left[...], 1, 1.0)
    for by in (1, 2, 4):
        before = before * shifted(before, by, 1.0)
    for c in range(3):
        row = jnp.sum(before * seen[c], axis=0, keepdims=True)
        image[c : c + 1, :] = row
        for t in range(TILES):
            pic[c * 8 + t : c * 8 + t + 1, :] = row[:, tile(t)]
    slope[...] = loss_slope(pic[...], tgt[...])
    behind = jnp.zeros((8, PIX), F32)
    for c in range(3):
        row = jnp.concatenate([slope[c * 8 + t : c * 8 + t + 1, :] for t in range(TILES)], axis=1)
        behind = behind + row * seen[c]
        tg[c] = before * row
    value, factor = shifted(behind, -1, 0.0), shifted(left[...], -1, 0.0)
    for by in (1, 2, 4):
        value = value + factor * shifted(value, -by, 0.0)
        factor = factor * shifted(factor, -by, 0.0)
    later[...] = before * value


def render_kernel(
    arr_ref, tgt, mono, step_s, sub_s, img_ref, red, perm, runs,
    bc, a_s, w_s, left, seen, tg, later, pic, slope, xq, image, runs_s
):
    for q in range(QUADS):
        xq[q] = arr_ref[:, q, :]

    def sort(p, carry):
        blocks = [p * TOGETHER + k for k in range(TOGETHER)]
        found = order(blocks, [xq[q] for q in blocks], perm, bc, mono, step_s, sub_s)
        for q, turn in zip(blocks, found):
            runs[q] = jnp.broadcast_to(turn * (8 * UNROLL), (8, 128))
            runs_s[q] = jnp.sum(turn).astype(jnp.int32) * UNROLL
        return carry

    def first(q, carry):
        blend(runs_s[q], bc.at[q], a_s.at[q], w_s.at[q], left.at[q], seen.at[q])
        return carry

    def second(q, carry):
        backward(runs_s[q], bc.at[q], a_s.at[q], w_s.at[q], tg.at[q], later.at[q], red.at[q])
        return carry

    if TOGETHER == QUADS:
        sort(0, 0)
    else:
        lax.fori_loop(0, QUADS // TOGETHER, sort, 0)
    lax.fori_loop(0, QUADS, first, 0)
    for q in range(QUADS):
        join(left.at[q], seen.at[q], pic.at[q], slope.at[q], tgt.at[q], tg.at[q], later.at[q], image.at[q])
    lax.fori_loop(0, QUADS, second, 0)
    for q in range(QUADS):
        for c in range(3):
            img_ref[c, q : q + 1, :] = image[q, c : c + 1, :]


def send_back(red_ref, perm_ref, runs_ref, sent, back):
    pixel = iota((128, 128), 0)
    across = ((pixel & 31) - 16).astype(F32)
    down = ((pixel >> 5) - 16).astype(F32)
    row = iota((BACK, 128), 1).astype(F32)

    def block(q, carry):
        groups = []
        for n in range(PLACES // 128):
            g0, g1, g2, plain, graded = (red_ref[q, tile(n), tile(k)].T for k in range(5))
            sums = (g0, g1, g2, plain * across, plain * down + 4.0 * graded, plain)
            sums = [jnp.sum(value, axis=0, keepdims=True) for value in sums]
            sums = jnp.concatenate(sums + [jnp.zeros((BACK - 6, 128), F32)], axis=0)
            groups.append(jnp.where(row + n * 128.0 < runs_ref[q], sums, 0.0))
        parts = jnp.concatenate(three_parts(jnp.concatenate(groups, axis=1)), axis=0)
        placed = jnp.dot(parts.astype(BF16), perm_ref[q], preferred_element_type=F32)
        placed = (placed[2 * BACK :] + placed[BACK : 2 * BACK]) + placed[0:BACK]
        rows = [placed[:, c * GS : (c + 1) * GS] for c in range(CAP)]
        back[q] = jnp.concatenate(rows, axis=0).T
        return carry

    lax.fori_loop(0, QUADS, block, 0)
    for j in range(QUADS // 2):
        sent[:, j, :] = jnp.concatenate([back[2 * j], back[2 * j + 1]], axis=1)


def unpack_kernel(
    red_ref, perm_ref, runs_ref, own_ref, angles_ref, parts_ref, move_ref, basis_ref,
    sent_ref, back, ret_ref, part_ref, sems
):
    greet()
    me, view = peers()
    send_back(red_ref, perm_ref, runs_ref, sent_ref, back)
    ret_ref[me] = sent_ref[me]
    slot = own_ref[0:1, :].astype(jnp.int32)
    owner = jnp.where(iota((GS, G), 0) == (slot >> 5), 1.0, 0.0).astype(BF16)
    owner = jnp.concatenate([owner] * 3, axis=0)
    place = slot & 31
    total = jnp.zeros((BACK, G), F32)
    greeted()
    deal(sent_ref, ret_ref, sems.at[0], sems.at[1])
    polar = jnp.concatenate([angles_ref[v, 0:1, :] for v in range(VIEWS)], axis=0)
    azimuth = jnp.concatenate([angles_ref[v, 1:2, :] for v in range(VIEWS)], axis=0)
    for k, values in enumerate(sh_basis(polar, azimuth)):
        basis_ref[k] = values
    settle(ret_ref, GS - 1, sems.at[1])
    for j in range(QUADS // 2):
        parts = jnp.concatenate(three_parts(ret_ref[:, j, :]), axis=0).astype(BF16)
        spread = lax.dot_general(
            parts, owner, (((0,), (0,)), ((), ())), preferred_element_type=F32
        )
        for i in range(16):
            total = jnp.where(place == j * 16 + i, spread[i * BACK : (i + 1) * BACK, :], total)
    m, n, a, b, c = (own_ref[k : k + 1, :] for k in range(1, 6))
    plain = total[5:6, :]
    du = total[3:4, :] - m * plain
    dw = total[4:5, :] - n * plain
    part_ref[0:3, :] = total[0:3, :]
    part_ref[3:4, :] = plain
    spread_views(part_ref, parts_ref, sems.at[2], sems.at[3])
    parts_ref[view] = part_ref[...]
    move_ref[0:1, :] = a * du + b * dw
    move_ref[1:2, :] = b * du + c * dw
    settle(parts_ref, VIEWS - 1, sems.at[3])
    settle(ret_ref, GS - 1, sems.at[0])
    settle(parts_ref, VIEWS - 1, sems.at[2])


def final_kernel(part_ref, move_ref, basis_ref, own_ref, sh_ref, logit_grad_ref, mean_grad_ref):
    mean_grad_ref[...] = move_ref[...]
    plain = part_ref[0, 3:4, :]
    for v in range(1, VIEWS):
        plain = plain + part_ref[v, 3:4, :]
    logit_grad_ref[...] = plain * (1.0 - jax.nn.sigmoid(own_ref[6:7, :]))
    for k in range(16):
        total = part_ref[0, 0:3, :] * basis_ref[k, 0:1, :]
        for v in range(1, VIEWS):
            total = total + part_ref[v, 0:3, :] * basis_ref[k, v : v + 1, :]
        sh_ref[3 * k : 3 * k + 3, :] = total


MESH = pl.DeviceIdType.MESH
VM = pl.BlockSpec(memory_space=pltpu.VMEM)


def call(kernel, ins, outs, scratch=(), limit=20, remote=None, far=False):
    extra = {} if remote is None else dict(collective_id=remote, has_side_effects=True)
    shapes = [o if isinstance(o, jax.ShapeDtypeStruct) else jax.ShapeDtypeStruct(o, F32) for o in outs]
    return pl.pallas_call(
        kernel,
        out_shape=shapes,
        in_specs=[pl.BlockSpec(memory_space=pltpu.HBM) if far else VM] * len(ins),
        out_specs=[VM] * len(shapes),
        scratch_shapes=list(scratch),
        compiler_params=pltpu.CompilerParams(vmem_limit_bytes=limit * 2**20, **extra),
    )(*ins)


def pack(*ins):
    return call(
        pack_kernel,
        [pltpu.with_memory_space_constraint(i, pltpu.HBM) for i in ins],
        [
            (GS, QUADS, 128),
            (VIEWS, 2, G),
            (OWN, G),
            (QUADS, 24, 128),
            jax.ShapeDtypeStruct((4 * WIDE, FORMS * 128), BF16),
            (PLACES, 128),
            (PLACES, 128),
        ],
        [pltpu.VMEM(i.shape, i.dtype) for i in ins]
        + [
            pltpu.VMEM((GS, QUADS, 128), F32),
            pltpu.VMEM((WIDE, G), F32),
            pltpu.SemaphoreType.DMA((4,)),
            pltpu.SemaphoreType.DMA((len(ins),)),
        ],
        remote=0,
        far=True,
    )


def render(*ins):
    return call(
        render_kernel,
        ins,
        [
            (3, QUADS, PIX),
            (QUADS, PLACES, 5 * 128),
            jax.ShapeDtypeStruct((QUADS, PLACES, PLACES), BF16),
            (QUADS, 8, 128),
        ],
        [
            pltpu.VMEM((QUADS, PLACES, FORMS * 128), F32),
            pltpu.VMEM((QUADS, PLACES, PIX), F32),
            pltpu.VMEM((QUADS, PLACES, PIX), F32),
            pltpu.VMEM((QUADS, 8, PIX), F32),
            pltpu.VMEM((QUADS, 3, 8, PIX), F32),
            pltpu.VMEM((QUADS, 3, 8, PIX), F32),
            pltpu.VMEM((QUADS, 8, PIX), F32),
            pltpu.VMEM((QUADS, 24, 128), F32),
            pltpu.VMEM((QUADS, 24, 128), F32),
            pltpu.VMEM((QUADS, GS, 128), F32),
            pltpu.VMEM((QUADS, 3, PIX), F32),
            pltpu.SMEM((QUADS,), jnp.int32),
        ],
        limit=44,
    )


def unpack(sums, perm, runs, own, angles):
    return call(
        unpack_kernel,
        [sums, perm, runs, own, angles],
        [(VIEWS, 4, G), (2, G), (16, VIEWS, G)],
        [
            pltpu.VMEM((GS, QUADS // 2, 128), F32),
            pltpu.VMEM((QUADS, GS, GS), F32),
            pltpu.VMEM((GS, QUADS // 2, 128), F32),
            pltpu.VMEM((4, G), F32),
            pltpu.SemaphoreType.DMA((4,)),
        ],
        limit=24,
        remote=1,
    )


def final(*ins):
    return call(final_kernel, ins, [(48, G), (1, G), (2, G)])


def local(sh_coef, opacity_logit, view_angle, mean_pos, conic, send_slot, depth_rank, target):
    arrived, angles, own, *prepared = pack(
        sh_coef,
        opacity_logit.reshape(1, G),
        view_angle[0],
        mean_pos[0],
        jnp.transpose(conic, (1, 0, 2)),
        send_slot,
        depth_rank,
        jnp.transpose(target[0], (1, 0, 2)),
    )
    images, sums, perm, runs = render(arrived, *prepared)
    parts, move, basis = unpack(sums, perm, runs, own, angles)
    sh_grad, logit_grad, mean_grad = final(parts, move, basis, own)
    return (sh_grad, logit_grad.reshape(G), mean_grad[None], jnp.transpose(images, (1, 0, 2))[None])


def solution(mesh):
    return jax.shard_map(
        local,
        mesh=mesh,
        in_specs=(
            P(None, "gs"),
            P("gs"),
            P("view", None, "gs"),
            P("view", None, "gs"),
            P("view", None, "gs"),
            P("view", "gs"),
            P("view", "gs"),
            P("view", "gs", None, None),
        ),
        out_specs=(P(None, "gs"), P("gs"), P("view", None, "gs"), P("view", "gs", None, None)),
        check_vma=False,
    )
```

```python
import jax
import jax.numpy as jnp
from jax import lax
from jax.experimental import pallas as pl
from jax.experimental.pallas import tpu as pltpu
from jax.sharding import PartitionSpec as P

F32 = jnp.float32
BF16 = jnp.bfloat16

SH_ZERO = 0.28209479177387814
SH_ONE = 0.4886025119029199
SH_TWO = (
    1.0925484305920792,
    -1.0925484305920792,
    0.31539156525252005,
    -1.0925484305920792,
    0.5462742152960396,
)
SH_THREE = (
    -0.5900435899266435,
    2.890611442640554,
    -0.4570457994644658,
    0.3731763325901154,
    -0.4570457994644658,
    1.445305721320277,
    -0.5900435899266435,
)
SSIM_MEAN = 0.0001
SSIM_SPREAD = 0.0009

GS = 64
VIEWS = 4
QUADS = 4
CAP = 8
G = 1024
PLACES = GS * CAP
PIX = 1024
TILES = PIX // 128
WIDE = 16
COL, KEY = 6, 9
BACK = 8
OWN = 7
SHIFT = 64.0
LOG2E = 1.4426950408889634
HALF = 8
PASSES = 8 // HALF
UNROLL = 8
RENDER_MIB = 36
UNPACK_MIB = 24
FORMS = 2 * PASSES + 4


def iota(shape, axis):
    return lax.broadcasted_iota(jnp.int32, shape, axis)


def sh_basis(polar, azimuth):
    across = jnp.sin(polar)
    x = across * jnp.cos(azimuth)
    y = across * jnp.sin(azimuth)
    z = jnp.cos(polar)
    xx, yy, zz = x * x, y * y, z * z
    return [
        jnp.full_like(x, SH_ZERO),
        -SH_ONE * y,
        SH_ONE * z,
        -SH_ONE * x,
        SH_TWO[0] * x * y,
        SH_TWO[1] * y * z,
        SH_TWO[2] * (2.0 * zz - xx - yy),
        SH_TWO[3] * x * z,
        SH_TWO[4] * (xx - yy),
        SH_THREE[0] * y * (3.0 * xx - yy),
        SH_THREE[1] * x * y * z,
        SH_THREE[2] * y * (4.0 * zz - xx - yy),
        SH_THREE[3] * z * (2.0 * zz - 3.0 * xx - 3.0 * yy),
        SH_THREE[4] * x * (4.0 * zz - xx - yy),
        SH_THREE[5] * z * (xx - yy),
        SH_THREE[6] * x * (xx - 3.0 * yy),
    ]


def three_parts(values):
    high = values.astype(BF16).astype(F32)
    rest = values - high
    middle = rest.astype(BF16).astype(F32)
    return high, middle, rest - middle


def centre(mean):
    return mean * 32.0 - 16.5


def peers():
    return lax.axis_index("gs"), lax.axis_index("view")


def far_first(me):
    across = [((me // 16 + d) % 4) * 16 for d in range(4)]
    along = [((me // 2 + d) % 8) * 2 for d in range(8)]
    core = [me % 2, 1 - me % 2]
    steps = [(x, z, c) for x in range(4) for z in range(8) for c in range(2)]
    steps.sort(key=lambda s: (-min(s[0], 4 - s[0]) - min(s[1], 8 - s[1]), -s[2]))
    return [across[x] + along[z] + core[c] for x, z, c in steps if (x, z, c) != (0, 0, 0)]


def greet():
    me, view = peers()
    barrier = pltpu.get_barrier_semaphore()
    for other in far_first(me):
        pl.semaphore_signal(barrier, inc=1, device_id=(other, view), device_id_type=MESH)
    for d in range(1, VIEWS):
        pl.semaphore_signal(barrier, inc=1, device_id=(me, lax.rem(view + d, VIEWS)), device_id_type=MESH)


def greeted():
    pl.semaphore_wait(pltpu.get_barrier_semaphore(), GS - 1 + VIEWS - 1)


def deal(sent, got, send_sem, recv_sem):
    me, view = peers()
    for other in far_first(me):
        pltpu.make_async_remote_copy(
            src_ref=sent.at[other],
            dst_ref=got.at[me],
            send_sem=send_sem,
            recv_sem=recv_sem,
            device_id=(other, view),
            device_id_type=MESH,
        ).start()


def spread_views(mine, got, send_sem, recv_sem):
    me, view = peers()
    for d in range(1, VIEWS):
        pltpu.make_async_remote_copy(
            src_ref=mine,
            dst_ref=got.at[view],
            send_sem=send_sem,
            recv_sem=recv_sem,
            device_id=(me, lax.rem(view + d, VIEWS)),
            device_id_type=MESH,
        ).start()


def settle(whole, count, sem):
    part = whole.at[pl.ds(0, count)]
    pltpu.make_async_copy(part, part, sem).wait()


def pack_kernel(*refs):
    far, outs, rest = refs[:8], refs[8:15], refs[15:]
    arr_ref, angles_ref, own_ref, tgt, mono, step_s, sub_s = outs
    near, (out_ref, pay, sems, load_sems) = rest[:8], rest[8:]
    loads = [
        pltpu.make_async_copy(src, dst, load_sems.at[k]) for k, (src, dst) in enumerate(zip(far, near))
    ]
    greet()
    for load in loads:
        load.start()
    for load in loads:
        load.wait()
    sh_ref, logit_ref, angle_ref, mean_ref, conic_ref, slot_ref, rank_ref, tgt_ref = near
    me, view = peers()
    angles_ref[view] = angle_ref[...]
    basis = sh_basis(angle_ref[0:1, :], angle_ref[1:2, :])
    colour = jnp.full((3, G), 0.5, F32)
    for k in range(16):
        colour = colour + sh_ref[3 * k : 3 * k + 3, :] * basis[k]
    m, n = centre(mean_ref[0:1, :]), centre(mean_ref[1:2, :])
    kept = [slot_ref[...].astype(F32), m, n] + [conic_ref[k] * (1.0 / 32.0) for k in range(3)]
    for k, row in enumerate(kept + [logit_ref[...]]):
        own_ref[k : k + 1, :] = row
    scale = LOG2E / 1024.0
    opacity = 0.99 * jax.nn.sigmoid(logit_ref[...])
    a, b, c = (conic_ref[k] * scale for k in range(3))
    pay[...] = jnp.zeros((WIDE, G), F32)
    away = 0.5 * (a * m * m + 2.0 * b * m * n + c * n * n)
    pay[0:1, :] = (jnp.log(opacity) * LOG2E + SHIFT) - away
    pay[1:2, :] = a * m + b * n
    pay[2:3, :] = b * m + c * n
    pay[3:4, :] = -0.5 * a
    pay[4:5, :] = -b
    pay[5:6, :] = -0.5 * c
    pay[COL : COL + 3, :] = colour
    pay[KEY : KEY + 1, :] = (rank_ref[...] + 1).astype(F32)
    parts = three_parts(pay[...])
    slot = slot_ref[...]
    owner = jnp.where(iota((GS, G), 0) == (slot >> 5), 1.0, 0.0).astype(BF16)
    place = slot & 31
    for q in range(QUADS):
        total = jnp.zeros((GS, 128), F32)
        for part in parts[::-1]:
            spread = jnp.concatenate(
                [jnp.where(place == q * CAP + cap, part, 0.0) for cap in range(CAP)], axis=0
            ).astype(BF16)
            total = total + lax.dot_general(
                owner, spread, (((1,), (1,)), ((), ())), preferred_element_type=F32
            )
        out_ref[:, q, :] = total
    arr_ref[me] = out_ref[me]
    mono[...] = monomials()
    at = iota((PLACES, 128), 0)
    step_s[...] = (at >> 3).astype(F32)
    sub_s[...] = (at & 7).astype(F32)
    for q in range(QUADS):
        for c in range(3):
            for t in range(TILES):
                tgt[q, c * 8 + t : c * 8 + t + 1, :] = tgt_ref[c, q : q + 1, tile(t)]
    greeted()
    deal(out_ref, arr_ref, sems.at[0], sems.at[1])
    spread_views(angle_ref, angles_ref, sems.at[2], sems.at[3])
    settle(arr_ref, GS - 1, sems.at[1])
    settle(angles_ref, VIEWS - 1, sems.at[3])
    settle(arr_ref, GS - 1, sems.at[0])
    settle(angles_ref, VIEWS - 1, sems.at[2])


def monomials():
    lane = iota((WIDE, 128), 1)
    row = iota((WIDE, 128), 0)
    u = ((lane & 31) - 16).astype(F32)
    top = ((lane >> 5) - 16).astype(F32)

    def rows(entries):
        out = jnp.zeros((WIDE, 128), F32)
        for k, value in entries.items():
            out = jnp.where(row == k, value, out)
        return out

    def power(w):
        return rows({0: 1.0, 1: u, 2: w, 3: u * u, 4: u * w, 5: w * w})

    def first(w):
        return rows({2: 4.0, 4: 4.0 * u, 5: 8.0 * w + 16.0})

    tiles = []
    for h in range(PASSES):
        tiles += [power(top + 4.0 * HALF * h), first(top + 4.0 * HALF * h)]
    tiles.append(rows({5: 32.0}))
    tiles += [rows({COL + c: 1.0}) for c in range(3)]
    base = jnp.concatenate(tiles, axis=1)
    shift = jnp.where(
        (iota((WIDE, 128), 0) == 0) & (iota((WIDE, 128), 1) >= 0), -SHIFT, 0.0
    )
    none = jnp.zeros((WIDE, 128), F32)
    shift = jnp.concatenate([shift, none] * PASSES + [none] * 4, axis=1)
    return jnp.concatenate([base, base, base, shift], axis=0).astype(BF16)


def loss_slope(x, y):
    lane = iota((128, 128), 1)
    other = iota((128, 128), 0)
    same = ((lane & 31) >> 2) == ((other & 31) >> 2)
    pool = jnp.where(same, 1.0 / 16.0, 0.0).astype(BF16)
    rows = x.shape[0]
    parts = three_parts(jnp.concatenate([x, y, x * x, y * y, x * y], axis=0))
    sums = jnp.dot(
        jnp.concatenate(parts, axis=0).astype(BF16), pool, preferred_element_type=F32
    )
    means = (sums[10 * rows : 15 * rows] + sums[5 * rows : 10 * rows]) + sums[0 : 5 * rows]
    mx, my, exx, eyy, exy = (means[k * rows : (k + 1) * rows] for k in range(5))
    n1 = 2.0 * mx * my + SSIM_MEAN
    n2 = 2.0 * (exy - mx * my) + SSIM_SPREAD
    d1 = mx * mx + my * my + SSIM_MEAN
    d2 = (exx - mx * mx) + (eyy - my * my) + SSIM_SPREAD
    i1, i2 = 1.0 / d1, 1.0 / d2
    both = i1 * i2
    ratio = n1 * n2 * both
    by_mean = 2.0 * my * (n2 - n1) * both + 2.0 * mx * ratio * (i2 - i1)
    by_square = -ratio * i2
    by_cross = 2.0 * n1 * both
    return 0.1 * (x - y) - (0.2 / 16.0) * (by_mean + 2.0 * x * by_square + y * by_cross)


def shifted(values, by, fill):
    sub = iota(values.shape, 0)
    keep = (sub >= by) if by > 0 else (sub < 8 + by)
    return jnp.where(keep, pltpu.roll(values, by % 8, 0), fill)


def order(blocks, xs, perm, bc, mono, step_s, sub_s):
    pick = jnp.where((iota((3 * WIDE, 128), 0) & 15) == KEY, 1.0, 0.0).astype(BF16)
    turned = [x.T for x in xs]
    packed = [
        jnp.concatenate([t[c * WIDE : (c + 1) * WIDE, :] for c in range(CAP)], axis=1) for t in turned
    ]
    parts = [jnp.concatenate(three_parts(p), axis=0).astype(BF16) for p in packed]
    keys = [p[KEY : KEY + 1, :] for p in packed]
    columns = [
        lax.dot_general(p, pick, (((0,), (0,)), ((), ())), preferred_element_type=F32) for p in parts
    ]
    filled = [jnp.sum(jnp.where(k > 0.0, 1.0, 0.0), axis=1, keepdims=True) for k in keys]
    turns = [jnp.floor((f + (8 * UNROLL - 1.0)) * (1.0 / (8 * UNROLL))) for f in filled]
    step, sub = step_s[...], sub_s[...]
    for q, key, column, turn, full in zip(blocks, keys, columns, turns, filled):
        span = turn * UNROLL
        wanted = jnp.where(step < span, sub * span + step + (PLACES - full), -1.0)
        for t in range(PLACES // 128):
            less = jnp.where(column < key[:, tile(t)], 1.0, 0.0)
            rank = jnp.sum(less, axis=0, keepdims=True)
            perm[q, :, tile(t)] = jnp.where(rank == wanted, 1.0, 0.0).astype(BF16)
    ordered = [
        lax.dot_general(p, perm[q], (((1,), (1,)), ((), ())), preferred_element_type=F32)
        for q, p in zip(blocks, parts)
    ]
    ones = jnp.ones((WIDE, PLACES), F32)
    ordered = [jnp.concatenate([o, ones], axis=0).astype(BF16) for o in ordered]
    for q, o in zip(blocks, ordered):
        bc[q] = lax.dot_general(o, mono[...], (((0,), (0,)), ((), ())), preferred_element_type=F32)
    return turns


def unroll_loop(run, body, start):
    def several(i, state):
        for k in range(UNROLL):
            state = body(i * UNROLL + k, state)
        return state

    return lax.fori_loop(0, run // UNROLL, several, start)


def tile(t):
    return slice(t * 128, (t + 1) * 128)


def blend(run, bc, a_s, w_s, col, left, seen):
    one = jnp.ones((8, 128), F32)
    zero = jnp.zeros((8, 128), F32)
    for h in range(PASSES):

        def ahead(i, state, h=h):
            passing, got = list(state[0]), [list(s) for s in state[1]]
            rows = pl.ds(pl.multiple_of(i * 8, 8), 8)
            power, first = bc[rows, tile(2 * h)], bc[rows, tile(2 * h + 1)]
            second = bc[rows, tile(2 * PASSES)]
            colours = [bc[rows, tile(2 * PASSES + 1 + c)] for c in range(3)]
            if h == 0 and col is not None:
                for c in range(3):
                    col[rows, tile(c)] = colours[c]
            for t in range(HALF):
                alpha = jnp.exp2(power)
                weight = passing[t] * alpha
                passing[t] = passing[t] - weight
                a_s[rows, tile(h * HALF + t)] = alpha
                w_s[rows, tile(h * HALF + t)] = weight
                for c in range(3):
                    got[c][t] = got[c][t] + colours[c] * weight
                if t < HALF - 1:
                    power = power + first
                    first = first + second
            return tuple(passing), tuple(tuple(s) for s in got)

        passing, got = unroll_loop(run, ahead, ((one,) * HALF, ((zero,) * HALF,) * 3))
        for t in range(HALF):
            left[:, tile(h * HALF + t)] = passing[t]
            for c in range(3):
                seen[c, :, tile(h * HALF + t)] = got[c][t]


def back_step(i, later, a_s, w_s, col, tg, red):
    zero = jnp.zeros((8, 128), F32)
    later = list(later)
    rows = pl.ds(pl.multiple_of(i * 8, 8), 8)
    c0, c1, c2 = (col[rows, tile(c)] for c in range(3))
    plain, graded = zero, zero
    sums = [zero, zero, zero]
    for t in range(TILES - 1, -1, -1):
        alpha, weight = a_s[rows, tile(t)], w_s[rows, tile(t)]
        g0, g1, g2 = (tg[c, :, tile(t)] for c in range(3))
        gap = c0 * g0 + c1 * g1 + c2 * g2 - later[t]
        later[t] = later[t] + alpha * gap
        plain = plain + weight * gap
        if t:
            graded = graded + plain
        sums = [sums[0] + weight * g0, sums[1] + weight * g1, sums[2] + weight * g2]
    for k, value in enumerate(sums + [plain, graded]):
        red[rows, tile(k)] = value
    return tuple(later)


def backward(run, a_s, w_s, col, tg, later, red):
    def back(i, state):
        return back_step(run - 1 - i, state, a_s, w_s, col, tg, red)

    unroll_loop(run, back, tuple(later[:, tile(t)] for t in range(TILES)))


def backward_whole(runs, a_s, w_s, col, tg, later, red):
    steps = PLACES // 8
    begin = tuple(later[:, tile(t)] for t in range(TILES))
    last = runs[...] * (1.0 / 8.0) - 1.0

    def several(n, state):
        for k in range(8):
            i = steps - 1 - (n * 8 + k)
            here = last == i.astype(F32)
            state = [jnp.where(here, b, v) for b, v in zip(begin, state)]
            state = back_step(i, state, a_s, w_s, col, tg, red)
        return tuple(state)

    lax.fori_loop(0, steps // 8, several, begin)


def join(left, seen, pic, slope, tgt, tg, later, image):
    before = shifted(left[...], 1, 1.0)
    for by in (1, 2, 4):
        before = before * shifted(before, by, 1.0)
    for c in range(3):
        row = jnp.sum(before * seen[c], axis=0, keepdims=True)
        image[c : c + 1, :] = row
        for t in range(TILES):
            pic[c * 8 + t : c * 8 + t + 1, :] = row[:, tile(t)]
    slope[...] = loss_slope(pic[...], tgt[...])
    behind = jnp.zeros((8, PIX), F32)
    for c in range(3):
        row = jnp.concatenate([slope[c * 8 + t : c * 8 + t + 1, :] for t in range(TILES)], axis=1)
        behind = behind + row * seen[c]
        tg[c] = before * row
    value, factor = shifted(behind, -1, 0.0), shifted(left[...], -1, 0.0)
    for by in (1, 2, 4):
        value = value + factor * shifted(value, -by, 0.0)
        factor = factor * shifted(factor, -by, 0.0)
    later[...] = before * value


def render_kernel(
    arr_ref, tgt, mono, step_s, sub_s,
    img_ref, red, perm, runs, largest, a_last, w_last, col_last, tg_last, later_last,
    bc, a_s, w_s, tg, later, left, seen, pic, slope, xq, image, runs_s
):
    for q in range(QUADS):
        xq[q] = arr_ref[:, q, :]
    found = order(list(range(QUADS)), [xq[q] for q in range(QUADS)], perm, bc, mono, step_s, sub_s)
    for q, turn in enumerate(found):
        runs_s[q] = jnp.sum(turn).astype(jnp.int32) * UNROLL
    best = jnp.int32(0)
    for q in range(1, QUADS):
        best = jnp.where(runs_s[q] > runs_s[best], q, best)
    last = QUADS - 1
    largest[...] = jnp.full((8, 128), best, jnp.int32).astype(F32)

    def block(at):
        return jnp.where(at == best, last, jnp.where(at == last, best, at))

    def first(at, carry):
        q = block(at)
        blend(runs_s[q], bc.at[q], a_s.at[at], w_s.at[at], None, left.at[at], seen.at[at])
        return carry

    def second(at, carry):
        q = block(at)
        col = bc.at[q, :, pl.ds((2 * PASSES + 1) * 128, 3 * 128)]
        backward(runs_s[q], a_s.at[at], w_s.at[at], col, tg.at[at], later.at[at], red.at[at])
        return carry

    lax.fori_loop(0, last, first, 0)
    blend(runs_s[best], bc.at[best], a_last, w_last, col_last, left.at[last], seen.at[last])
    for at in range(QUADS):
        q = block(at)
        runs[at] = jnp.full((8, 128), 8 * runs_s[q], jnp.int32).astype(F32)
        to = (tg_last, later_last) if at == last else (tg.at[at], later.at[at])
        join(left.at[at], seen.at[at], pic.at[at], slope.at[at], tgt.at[q], *to, image.at[q])
    lax.fori_loop(0, last, second, 0)
    for q in range(QUADS):
        for c in range(3):
            img_ref[c, q : q + 1, :] = image[q, c : c + 1, :]


def reduced(red, runs):
    pixel = iota((128, 128), 0)
    across = ((pixel & 31) - 16).astype(F32)
    down = ((pixel >> 5) - 16).astype(F32)
    row = iota((BACK, 128), 1).astype(F32)
    groups = []
    for n in range(PLACES // 128):
        g0, g1, g2, plain, graded = (red[tile(n), tile(k)].T for k in range(5))
        sums = (g0, g1, g2, plain * across, plain * down + 4.0 * graded, plain)
        sums = [jnp.sum(value, axis=0, keepdims=True) for value in sums]
        sums = jnp.concatenate(sums + [jnp.zeros((BACK - 6, 128), F32)], axis=0)
        groups.append(jnp.where(row + n * 128.0 < runs[...], sums, 0.0))
    return jnp.concatenate(groups, axis=1)


def send_back(red, perm, runs, largest, a_s, w_s, col, tg, later, sent, red_last, sums_s):
    last = QUADS - 1
    for at in range(last):
        sums_s[at] = reduced(red.at[at], runs.at[at])
    backward_whole(
        runs.at[last], a_s, w_s, col, tg, later, red_last
    )
    sums = [sums_s[at] for at in range(last)] + [reduced(red_last, runs.at[last])]
    swap = [largest[:, 0:1] == float(q) for q in range(last)]
    moved = sums[last]
    for q in range(last):
        moved = jnp.where(swap[q], sums[q], moved)
    sums = [jnp.where(swap[q], sums[last], sums[q]) for q in range(last)] + [moved]
    parts = [jnp.concatenate(three_parts(p), axis=0).astype(BF16) for p in sums]
    placed = [jnp.dot(p, perm[q], preferred_element_type=F32) for q, p in enumerate(parts)]
    placed = [(p[2 * BACK :] + p[BACK : 2 * BACK]) + p[0:BACK] for p in placed]
    back = [jnp.concatenate([p[:, c * GS : (c + 1) * GS] for c in range(CAP)], axis=0).T for p in placed]
    for j in range(QUADS // 2):
        sent[:, j, :] = jnp.concatenate([back[2 * j], back[2 * j + 1]], axis=1)


def unpack_kernel(
    red, perm, runs, largest, a_s, w_s, col, tg, later, own_ref, angles_ref, parts_ref, move_ref, basis_ref,
    sent_ref, red_last, sums_s, ret_ref, part_ref, sems
):
    greet()
    me, view = peers()
    send_back(red, perm, runs, largest, a_s, w_s, col, tg, later, sent_ref, red_last, sums_s)
    ret_ref[me] = sent_ref[me]
    slot = own_ref[0:1, :].astype(jnp.int32)
    owner = jnp.where(iota((GS, G), 0) == (slot >> 5), 1.0, 0.0).astype(BF16)
    owner = jnp.concatenate([owner] * 3, axis=0)
    place = slot & 31
    greeted()
    deal(sent_ref, ret_ref, sems.at[0], sems.at[1])
    polar = jnp.concatenate([angles_ref[v, 0:1, :] for v in range(VIEWS)], axis=0)
    azimuth = jnp.concatenate([angles_ref[v, 1:2, :] for v in range(VIEWS)], axis=0)
    for k, values in enumerate(sh_basis(polar, azimuth)):
        basis_ref[k] = values
    settle(ret_ref, GS - 1, sems.at[1])
    both = jnp.concatenate([ret_ref[:, j, :] for j in range(QUADS // 2)], axis=1)
    parts = jnp.concatenate(three_parts(both), axis=0).astype(BF16)
    spread = lax.dot_general(parts, owner, (((0,), (0,)), ((), ())), preferred_element_type=F32)
    found = [spread[i * BACK : (i + 1) * BACK, :] for i in range(QUADS * CAP)]
    for bit in range(5):
        odd = ((place >> bit) & 1) == 1
        found = [jnp.where(odd, found[i + 1], found[i]) for i in range(0, len(found), 2)]
    total = found[0]
    m, n, a, b, c = (own_ref[k : k + 1, :] for k in range(1, 6))
    plain = total[5:6, :]
    du = total[3:4, :] - m * plain
    dw = total[4:5, :] - n * plain
    part_ref[0:3, :] = total[0:3, :]
    part_ref[3:4, :] = plain
    spread_views(part_ref, parts_ref, sems.at[2], sems.at[3])
    parts_ref[view] = part_ref[...]
    move_ref[0:1, :] = a * du + b * dw
    move_ref[1:2, :] = b * du + c * dw
    settle(parts_ref, VIEWS - 1, sems.at[3])
    settle(ret_ref, GS - 1, sems.at[0])
    settle(parts_ref, VIEWS - 1, sems.at[2])


def final_kernel(part_ref, move_ref, basis_ref, own_ref, sh_ref, logit_grad_ref, mean_grad_ref):
    mean_grad_ref[...] = move_ref[...]
    plain = part_ref[0, 3:4, :]
    for v in range(1, VIEWS):
        plain = plain + part_ref[v, 3:4, :]
    logit_grad_ref[...] = plain * (1.0 - jax.nn.sigmoid(own_ref[6:7, :]))
    for k in range(16):
        total = part_ref[0, 0:3, :] * basis_ref[k, 0:1, :]
        for v in range(1, VIEWS):
            total = total + part_ref[v, 0:3, :] * basis_ref[k, v : v + 1, :]
        sh_ref[3 * k : 3 * k + 3, :] = total


MESH = pl.DeviceIdType.MESH
VM = pl.BlockSpec(memory_space=pltpu.VMEM)


def call(kernel, ins, outs, scratch=(), limit=20, remote=None, far=False):
    extra = {} if remote is None else dict(collective_id=remote, has_side_effects=True)
    shapes = [o if isinstance(o, jax.ShapeDtypeStruct) else jax.ShapeDtypeStruct(o, F32) for o in outs]
    return pl.pallas_call(
        kernel,
        out_shape=shapes,
        in_specs=[pl.BlockSpec(memory_space=pltpu.HBM) if far else VM] * len(ins),
        out_specs=[VM] * len(shapes),
        scratch_shapes=list(scratch),
        compiler_params=pltpu.CompilerParams(vmem_limit_bytes=limit * 2**20, **extra),
    )(*ins)


def pack(*ins):
    return call(
        pack_kernel,
        [pltpu.with_memory_space_constraint(i, pltpu.HBM) for i in ins],
        [
            (GS, QUADS, 128),
            (VIEWS, 2, G),
            (OWN, G),
            (QUADS, 24, 128),
            jax.ShapeDtypeStruct((4 * WIDE, FORMS * 128), BF16),
            (PLACES, 128),
            (PLACES, 128),
        ],
        [pltpu.VMEM(i.shape, i.dtype) for i in ins]
        + [
            pltpu.VMEM((GS, QUADS, 128), F32),
            pltpu.VMEM((WIDE, G), F32),
            pltpu.SemaphoreType.DMA((4,)),
            pltpu.SemaphoreType.DMA((len(ins),)),
        ],
        remote=0,
        far=True,
    )


def render(*ins):
    return call(
        render_kernel,
        ins,
        [
            (3, QUADS, PIX),
            (QUADS - 1, PLACES, 5 * 128),
            jax.ShapeDtypeStruct((QUADS, PLACES, PLACES), BF16),
            (QUADS, 8, 128),
            (8, 128),
            (PLACES, PIX),
            (PLACES, PIX),
            (PLACES, 3 * 128),
            (3, 8, PIX),
            (8, PIX),
        ],
        [
            pltpu.VMEM((QUADS, PLACES, FORMS * 128), F32),
            pltpu.VMEM((QUADS - 1, PLACES, PIX), F32),
            pltpu.VMEM((QUADS - 1, PLACES, PIX), F32),
            pltpu.VMEM((QUADS - 1, 3, 8, PIX), F32),
            pltpu.VMEM((QUADS - 1, 8, PIX), F32),
            pltpu.VMEM((QUADS, 8, PIX), F32),
            pltpu.VMEM((QUADS, 3, 8, PIX), F32),
            pltpu.VMEM((QUADS, 24, 128), F32),
            pltpu.VMEM((QUADS, 24, 128), F32),
            pltpu.VMEM((QUADS, GS, 128), F32),
            pltpu.VMEM((QUADS, 3, PIX), F32),
            pltpu.SMEM((QUADS,), jnp.int32),
        ],
        limit=RENDER_MIB,
    )


def unpack(*ins):
    return call(
        unpack_kernel,
        ins,
        [(VIEWS, 4, G), (2, G), (16, VIEWS, G)],
        [
            pltpu.VMEM((GS, QUADS // 2, 128), F32),
            pltpu.VMEM((PLACES, 5 * 128), F32),
            pltpu.VMEM((QUADS - 1, BACK, PLACES), F32),
            pltpu.VMEM((GS, QUADS // 2, 128), F32),
            pltpu.VMEM((4, G), F32),
            pltpu.SemaphoreType.DMA((4,)),
        ],
        limit=UNPACK_MIB,
        remote=1,
    )


def final(*ins):
    return call(final_kernel, ins, [(48, G), (1, G), (2, G)])


def local(sh_coef, opacity_logit, view_angle, mean_pos, conic, send_slot, depth_rank, target):
    arrived, angles, own, *prepared = pack(
        sh_coef,
        opacity_logit.reshape(1, G),
        view_angle[0],
        mean_pos[0],
        jnp.transpose(conic, (1, 0, 2)),
        send_slot,
        depth_rank,
        jnp.transpose(target[0], (1, 0, 2)),
    )
    images, *blended = render(arrived, *prepared)
    parts, move, basis = unpack(*blended, own, angles)
    sh_grad, logit_grad, mean_grad = final(parts, move, basis, own)
    return (sh_grad, logit_grad.reshape(G), mean_grad[None], jnp.transpose(images, (1, 0, 2))[None])


def solution(mesh):
    return jax.shard_map(
        local,
        mesh=mesh,
        in_specs=(
            P(None, "gs"),
            P("gs"),
            P("view", None, "gs"),
            P("view", None, "gs"),
            P("view", None, "gs"),
            P("view", "gs"),
            P("view", "gs"),
            P("view", "gs", None, None),
        ),
        out_specs=(P(None, "gs"), P("gs"), P("view", None, "gs"), P("view", "gs", None, None)),
        check_vma=False,
    )
```

```python
import jax
import jax.numpy as jnp
from jax import lax
from jax.experimental import pallas as pl
from jax.experimental.pallas import tpu as pltpu
from jax.sharding import PartitionSpec as P

F32 = jnp.float32
BF16 = jnp.bfloat16

SH_ZERO = 0.28209479177387814
SH_ONE = 0.4886025119029199
SH_TWO = (
    1.0925484305920792,
    -1.0925484305920792,
    0.31539156525252005,
    -1.0925484305920792,
    0.5462742152960396,
)
SH_THREE = (
    -0.5900435899266435,
    2.890611442640554,
    -0.4570457994644658,
    0.3731763325901154,
    -0.4570457994644658,
    1.445305721320277,
    -0.5900435899266435,
)
SSIM_MEAN = 0.0001
SSIM_SPREAD = 0.0009

GS = 64
VIEWS = 4
QUADS = 4
CAP = 8
G = 1024
PLACES = GS * CAP
PIX = 1024
TILES = PIX // 128
WIDE = 16
COL, KEY = 6, 9
SENT = 12
ROWS = QUADS * CAP * SENT // 128
BACK = 8
OWN = 7
SHIFT = 64.0
LOG2E = 1.4426950408889634
HALF = 8
PASSES = 8 // HALF
UNROLL = 8
RENDER_MIB = 36
UNPACK_MIB = 24
FORMS = 2 * PASSES + 4


def iota(shape, axis):
    return lax.broadcasted_iota(jnp.int32, shape, axis)


def sh_basis(polar, azimuth):
    across = jnp.sin(polar)
    x = across * jnp.cos(azimuth)
    y = across * jnp.sin(azimuth)
    z = jnp.cos(polar)
    xx, yy, zz = x * x, y * y, z * z
    return [
        jnp.full_like(x, SH_ZERO),
        -SH_ONE * y,
        SH_ONE * z,
        -SH_ONE * x,
        SH_TWO[0] * x * y,
        SH_TWO[1] * y * z,
        SH_TWO[2] * (2.0 * zz - xx - yy),
        SH_TWO[3] * x * z,
        SH_TWO[4] * (xx - yy),
        SH_THREE[0] * y * (3.0 * xx - yy),
        SH_THREE[1] * x * y * z,
        SH_THREE[2] * y * (4.0 * zz - xx - yy),
        SH_THREE[3] * z * (2.0 * zz - 3.0 * xx - 3.0 * yy),
        SH_THREE[4] * x * (4.0 * zz - xx - yy),
        SH_THREE[5] * z * (xx - yy),
        SH_THREE[6] * x * (xx - 3.0 * yy),
    ]


def three_parts(values):
    high = values.astype(BF16).astype(F32)
    rest = values - high
    middle = rest.astype(BF16).astype(F32)
    return high, middle, rest - middle


def centre(mean):
    return mean * 32.0 - 16.5


def peers():
    return lax.axis_index("gs"), lax.axis_index("view")


def far_first(me):
    across = [((me // 16 + d) % 4) * 16 for d in range(4)]
    along = [((me // 2 + d) % 8) * 2 for d in range(8)]
    core = [me % 2, 1 - me % 2]
    steps = [(x, z, c) for x in range(4) for z in range(8) for c in range(2)]
    steps.sort(key=lambda s: (-min(s[0], 4 - s[0]) - min(s[1], 8 - s[1]), -s[2]))
    return [across[x] + along[z] + core[c] for x, z, c in steps if (x, z, c) != (0, 0, 0)]


def greet():
    me, view = peers()
    barrier = pltpu.get_barrier_semaphore()
    for other in far_first(me):
        pl.semaphore_signal(barrier, inc=1, device_id=(other, view), device_id_type=MESH)
    for d in range(1, VIEWS):
        pl.semaphore_signal(barrier, inc=1, device_id=(me, lax.rem(view + d, VIEWS)), device_id_type=MESH)


def greeted():
    pl.semaphore_wait(pltpu.get_barrier_semaphore(), GS - 1 + VIEWS - 1)


def deal(sent, got, send_sem, recv_sem):
    me, view = peers()
    for other in far_first(me):
        pltpu.make_async_remote_copy(
            src_ref=sent.at[other],
            dst_ref=got.at[me],
            send_sem=send_sem,
            recv_sem=recv_sem,
            device_id=(other, view),
            device_id_type=MESH,
        ).start()


def spread_views(mine, got, send_sem, recv_sem):
    me, view = peers()
    for d in range(1, VIEWS):
        pltpu.make_async_remote_copy(
            src_ref=mine,
            dst_ref=got.at[view],
            send_sem=send_sem,
            recv_sem=recv_sem,
            device_id=(me, lax.rem(view + d, VIEWS)),
            device_id_type=MESH,
        ).start()


def settle(whole, count, sem):
    part = whole.at[pl.ds(0, count)]
    pltpu.make_async_copy(part, part, sem).wait()


def pack_kernel(*refs):
    far, outs, rest = refs[:8], refs[8:15], refs[15:]
    arr_ref, angles_ref, own_ref, tgt, mono, step_s, sub_s = outs
    near, (out_ref, pay, sems, load_sems) = rest[:8], rest[8:]
    loads = [
        pltpu.make_async_copy(src, dst, load_sems.at[k]) for k, (src, dst) in enumerate(zip(far, near))
    ]
    greet()
    for load in loads:
        load.start()
    for load in loads:
        load.wait()
    sh_ref, logit_ref, angle_ref, mean_ref, conic_ref, slot_ref, rank_ref, tgt_ref = near
    me, view = peers()
    angles_ref[view] = angle_ref[...]
    basis = sh_basis(angle_ref[0:1, :], angle_ref[1:2, :])
    colour = jnp.full((3, G), 0.5, F32)
    for k in range(16):
        colour = colour + sh_ref[3 * k : 3 * k + 3, :] * basis[k]
    m, n = centre(mean_ref[0:1, :]), centre(mean_ref[1:2, :])
    kept = [slot_ref[...].astype(F32), m, n] + [conic_ref[k] * (1.0 / 32.0) for k in range(3)]
    for k, row in enumerate(kept + [logit_ref[...]]):
        own_ref[k : k + 1, :] = row
    scale = LOG2E / 1024.0
    opacity = 0.99 * jax.nn.sigmoid(logit_ref[...])
    a, b, c = (conic_ref[k] * scale for k in range(3))
    pay[...] = jnp.zeros((SENT, G), F32)
    away = 0.5 * (a * m * m + 2.0 * b * m * n + c * n * n)
    pay[0:1, :] = (jnp.log(opacity) * LOG2E + SHIFT) - away
    pay[1:2, :] = a * m + b * n
    pay[2:3, :] = b * m + c * n
    pay[3:4, :] = -0.5 * a
    pay[4:5, :] = -b
    pay[5:6, :] = -0.5 * c
    pay[COL : COL + 3, :] = colour
    pay[KEY : KEY + 1, :] = (rank_ref[...] + 1).astype(F32)
    parts = three_parts(pay[...])
    slot = slot_ref[...]
    owner = jnp.where(iota((GS, G), 0) == (slot >> 5), 1.0, 0.0).astype(BF16)
    place = (slot & 31) - jnp.where(iota((2 * SENT, G), 0) >= SENT, 1, 0)
    total = jnp.zeros((GS, ROWS * 128), F32)
    for part in parts[::-1]:
        pair = jnp.concatenate([part, part], axis=0)
        spread = jnp.concatenate(
            [jnp.where(place == i, pair, 0.0) for i in range(0, QUADS * CAP, 2)], axis=0
        ).astype(BF16)
        total = total + lax.dot_general(
            owner, spread, (((1,), (1,)), ((), ())), preferred_element_type=F32
        )
    for r in range(ROWS):
        out_ref[:, r, :] = total[:, tile(r)]
    arr_ref[me] = out_ref[me]
    mono[...] = monomials()
    at = iota((PLACES, 128), 0)
    step_s[...] = (at >> 3).astype(F32)
    sub_s[...] = (at & 7).astype(F32)
    for q in range(QUADS):
        for c in range(3):
            for t in range(TILES):
                tgt[q, c * 8 + t : c * 8 + t + 1, :] = tgt_ref[c, q : q + 1, tile(t)]
    for q in range(QUADS):
        y = tgt[q, 0:24, :]
        means = window_means(jnp.concatenate([y, y * y], axis=0))
        tgt[q, 24:48, :] = means[0:24]
        tgt[q, 48:72, :] = means[24:48] - means[0:24] * means[0:24]
    greeted()
    deal(out_ref, arr_ref, sems.at[0], sems.at[1])
    spread_views(angle_ref, angles_ref, sems.at[2], sems.at[3])
    settle(arr_ref, GS - 1, sems.at[1])
    settle(angles_ref, VIEWS - 1, sems.at[3])
    settle(arr_ref, GS - 1, sems.at[0])
    settle(angles_ref, VIEWS - 1, sems.at[2])


def monomials():
    lane = iota((WIDE, 128), 1)
    row = iota((WIDE, 128), 0)
    u = ((lane & 31) - 16).astype(F32)
    top = ((lane >> 5) - 16).astype(F32)

    def rows(entries):
        out = jnp.zeros((WIDE, 128), F32)
        for k, value in entries.items():
            out = jnp.where(row == k, value, out)
        return out

    def power(w):
        return rows({0: 1.0, 1: u, 2: w, 3: u * u, 4: u * w, 5: w * w})

    def first(w):
        return rows({2: 4.0, 4: 4.0 * u, 5: 8.0 * w + 16.0})

    tiles = []
    for h in range(PASSES):
        tiles += [power(top + 4.0 * HALF * h), first(top + 4.0 * HALF * h)]
    tiles.append(rows({5: 32.0}))
    tiles += [rows({COL + c: 1.0}) for c in range(3)]
    base = jnp.concatenate(tiles, axis=1)
    shift = jnp.where(
        (iota((WIDE, 128), 0) == 0) & (iota((WIDE, 128), 1) >= 0), -SHIFT, 0.0
    )
    none = jnp.zeros((WIDE, 128), F32)
    shift = jnp.concatenate([shift, none] * PASSES + [none] * 4, axis=1)
    return jnp.concatenate([base, base, base, shift], axis=0).astype(BF16)


def window_means(values):
    lane = iota((128, 128), 1)
    other = iota((128, 128), 0)
    same = ((lane & 31) >> 2) == ((other & 31) >> 2)
    pool = jnp.where(same, 1.0 / 16.0, 0.0).astype(BF16)
    rows = values.shape[0]
    sums = jnp.dot(
        jnp.concatenate(three_parts(values), axis=0).astype(BF16), pool, preferred_element_type=F32
    )
    return (sums[2 * rows :] + sums[rows : 2 * rows]) + sums[0:rows]


def loss_slope(x, y, my, vy):
    rows = x.shape[0]
    means = window_means(jnp.concatenate([x, x * x, x * y], axis=0))
    mx, exx, exy = (means[k * rows : (k + 1) * rows] for k in range(3))
    n1 = 2.0 * mx * my + SSIM_MEAN
    n2 = 2.0 * (exy - mx * my) + SSIM_SPREAD
    d1 = mx * mx + my * my + SSIM_MEAN
    d2 = (exx - mx * mx) + vy + SSIM_SPREAD
    i1, i2 = 1.0 / d1, 1.0 / d2
    both = i1 * i2
    ratio = n1 * n2 * both
    by_mean = 2.0 * my * (n2 - n1) * both + 2.0 * mx * ratio * (i2 - i1)
    by_square = -ratio * i2
    by_cross = 2.0 * n1 * both
    return 0.1 * (x - y) - (0.2 / 16.0) * (by_mean + 2.0 * x * by_square + y * by_cross)


def shifted(values, by, fill):
    sub = iota(values.shape, 0)
    keep = (sub >= by) if by > 0 else (sub < 8 + by)
    return jnp.where(keep, pltpu.roll(values, by % 8, 0), fill)


def order(blocks, arrived, perm, bc, mono, step_s, sub_s):
    pick = jnp.where((iota((3 * WIDE, 128), 0) & 15) == KEY, 1.0, 0.0).astype(BF16)
    turned = jnp.concatenate([arrived[:, r, :].T for r in range(ROWS)], axis=0)
    rest = jnp.zeros((WIDE - SENT, PLACES), F32)
    packed = []
    for q in blocks:
        places = [turned[i * SENT : (i + 1) * SENT, :] for i in range(q * CAP, (q + 1) * CAP)]
        packed.append(jnp.concatenate([jnp.concatenate(places, axis=1), rest], axis=0))
    parts = [jnp.concatenate(three_parts(p), axis=0).astype(BF16) for p in packed]
    keys = [p[KEY : KEY + 1, :] for p in packed]
    columns = [
        lax.dot_general(p, pick, (((0,), (0,)), ((), ())), preferred_element_type=F32) for p in parts
    ]
    filled = [jnp.sum(jnp.where(k > 0.0, 1.0, 0.0), axis=1, keepdims=True) for k in keys]
    turns = [jnp.floor((f + (8 * UNROLL - 1.0)) * (1.0 / (8 * UNROLL))) for f in filled]
    step, sub = step_s[...], sub_s[...]
    for q, key, column, turn, full in zip(blocks, keys, columns, turns, filled):
        span = turn * UNROLL
        wanted = jnp.where(step < span, sub * span + step + (PLACES - full), -1.0)
        for t in range(PLACES // 128):
            less = jnp.where(column < key[:, tile(t)], 1.0, 0.0)
            rank = jnp.sum(less, axis=0, keepdims=True)
            perm[q, :, tile(t)] = jnp.where(rank == wanted, 1.0, 0.0).astype(BF16)
    ordered = [
        lax.dot_general(p, perm[q], (((1,), (1,)), ((), ())), preferred_element_type=F32)
        for q, p in zip(blocks, parts)
    ]
    ones = jnp.ones((WIDE, PLACES), F32)
    ordered = [jnp.concatenate([o, ones], axis=0).astype(BF16) for o in ordered]
    for q, o in zip(blocks, ordered):
        bc[q] = lax.dot_general(o, mono[...], (((0,), (0,)), ((), ())), preferred_element_type=F32)
    return turns


def unroll_loop(run, body, start):
    def several(i, state):
        for k in range(UNROLL):
            state = body(i * UNROLL + k, state)
        return state

    return lax.fori_loop(0, run // UNROLL, several, start)


def tile(t):
    return slice(t * 128, (t + 1) * 128)


def blend(run, bc, a_s, w_s, col, left, seen):
    one = jnp.ones((8, 128), F32)
    zero = jnp.zeros((8, 128), F32)
    for h in range(PASSES):

        def ahead(i, state, h=h):
            passing, got = list(state[0]), [list(s) for s in state[1]]
            rows = pl.ds(pl.multiple_of(i * 8, 8), 8)
            power, first = bc[rows, tile(2 * h)], bc[rows, tile(2 * h + 1)]
            second = bc[rows, tile(2 * PASSES)]
            colours = [bc[rows, tile(2 * PASSES + 1 + c)] for c in range(3)]
            if h == 0 and col is not None:
                for c in range(3):
                    col[rows, tile(c)] = colours[c]
            for t in range(HALF):
                alpha = jnp.exp2(power)
                weight = passing[t] * alpha
                passing[t] = passing[t] - weight
                a_s[rows, tile(h * HALF + t)] = alpha
                w_s[rows, tile(h * HALF + t)] = weight
                for c in range(3):
                    got[c][t] = got[c][t] + colours[c] * weight
                if t < HALF - 1:
                    power = power + first
                    first = first + second
            return tuple(passing), tuple(tuple(s) for s in got)

        passing, got = unroll_loop(run, ahead, ((one,) * HALF, ((zero,) * HALF,) * 3))
        for t in range(HALF):
            left[:, tile(h * HALF + t)] = passing[t]
            for c in range(3):
                seen[c, :, tile(h * HALF + t)] = got[c][t]


def back_step(i, later, a_s, w_s, col, tg, red):
    zero = jnp.zeros((8, 128), F32)
    later = list(later)
    rows = pl.ds(pl.multiple_of(i * 8, 8), 8)
    c0, c1, c2 = (col[rows, tile(c)] for c in range(3))
    plain, graded = zero, zero
    sums = [zero, zero, zero]
    for t in range(TILES - 1, -1, -1):
        alpha, weight = a_s[rows, tile(t)], w_s[rows, tile(t)]
        g0, g1, g2 = (tg[c, :, tile(t)] for c in range(3))
        gap = c0 * g0 + c1 * g1 + c2 * g2 - later[t]
        later[t] = later[t] + alpha * gap
        plain = plain + weight * gap
        if t:
            graded = graded + plain
        sums = [sums[0] + weight * g0, sums[1] + weight * g1, sums[2] + weight * g2]
    for k, value in enumerate(sums + [plain, graded]):
        red[rows, tile(k)] = value
    return tuple(later)


def backward(run, a_s, w_s, col, tg, later, red):
    def back(i, state):
        return back_step(run - 1 - i, state, a_s, w_s, col, tg, red)

    unroll_loop(run, back, tuple(later[:, tile(t)] for t in range(TILES)))


def backward_whole(runs, a_s, w_s, col, tg, later, red):
    steps = PLACES // 8
    begin = tuple(later[:, tile(t)] for t in range(TILES))
    last = runs[...] * (1.0 / 8.0) - 1.0

    def several(n, state):
        for k in range(8):
            i = steps - 1 - (n * 8 + k)
            here = last == i.astype(F32)
            state = [jnp.where(here, b, v) for b, v in zip(begin, state)]
            state = back_step(i, state, a_s, w_s, col, tg, red)
        return tuple(state)

    lax.fori_loop(0, steps // 8, several, begin)


def join(left, seen, pic, slope, tgt, tg, later, image):
    before = shifted(left[...], 1, 1.0)
    for by in (1, 2, 4):
        before = before * shifted(before, by, 1.0)
    for c in range(3):
        row = jnp.sum(before * seen[c], axis=0, keepdims=True)
        image[c : c + 1, :] = row
        for t in range(TILES):
            pic[c * 8 + t : c * 8 + t + 1, :] = row[:, tile(t)]
    slope[...] = loss_slope(pic[...], *(tgt[24 * k : 24 * k + 24, :] for k in range(3)))
    behind = jnp.zeros((8, PIX), F32)
    for c in range(3):
        row = jnp.concatenate([slope[c * 8 + t : c * 8 + t + 1, :] for t in range(TILES)], axis=1)
        behind = behind + row * seen[c]
        tg[c] = before * row
    value, factor = shifted(behind, -1, 0.0), shifted(left[...], -1, 0.0)
    for by in (1, 2, 4):
        value = value + factor * shifted(value, -by, 0.0)
        factor = factor * shifted(factor, -by, 0.0)
    later[...] = before * value


def render_kernel(
    arr_ref, tgt, mono, step_s, sub_s,
    img_ref, red, perm, runs, largest, a_last, w_last, col_last, tg_last, later_last,
    bc, a_s, w_s, tg, later, left, seen, pic, slope, image, runs_s
):
    found = order(list(range(QUADS)), arr_ref, perm, bc, mono, step_s, sub_s)
    for q, turn in enumerate(found):
        runs_s[q] = jnp.sum(turn).astype(jnp.int32) * UNROLL
    best = jnp.int32(0)
    for q in range(1, QUADS):
        best = jnp.where(runs_s[q] > runs_s[best], q, best)
    last = QUADS - 1
    largest[...] = jnp.full((8, 128), best, jnp.int32).astype(F32)

    def block(at):
        return jnp.where(at == best, last, jnp.where(at == last, best, at))

    def first(at, carry):
        q = block(at)
        blend(runs_s[q], bc.at[q], a_s.at[at], w_s.at[at], None, left.at[at], seen.at[at])
        return carry

    def second(at, carry):
        q = block(at)
        col = bc.at[q, :, pl.ds((2 * PASSES + 1) * 128, 3 * 128)]
        backward(runs_s[q], a_s.at[at], w_s.at[at], col, tg.at[at], later.at[at], red.at[at])
        return carry

    lax.fori_loop(0, last, first, 0)
    blend(runs_s[best], bc.at[best], a_last, w_last, col_last, left.at[last], seen.at[last])
    for at in range(QUADS):
        q = block(at)
        runs[at] = jnp.full((8, 128), 8 * runs_s[q], jnp.int32).astype(F32)
        to = (tg_last, later_last) if at == last else (tg.at[at], later.at[at])
        join(left.at[at], seen.at[at], pic.at[at], slope.at[at], tgt.at[q], *to, image.at[q])
    lax.fori_loop(0, last, second, 0)
    for q in range(QUADS):
        for c in range(3):
            img_ref[c, q : q + 1, :] = image[q, c : c + 1, :]


def reduced(red, runs):
    pixel = iota((128, 128), 0)
    across = ((pixel & 31) - 16).astype(F32)
    down = ((pixel >> 5) - 16).astype(F32)
    row = iota((BACK, PLACES), 1).astype(F32)
    colour = red[:, 0 : 3 * 128]
    high = colour.astype(BF16)
    low = (colour - high.astype(F32)).astype(BF16)
    pick = jnp.where(iota((BACK, 3 * 128), 1) >> 7 == iota((BACK, 3 * 128), 0), 1.0, 0.0).astype(BF16)
    nt = (((1,), (1,)), ((), ()))
    sums = lax.dot_general(pick, low, nt, preferred_element_type=F32) + lax.dot_general(
        pick, high, nt, preferred_element_type=F32
    )
    groups = []
    for n in range(PLACES // 128):
        plain, graded = (red[tile(n), tile(k)].T for k in (3, 4))
        moved = (plain * across, plain * down + 4.0 * graded, plain)
        moved = [jnp.sum(value, axis=0, keepdims=True) for value in moved]
        groups.append(jnp.concatenate(moved, axis=0))
    sums = jnp.concatenate(
        [sums[0:3], jnp.concatenate(groups, axis=1), jnp.zeros((BACK - 6, PLACES), F32)], axis=0
    )
    return jnp.where(row < runs[0:1, 0:1], sums, 0.0)


def send_back(red, perm, runs, largest, a_s, w_s, col, tg, later, sent, red_last, sums_s):
    last = QUADS - 1
    for at in range(last):
        sums_s[at] = reduced(red.at[at], runs.at[at])
    backward_whole(
        runs.at[last], a_s, w_s, col, tg, later, red_last
    )
    sums = [sums_s[at] for at in range(last)] + [reduced(red_last, runs.at[last])]
    swap = [largest[:, 0:1] == float(q) for q in range(last)]
    moved = sums[last]
    for q in range(last):
        moved = jnp.where(swap[q], sums[q], moved)
    sums = [jnp.where(swap[q], sums[last], sums[q]) for q in range(last)] + [moved]
    parts = [jnp.concatenate(three_parts(p), axis=0).astype(BF16) for p in sums]
    placed = [jnp.dot(p, perm[q], preferred_element_type=F32) for q, p in enumerate(parts)]
    placed = [(p[2 * BACK :] + p[BACK : 2 * BACK]) + p[0:BACK] for p in placed]
    back = [jnp.concatenate([p[:, c * GS : (c + 1) * GS] for c in range(CAP)], axis=0).T for p in placed]
    for j in range(QUADS // 2):
        sent[:, j, :] = jnp.concatenate([back[2 * j], back[2 * j + 1]], axis=1)


def unpack_kernel(
    red, perm, runs, largest, a_s, w_s, col, tg, later, own_ref, angles_ref, parts_ref, move_ref, basis_ref,
    sent_ref, red_last, sums_s, ret_ref, part_ref, sems
):
    greet()
    me, view = peers()
    send_back(red, perm, runs, largest, a_s, w_s, col, tg, later, sent_ref, red_last, sums_s)
    ret_ref[me] = sent_ref[me]
    slot = own_ref[0:1, :].astype(jnp.int32)
    owner = jnp.where(iota((GS, G), 0) == (slot >> 5), 1.0, 0.0).astype(BF16)
    owner = jnp.concatenate([owner] * 3, axis=0)
    place = slot & 31
    greeted()
    deal(sent_ref, ret_ref, sems.at[0], sems.at[1])
    polar = jnp.concatenate([angles_ref[v, 0:1, :] for v in range(VIEWS)], axis=0)
    azimuth = jnp.concatenate([angles_ref[v, 1:2, :] for v in range(VIEWS)], axis=0)
    for k, values in enumerate(sh_basis(polar, azimuth)):
        basis_ref[k] = values
    settle(ret_ref, GS - 1, sems.at[1])
    both = jnp.concatenate([ret_ref[:, j, :] for j in range(QUADS // 2)], axis=1)
    parts = jnp.concatenate(three_parts(both), axis=0).astype(BF16)
    spread = lax.dot_general(parts, owner, (((0,), (0,)), ((), ())), preferred_element_type=F32)
    found = [spread[i * BACK : (i + 1) * BACK, :] for i in range(QUADS * CAP)]
    for bit in range(5):
        odd = ((place >> bit) & 1) == 1
        found = [jnp.where(odd, found[i + 1], found[i]) for i in range(0, len(found), 2)]
    total = found[0]
    m, n, a, b, c = (own_ref[k : k + 1, :] for k in range(1, 6))
    plain = total[5:6, :]
    du = total[3:4, :] - m * plain
    dw = total[4:5, :] - n * plain
    part_ref[0:3, :] = total[0:3, :]
    part_ref[3:4, :] = plain
    spread_views(part_ref, parts_ref, sems.at[2], sems.at[3])
    parts_ref[view] = part_ref[...]
    move_ref[0:1, :] = a * du + b * dw
    move_ref[1:2, :] = b * du + c * dw
    settle(parts_ref, VIEWS - 1, sems.at[3])
    settle(ret_ref, GS - 1, sems.at[0])
    settle(parts_ref, VIEWS - 1, sems.at[2])


def final_kernel(part_ref, move_ref, basis_ref, own_ref, image_ref, sh_ref, logit_grad_ref, mean_grad_ref, img_ref):
    mean_grad_ref[...] = move_ref[...]
    img_ref[...] = image_ref[...]
    plain = part_ref[0, 3:4, :]
    for v in range(1, VIEWS):
        plain = plain + part_ref[v, 3:4, :]
    logit_grad_ref[...] = plain * (1.0 - jax.nn.sigmoid(own_ref[6:7, :]))
    for k in range(16):
        total = part_ref[0, 0:3, :] * basis_ref[k, 0:1, :]
        for v in range(1, VIEWS):
            total = total + part_ref[v, 0:3, :] * basis_ref[k, v : v + 1, :]
        sh_ref[3 * k : 3 * k + 3, :] = total


MESH = pl.DeviceIdType.MESH
VM = pl.BlockSpec(memory_space=pltpu.VMEM)


def call(kernel, ins, outs, scratch=(), limit=20, remote=None, far=False):
    extra = {} if remote is None else dict(collective_id=remote, has_side_effects=True)
    shapes = [o if isinstance(o, jax.ShapeDtypeStruct) else jax.ShapeDtypeStruct(o, F32) for o in outs]
    return pl.pallas_call(
        kernel,
        out_shape=shapes,
        in_specs=[pl.BlockSpec(memory_space=pltpu.HBM) if far else VM] * len(ins),
        out_specs=[VM] * len(shapes),
        scratch_shapes=list(scratch),
        compiler_params=pltpu.CompilerParams(vmem_limit_bytes=limit * 2**20, **extra),
    )(*ins)


def pack(*ins):
    return call(
        pack_kernel,
        [pltpu.with_memory_space_constraint(i, pltpu.HBM) for i in ins],
        [
            (GS, ROWS, 128),
            (VIEWS, 2, G),
            (OWN, G),
            (QUADS, 72, 128),
            jax.ShapeDtypeStruct((4 * WIDE, FORMS * 128), BF16),
            (PLACES, 128),
            (PLACES, 128),
        ],
        [pltpu.VMEM(i.shape, i.dtype) for i in ins]
        + [
            pltpu.VMEM((GS, ROWS, 128), F32),
            pltpu.VMEM((SENT, G), F32),
            pltpu.SemaphoreType.DMA((4,)),
            pltpu.SemaphoreType.DMA((len(ins),)),
        ],
        remote=0,
        far=True,
    )


def render(*ins):
    return call(
        render_kernel,
        ins,
        [
            (3, QUADS, PIX),
            (QUADS - 1, PLACES, 5 * 128),
            jax.ShapeDtypeStruct((QUADS, PLACES, PLACES), BF16),
            (QUADS, 8, 128),
            (8, 128),
            (PLACES, PIX),
            (PLACES, PIX),
            (PLACES, 3 * 128),
            (3, 8, PIX),
            (8, PIX),
        ],
        [
            pltpu.VMEM((QUADS, PLACES, FORMS * 128), F32),
            pltpu.VMEM((QUADS - 1, PLACES, PIX), F32),
            pltpu.VMEM((QUADS - 1, PLACES, PIX), F32),
            pltpu.VMEM((QUADS - 1, 3, 8, PIX), F32),
            pltpu.VMEM((QUADS - 1, 8, PIX), F32),
            pltpu.VMEM((QUADS, 8, PIX), F32),
            pltpu.VMEM((QUADS, 3, 8, PIX), F32),
            pltpu.VMEM((QUADS, 24, 128), F32),
            pltpu.VMEM((QUADS, 24, 128), F32),
            pltpu.VMEM((QUADS, 3, PIX), F32),
            pltpu.SMEM((QUADS,), jnp.int32),
        ],
        limit=RENDER_MIB,
    )


def unpack(*ins):
    return call(
        unpack_kernel,
        ins,
        [(VIEWS, 4, G), (2, G), (16, VIEWS, G)],
        [
            pltpu.VMEM((GS, QUADS // 2, 128), F32),
            pltpu.VMEM((PLACES, 5 * 128), F32),
            pltpu.VMEM((QUADS - 1, BACK, PLACES), F32),
            pltpu.VMEM((GS, QUADS // 2, 128), F32),
            pltpu.VMEM((4, G), F32),
            pltpu.SemaphoreType.DMA((4,)),
        ],
        limit=UNPACK_MIB,
        remote=1,
    )


def final(*ins):
    return call(final_kernel, ins, [(48, G), (1, G), (2, G), (3, QUADS, PIX)])


def local(sh_coef, opacity_logit, view_angle, mean_pos, conic, send_slot, depth_rank, target):
    arrived, angles, own, *prepared = pack(
        sh_coef,
        opacity_logit.reshape(1, G),
        view_angle[0],
        mean_pos[0],
        jnp.transpose(conic, (1, 0, 2)),
        send_slot,
        depth_rank,
        jnp.transpose(target[0], (1, 0, 2)),
    )
    images, *blended = render(arrived, *prepared)
    parts, move, basis = unpack(*blended, own, angles)
    sh_grad, logit_grad, mean_grad, images = final(parts, move, basis, own, images)
    return (sh_grad, logit_grad.reshape(G), mean_grad[None], jnp.transpose(images, (1, 0, 2))[None])


def solution(mesh):
    return jax.shard_map(
        local,
        mesh=mesh,
        in_specs=(
            P(None, "gs"),
            P("gs"),
            P("view", None, "gs"),
            P("view", None, "gs"),
            P("view", None, "gs"),
            P("view", "gs"),
            P("view", "gs"),
            P("view", "gs", None, None),
        ),
        out_specs=(P(None, "gs"), P("gs"), P("view", None, "gs"), P("view", "gs", None, None)),
        check_vma=False,
    )
```

```python
import jax
import jax.numpy as jnp
from jax import lax
from jax.experimental import pallas as pl
from jax.experimental.pallas import tpu as pltpu
from jax.sharding import PartitionSpec as P

F32 = jnp.float32
BF16 = jnp.bfloat16

SH_ZERO = 0.28209479177387814
SH_ONE = 0.4886025119029199
SH_TWO = (
    1.0925484305920792,
    -1.0925484305920792,
    0.31539156525252005,
    -1.0925484305920792,
    0.5462742152960396,
)
SH_THREE = (
    -0.5900435899266435,
    2.890611442640554,
    -0.4570457994644658,
    0.3731763325901154,
    -0.4570457994644658,
    1.445305721320277,
    -0.5900435899266435,
)
SSIM_MEAN = 0.0001
SSIM_SPREAD = 0.0009

GS = 64
VIEWS = 4
QUADS = 4
CAP = 8
G = 1024
PLACES = GS * CAP
PIX = 1024
TILES = PIX // 128
WIDE = 16
COL, KEY = 6, 9
SENT = 12
ROWS = QUADS * CAP * SENT // 128
BACK = 8
OWN = 7
SHIFT = 64.0
LOG2E = 1.4426950408889634
HALF = 8
PASSES = 8 // HALF
UNROLL = 8
RENDER_MIB = 36
UNPACK_MIB = 24
FORMS = 2 * PASSES + 4


def iota(shape, axis):
    return lax.broadcasted_iota(jnp.int32, shape, axis)


def sh_basis(polar, azimuth):
    across = jnp.sin(polar)
    x = across * jnp.cos(azimuth)
    y = across * jnp.sin(azimuth)
    z = jnp.cos(polar)
    xx, yy, zz = x * x, y * y, z * z
    return [
        jnp.full_like(x, SH_ZERO),
        -SH_ONE * y,
        SH_ONE * z,
        -SH_ONE * x,
        SH_TWO[0] * x * y,
        SH_TWO[1] * y * z,
        SH_TWO[2] * (2.0 * zz - xx - yy),
        SH_TWO[3] * x * z,
        SH_TWO[4] * (xx - yy),
        SH_THREE[0] * y * (3.0 * xx - yy),
        SH_THREE[1] * x * y * z,
        SH_THREE[2] * y * (4.0 * zz - xx - yy),
        SH_THREE[3] * z * (2.0 * zz - 3.0 * xx - 3.0 * yy),
        SH_THREE[4] * x * (4.0 * zz - xx - yy),
        SH_THREE[5] * z * (xx - yy),
        SH_THREE[6] * x * (xx - 3.0 * yy),
    ]


def three_parts(values):
    high = values.astype(BF16).astype(F32)
    rest = values - high
    middle = rest.astype(BF16).astype(F32)
    return high, middle, rest - middle


def centre(mean):
    return mean * 32.0 - 16.5


def peers():
    return lax.axis_index("gs"), lax.axis_index("view")


def far_first(me):
    across = [((me // 16 + d) % 4) * 16 for d in range(4)]
    along = [((me // 2 + d) % 8) * 2 for d in range(8)]
    core = [me % 2, 1 - me % 2]
    steps = [(x, z, c) for x in range(4) for z in range(8) for c in range(2)]
    steps.sort(key=lambda s: (-min(s[0], 4 - s[0]) - min(s[1], 8 - s[1]), -s[2]))
    return [across[x] + along[z] + core[c] for x, z, c in steps if (x, z, c) != (0, 0, 0)]


def greet(between=()):
    me, view = peers()
    barrier = pltpu.get_barrier_semaphore()
    for n, other in enumerate(far_first(me)):
        if n == 16:
            for copy in between:
                copy.start()
        pl.semaphore_signal(barrier, inc=1, device_id=(other, view), device_id_type=MESH)
    for d in range(1, VIEWS):
        pl.semaphore_signal(barrier, inc=1, device_id=(me, lax.rem(view + d, VIEWS)), device_id_type=MESH)


def greeted():
    pl.semaphore_wait(pltpu.get_barrier_semaphore(), GS - 1 + VIEWS - 1)


def deal(sent, got, send_sem, recv_sem):
    me, view = peers()
    for other in far_first(me):
        pltpu.make_async_remote_copy(
            src_ref=sent.at[other],
            dst_ref=got.at[me],
            send_sem=send_sem,
            recv_sem=recv_sem,
            device_id=(other, view),
            device_id_type=MESH,
        ).start()


def spread_views(mine, got, send_sem, recv_sem):
    me, view = peers()
    for d in (2, 1, 3):
        pltpu.make_async_remote_copy(
            src_ref=mine,
            dst_ref=got.at[view],
            send_sem=send_sem,
            recv_sem=recv_sem,
            device_id=(me, lax.rem(view + d, VIEWS)),
            device_id_type=MESH,
        ).start()


def settle(whole, count, sem):
    part = whole.at[pl.ds(0, count)]
    pltpu.make_async_copy(part, part, sem).wait()


def pack_kernel(*refs):
    far, outs, rest = refs[:8], refs[8:15], refs[15:]
    arr_ref, angles_ref, own_ref, tgt, mono, step_s, sub_s = outs
    near, (out_ref, pay, sems, load_sems) = rest[:8], rest[8:]
    loads = [
        pltpu.make_async_copy(src, dst, load_sems.at[k]) for k, (src, dst) in enumerate(zip(far, near))
    ]
    greet(loads)
    for load in loads:
        load.wait()
    sh_ref, logit_ref, angle_ref, mean_ref, conic_ref, slot_ref, rank_ref, tgt_ref = near
    me, view = peers()
    angles_ref[view] = angle_ref[...]
    basis = sh_basis(angle_ref[0:1, :], angle_ref[1:2, :])
    colour = jnp.full((3, G), 0.5, F32)
    for k in range(16):
        colour = colour + sh_ref[3 * k : 3 * k + 3, :] * basis[k]
    m, n = centre(mean_ref[0:1, :]), centre(mean_ref[1:2, :])
    kept = [slot_ref[...].astype(F32), m, n] + [conic_ref[k] * (1.0 / 32.0) for k in range(3)]
    for k, row in enumerate(kept + [logit_ref[...]]):
        own_ref[k : k + 1, :] = row
    scale = LOG2E / 1024.0
    opacity = 0.99 * jax.nn.sigmoid(logit_ref[...])
    a, b, c = (conic_ref[k] * scale for k in range(3))
    pay[...] = jnp.zeros((SENT, G), F32)
    away = 0.5 * (a * m * m + 2.0 * b * m * n + c * n * n)
    pay[0:1, :] = (jnp.log(opacity) * LOG2E + SHIFT) - away
    pay[1:2, :] = a * m + b * n
    pay[2:3, :] = b * m + c * n
    pay[3:4, :] = -0.5 * a
    pay[4:5, :] = -b
    pay[5:6, :] = -0.5 * c
    pay[COL : COL + 3, :] = colour
    pay[KEY : KEY + 1, :] = (rank_ref[...] + 1).astype(F32)
    parts = three_parts(pay[...])
    slot = slot_ref[...]
    owner = jnp.where(iota((GS, G), 0) == (slot >> 5), 1.0, 0.0).astype(BF16)
    place = (slot & 31) - jnp.where(iota((2 * SENT, G), 0) >= SENT, 1, 0)
    total = jnp.zeros((GS, ROWS * 128), F32)
    for part in parts[::-1]:
        pair = jnp.concatenate([part, part], axis=0)
        spread = jnp.concatenate(
            [jnp.where(place == i, pair, 0.0) for i in range(0, QUADS * CAP, 2)], axis=0
        ).astype(BF16)
        total = total + lax.dot_general(
            owner, spread, (((1,), (1,)), ((), ())), preferred_element_type=F32
        )
    for r in range(ROWS):
        out_ref[:, r, :] = total[:, tile(r)]
    arr_ref[me] = out_ref[me]
    mono[...] = monomials()
    at = iota((PLACES, 128), 0)
    step_s[...] = (at >> 3).astype(F32)
    sub_s[...] = (at & 7).astype(F32)
    for q in range(QUADS):
        for c in range(3):
            for t in range(TILES):
                tgt[q, c * 8 + t : c * 8 + t + 1, :] = tgt_ref[c, q : q + 1, tile(t)]
    for q in range(QUADS):
        y = tgt[q, 0:24, :]
        means = window_means(jnp.concatenate([y, y * y], axis=0))
        tgt[q, 24:48, :] = means[0:24]
        tgt[q, 48:72, :] = means[24:48] - means[0:24] * means[0:24]
    greeted()
    deal(out_ref, arr_ref, sems.at[0], sems.at[1])
    spread_views(angle_ref, angles_ref, sems.at[2], sems.at[3])
    settle(arr_ref, GS - 1, sems.at[1])
    settle(angles_ref, VIEWS - 1, sems.at[3])
    settle(arr_ref, GS - 1, sems.at[0])
    settle(angles_ref, VIEWS - 1, sems.at[2])


def monomials():
    lane = iota((WIDE, 128), 1)
    row = iota((WIDE, 128), 0)
    u = ((lane & 31) - 16).astype(F32)
    top = ((lane >> 5) - 16).astype(F32)

    def rows(entries):
        out = jnp.zeros((WIDE, 128), F32)
        for k, value in entries.items():
            out = jnp.where(row == k, value, out)
        return out

    def power(w):
        return rows({0: 1.0, 1: u, 2: w, 3: u * u, 4: u * w, 5: w * w})

    def first(w):
        return rows({2: 4.0, 4: 4.0 * u, 5: 8.0 * w + 16.0})

    tiles = []
    for h in range(PASSES):
        tiles += [power(top + 4.0 * HALF * h), first(top + 4.0 * HALF * h)]
    tiles.append(rows({5: 32.0}))
    tiles += [rows({COL + c: 1.0}) for c in range(3)]
    base = jnp.concatenate(tiles, axis=1)
    shift = jnp.where(
        (iota((WIDE, 128), 0) == 0) & (iota((WIDE, 128), 1) >= 0), -SHIFT, 0.0
    )
    none = jnp.zeros((WIDE, 128), F32)
    shift = jnp.concatenate([shift, none] * PASSES + [none] * 4, axis=1)
    return jnp.concatenate([base, base, base, shift], axis=0).astype(BF16)


def window_means(values):
    lane = iota((128, 128), 1)
    other = iota((128, 128), 0)
    same = ((lane & 31) >> 2) == ((other & 31) >> 2)
    pool = jnp.where(same, 1.0 / 16.0, 0.0).astype(BF16)
    rows = values.shape[0]
    sums = jnp.dot(
        jnp.concatenate(three_parts(values), axis=0).astype(BF16), pool, preferred_element_type=F32
    )
    return (sums[2 * rows :] + sums[rows : 2 * rows]) + sums[0:rows]


def loss_slope(x, y, my, vy):
    rows = x.shape[0]
    means = window_means(jnp.concatenate([x, x * x, x * y], axis=0))
    mx, exx, exy = (means[k * rows : (k + 1) * rows] for k in range(3))
    n1 = 2.0 * mx * my + SSIM_MEAN
    n2 = 2.0 * (exy - mx * my) + SSIM_SPREAD
    d1 = mx * mx + my * my + SSIM_MEAN
    d2 = (exx - mx * mx) + vy + SSIM_SPREAD
    i1, i2 = 1.0 / d1, 1.0 / d2
    both = i1 * i2
    ratio = n1 * n2 * both
    by_mean = 2.0 * my * (n2 - n1) * both + 2.0 * mx * ratio * (i2 - i1)
    by_square = -ratio * i2
    by_cross = 2.0 * n1 * both
    return 0.1 * (x - y) - (0.2 / 16.0) * (by_mean + 2.0 * x * by_square + y * by_cross)


def shifted(values, by, fill):
    sub = iota(values.shape, 0)
    keep = (sub >= by) if by > 0 else (sub < 8 + by)
    return jnp.where(keep, pltpu.roll(values, by % 8, 0), fill)


def order(blocks, arrived, perm, bc, mono, step_s, sub_s):
    pick = jnp.where((iota((3 * WIDE, 128), 0) & 15) == KEY, 1.0, 0.0).astype(BF16)
    turned = jnp.concatenate([arrived[:, r, :].T for r in range(ROWS)], axis=0)
    rest = jnp.zeros((WIDE - SENT, PLACES), F32)
    packed = []
    for q in blocks:
        places = [turned[i * SENT : (i + 1) * SENT, :] for i in range(q * CAP, (q + 1) * CAP)]
        packed.append(jnp.concatenate([jnp.concatenate(places, axis=1), rest], axis=0))
    parts = [jnp.concatenate(three_parts(p), axis=0).astype(BF16) for p in packed]
    keys = [p[KEY : KEY + 1, :] for p in packed]
    columns = [
        lax.dot_general(p, pick, (((0,), (0,)), ((), ())), preferred_element_type=F32) for p in parts
    ]
    filled = [jnp.sum(jnp.where(k > 0.0, 1.0, 0.0), axis=1, keepdims=True) for k in keys]
    turns = [jnp.floor((f + (8 * UNROLL - 1.0)) * (1.0 / (8 * UNROLL))) for f in filled]
    step, sub = step_s[...], sub_s[...]
    for q, key, column, turn, full in zip(blocks, keys, columns, turns, filled):
        span = turn * UNROLL
        wanted = jnp.where(step < span, sub * span + step + (PLACES - full), -1.0)
        for t in range(PLACES // 128):
            less = jnp.where(column < key[:, tile(t)], 1.0, 0.0)
            rank = jnp.sum(less, axis=0, keepdims=True)
            perm[q, :, tile(t)] = jnp.where(rank == wanted, 1.0, 0.0).astype(BF16)
    ordered = [
        lax.dot_general(p, perm[q], (((1,), (1,)), ((), ())), preferred_element_type=F32)
        for q, p in zip(blocks, parts)
    ]
    ones = jnp.ones((WIDE, PLACES), F32)
    ordered = [jnp.concatenate([o, ones], axis=0).astype(BF16) for o in ordered]
    for q, o in zip(blocks, ordered):
        bc[q] = lax.dot_general(o, mono[...], (((0,), (0,)), ((), ())), preferred_element_type=F32)
    return turns


def unroll_loop(run, body, start):
    def several(i, state):
        for k in range(UNROLL):
            state = body(i * UNROLL + k, state)
        return state

    return lax.fori_loop(0, run // UNROLL, several, start)


def tile(t):
    return slice(t * 128, (t + 1) * 128)


def blend(run, bc, a_s, w_s, col, left, seen):
    one = jnp.ones((8, 128), F32)
    zero = jnp.zeros((8, 128), F32)
    for h in range(PASSES):

        def ahead(i, state, h=h):
            passing, got = list(state[0]), [list(s) for s in state[1]]
            rows = pl.ds(pl.multiple_of(i * 8, 8), 8)
            power, first = bc[rows, tile(2 * h)], bc[rows, tile(2 * h + 1)]
            second = bc[rows, tile(2 * PASSES)]
            colours = [bc[rows, tile(2 * PASSES + 1 + c)] for c in range(3)]
            if h == 0 and col is not None:
                for c in range(3):
                    col[rows, tile(c)] = colours[c]
            for t in range(HALF):
                alpha = jnp.exp2(power)
                weight = passing[t] * alpha
                passing[t] = passing[t] - weight
                a_s[rows, tile(h * HALF + t)] = alpha
                w_s[rows, tile(h * HALF + t)] = weight
                for c in range(3):
                    got[c][t] = got[c][t] + colours[c] * weight
                if t < HALF - 1:
                    power = power + first
                    first = first + second
            return tuple(passing), tuple(tuple(s) for s in got)

        passing, got = unroll_loop(run, ahead, ((one,) * HALF, ((zero,) * HALF,) * 3))
        for t in range(HALF):
            left[:, tile(h * HALF + t)] = passing[t]
            for c in range(3):
                seen[c, :, tile(h * HALF + t)] = got[c][t]


def back_step(i, later, a_s, w_s, col, tg, red):
    zero = jnp.zeros((8, 128), F32)
    later = list(later)
    rows = pl.ds(pl.multiple_of(i * 8, 8), 8)
    c0, c1, c2 = (col[rows, tile(c)] for c in range(3))
    plain, graded = zero, zero
    sums = [zero, zero, zero]
    for t in range(TILES - 1, -1, -1):
        alpha, weight = a_s[rows, tile(t)], w_s[rows, tile(t)]
        g0, g1, g2 = (tg[c, :, tile(t)] for c in range(3))
        gap = c0 * g0 + c1 * g1 + c2 * g2 - later[t]
        later[t] = later[t] + alpha * gap
        plain = plain + weight * gap
        if t:
            graded = graded + plain
        sums = [sums[0] + weight * g0, sums[1] + weight * g1, sums[2] + weight * g2]
    for k, value in enumerate(sums + [plain, graded]):
        red[rows, tile(k)] = value
    return tuple(later)


def backward(run, a_s, w_s, col, tg, later, red):
    def back(i, state):
        return back_step(run - 1 - i, state, a_s, w_s, col, tg, red)

    unroll_loop(run, back, tuple(later[:, tile(t)] for t in range(TILES)))


def backward_whole(runs, a_s, w_s, col, tg, later, red):
    steps = PLACES // 8
    begin = tuple(later[:, tile(t)] for t in range(TILES))
    last = runs[...] * (1.0 / 8.0) - 1.0

    def several(n, state):
        for k in range(8):
            i = steps - 1 - (n * 8 + k)
            here = last == i.astype(F32)
            state = [jnp.where(here, b, v) for b, v in zip(begin, state)]
            state = back_step(i, state, a_s, w_s, col, tg, red)
        return tuple(state)

    lax.fori_loop(0, steps // 8, several, begin)


def join(left, seen, pic, slope, tgt, tg, later, image):
    before = shifted(left[...], 1, 1.0)
    for by in (1, 2, 4):
        before = before * shifted(before, by, 1.0)
    for c in range(3):
        row = jnp.sum(before * seen[c], axis=0, keepdims=True)
        image[c : c + 1, :] = row
        for t in range(TILES):
            pic[c * 8 + t : c * 8 + t + 1, :] = row[:, tile(t)]
    slope[...] = loss_slope(pic[...], *(tgt[24 * k : 24 * k + 24, :] for k in range(3)))
    behind = jnp.zeros((8, PIX), F32)
    for c in range(3):
        row = jnp.concatenate([slope[c * 8 + t : c * 8 + t + 1, :] for t in range(TILES)], axis=1)
        behind = behind + row * seen[c]
        tg[c] = before * row
    value, factor = shifted(behind, -1, 0.0), shifted(left[...], -1, 0.0)
    for by in (1, 2, 4):
        value = value + factor * shifted(value, -by, 0.0)
        factor = factor * shifted(factor, -by, 0.0)
    later[...] = before * value


def render_kernel(
    arr_ref, tgt, mono, step_s, sub_s,
    img_ref, red, perm, runs, largest, a_last, w_last, col_last, tg_last, later_last,
    bc, a_s, w_s, tg, later, left, seen, pic, slope, image, runs_s
):
    found = order(list(range(QUADS)), arr_ref, perm, bc, mono, step_s, sub_s)
    for q, turn in enumerate(found):
        runs_s[q] = jnp.sum(turn).astype(jnp.int32) * UNROLL
    best = jnp.int32(0)
    for q in range(1, QUADS):
        best = jnp.where(runs_s[q] > runs_s[best], q, best)
    last = QUADS - 1
    largest[...] = jnp.full((8, 128), best, jnp.int32).astype(F32)

    def block(at):
        return jnp.where(at == best, last, jnp.where(at == last, best, at))

    def first(at, carry):
        q = block(at)
        blend(runs_s[q], bc.at[q], a_s.at[at], w_s.at[at], None, left.at[at], seen.at[at])
        return carry

    def second(at, carry):
        q = block(at)
        col = bc.at[q, :, pl.ds((2 * PASSES + 1) * 128, 3 * 128)]
        backward(runs_s[q], a_s.at[at], w_s.at[at], col, tg.at[at], later.at[at], red.at[at])
        return carry

    lax.fori_loop(0, last, first, 0)
    blend(runs_s[best], bc.at[best], a_last, w_last, col_last, left.at[last], seen.at[last])
    for at in range(QUADS):
        q = block(at)
        runs[at] = jnp.full((8, 128), 8 * runs_s[q], jnp.int32).astype(F32)
        to = (tg_last, later_last) if at == last else (tg.at[at], later.at[at])
        join(left.at[at], seen.at[at], pic.at[at], slope.at[at], tgt.at[q], *to, image.at[q])
    lax.fori_loop(0, last, second, 0)
    for q in range(QUADS):
        for c in range(3):
            img_ref[c, q : q + 1, :] = image[q, c : c + 1, :]


def reduced(red, runs):
    pixel = iota((128, 128), 0)
    across = ((pixel & 31) - 16).astype(F32)
    down = ((pixel >> 5) - 16).astype(F32)
    row = iota((BACK, PLACES), 1).astype(F32)
    colour = red[:, 0 : 3 * 128]
    high = colour.astype(BF16)
    low = (colour - high.astype(F32)).astype(BF16)
    pick = jnp.where(iota((BACK, 3 * 128), 1) >> 7 == iota((BACK, 3 * 128), 0), 1.0, 0.0).astype(BF16)
    nt = (((1,), (1,)), ((), ()))
    sums = lax.dot_general(pick, low, nt, preferred_element_type=F32) + lax.dot_general(
        pick, high, nt, preferred_element_type=F32
    )
    groups = []
    for n in range(PLACES // 128):
        plain, graded = (red[tile(n), tile(k)].T for k in (3, 4))
        moved = (plain * across, plain * down + 4.0 * graded, plain)
        moved = [jnp.sum(value, axis=0, keepdims=True) for value in moved]
        groups.append(jnp.concatenate(moved, axis=0))
    sums = jnp.concatenate(
        [sums[0:3], jnp.concatenate(groups, axis=1), jnp.zeros((BACK - 6, PLACES), F32)], axis=0
    )
    return jnp.where(row < runs[0:1, 0:1], sums, 0.0)


def send_back(red, perm, runs, largest, a_s, w_s, col, tg, later, sent, red_last, sums_s):
    last = QUADS - 1
    for at in range(last):
        sums_s[at] = reduced(red.at[at], runs.at[at])
    backward_whole(
        runs.at[last], a_s, w_s, col, tg, later, red_last
    )
    sums = [sums_s[at] for at in range(last)] + [reduced(red_last, runs.at[last])]
    swap = [largest[:, 0:1] == float(q) for q in range(last)]
    moved = sums[last]
    for q in range(last):
        moved = jnp.where(swap[q], sums[q], moved)
    sums = [jnp.where(swap[q], sums[last], sums[q]) for q in range(last)] + [moved]
    parts = [jnp.concatenate(three_parts(p), axis=0).astype(BF16) for p in sums]
    placed = [jnp.dot(p, perm[q], preferred_element_type=F32) for q, p in enumerate(parts)]
    placed = [(p[2 * BACK :] + p[BACK : 2 * BACK]) + p[0:BACK] for p in placed]
    back = [jnp.concatenate([p[:, c * GS : (c + 1) * GS] for c in range(CAP)], axis=0).T for p in placed]
    for j in range(QUADS // 2):
        sent[:, j, :] = jnp.concatenate([back[2 * j], back[2 * j + 1]], axis=1)


def unpack_kernel(
    red, perm, runs, largest, a_s, w_s, col, tg, later, own_ref, angles_ref, parts_ref, move_ref, basis_ref,
    sent_ref, red_last, sums_s, ret_ref, part_ref, sems
):
    greet()
    me, view = peers()
    send_back(red, perm, runs, largest, a_s, w_s, col, tg, later, sent_ref, red_last, sums_s)
    ret_ref[me] = sent_ref[me]
    slot = own_ref[0:1, :].astype(jnp.int32)
    owner = jnp.where(iota((GS, G), 0) == (slot >> 5), 1.0, 0.0).astype(BF16)
    owner = jnp.concatenate([owner] * 3, axis=0)
    place = slot & 31
    greeted()
    deal(sent_ref, ret_ref, sems.at[0], sems.at[1])
    polar = jnp.concatenate([angles_ref[v, 0:1, :] for v in range(VIEWS)], axis=0)
    azimuth = jnp.concatenate([angles_ref[v, 1:2, :] for v in range(VIEWS)], axis=0)
    for k, values in enumerate(sh_basis(polar, azimuth)):
        for v in range(VIEWS):
            basis_ref[v, 3 * k : 3 * k + 3, :] = jnp.broadcast_to(values[v : v + 1, :], (3, G))
    settle(ret_ref, GS - 1, sems.at[1])
    both = jnp.concatenate([ret_ref[:, j, :] for j in range(QUADS // 2)], axis=1)
    parts = jnp.concatenate(three_parts(both), axis=0).astype(BF16)
    spread = lax.dot_general(parts, owner, (((0,), (0,)), ((), ())), preferred_element_type=F32)
    found = [spread[i * BACK : (i + 1) * BACK, :] for i in range(QUADS * CAP)]
    for bit in range(5):
        odd = ((place >> bit) & 1) == 1
        found = [jnp.where(odd, found[i + 1], found[i]) for i in range(0, len(found), 2)]
    total = found[0]
    m, n, a, b, c = (own_ref[k : k + 1, :] for k in range(1, 6))
    plain = total[5:6, :]
    du = total[3:4, :] - m * plain
    dw = total[4:5, :] - n * plain
    part_ref[0:3, :] = total[0:3, :]
    part_ref[3:4, :] = plain
    spread_views(part_ref, parts_ref, sems.at[2], sems.at[3])
    parts_ref[view] = part_ref[...]
    move_ref[0:1, :] = a * du + b * dw
    move_ref[1:2, :] = b * du + c * dw
    settle(parts_ref, VIEWS - 1, sems.at[3])
    settle(ret_ref, GS - 1, sems.at[0])
    settle(parts_ref, VIEWS - 1, sems.at[2])


def final_kernel(part_ref, move_ref, basis_ref, own_ref, image_ref, sh_ref, logit_grad_ref, mean_grad_ref, img_ref):
    mean_grad_ref[...] = move_ref[...]
    img_ref[...] = image_ref[...]
    plain = part_ref[0, 3:4, :]
    for v in range(1, VIEWS):
        plain = plain + part_ref[v, 3:4, :]
    logit_grad_ref[...] = plain * (1.0 - jax.nn.sigmoid(own_ref[6:7, :]))
    colours = [jnp.concatenate([part_ref[v, 0:3, :]] * 8, axis=0) for v in range(VIEWS)]
    for half in (slice(0, 24), slice(24, 48)):
        total = colours[0] * basis_ref[0, half, :]
        for v in range(1, VIEWS):
            total = total + colours[v] * basis_ref[v, half, :]
        sh_ref[half, :] = total


MESH = pl.DeviceIdType.MESH
VM = pl.BlockSpec(memory_space=pltpu.VMEM)


def call(kernel, ins, outs, scratch=(), limit=20, remote=None, far=False):
    extra = {} if remote is None else dict(collective_id=remote, has_side_effects=True)
    shapes = [o if isinstance(o, jax.ShapeDtypeStruct) else jax.ShapeDtypeStruct(o, F32) for o in outs]
    return pl.pallas_call(
        kernel,
        out_shape=shapes,
        in_specs=[pl.BlockSpec(memory_space=pltpu.HBM) if far else VM] * len(ins),
        out_specs=[VM] * len(shapes),
        scratch_shapes=list(scratch),
        compiler_params=pltpu.CompilerParams(vmem_limit_bytes=limit * 2**20, **extra),
    )(*ins)


def pack(*ins):
    return call(
        pack_kernel,
        [pltpu.with_memory_space_constraint(i, pltpu.HBM) for i in ins],
        [
            (GS, ROWS, 128),
            (VIEWS, 2, G),
            (OWN, G),
            (QUADS, 72, 128),
            jax.ShapeDtypeStruct((4 * WIDE, FORMS * 128), BF16),
            (PLACES, 128),
            (PLACES, 128),
        ],
        [pltpu.VMEM(i.shape, i.dtype) for i in ins]
        + [
            pltpu.VMEM((GS, ROWS, 128), F32),
            pltpu.VMEM((SENT, G), F32),
            pltpu.SemaphoreType.DMA((4,)),
            pltpu.SemaphoreType.DMA((len(ins),)),
        ],
        remote=0,
        far=True,
    )


def render(*ins):
    return call(
        render_kernel,
        ins,
        [
            (3, QUADS, PIX),
            (QUADS - 1, PLACES, 5 * 128),
            jax.ShapeDtypeStruct((QUADS, PLACES, PLACES), BF16),
            (QUADS, 8, 128),
            (8, 128),
            (PLACES, PIX),
            (PLACES, PIX),
            (PLACES, 3 * 128),
            (3, 8, PIX),
            (8, PIX),
        ],
        [
            pltpu.VMEM((QUADS, PLACES, FORMS * 128), F32),
            pltpu.VMEM((QUADS - 1, PLACES, PIX), F32),
            pltpu.VMEM((QUADS - 1, PLACES, PIX), F32),
            pltpu.VMEM((QUADS - 1, 3, 8, PIX), F32),
            pltpu.VMEM((QUADS - 1, 8, PIX), F32),
            pltpu.VMEM((QUADS, 8, PIX), F32),
            pltpu.VMEM((QUADS, 3, 8, PIX), F32),
            pltpu.VMEM((QUADS, 24, 128), F32),
            pltpu.VMEM((QUADS, 24, 128), F32),
            pltpu.VMEM((QUADS, 3, PIX), F32),
            pltpu.SMEM((QUADS,), jnp.int32),
        ],
        limit=RENDER_MIB,
    )


def unpack(*ins):
    return call(
        unpack_kernel,
        ins,
        [(VIEWS, 4, G), (2, G), (VIEWS, 48, G)],
        [
            pltpu.VMEM((GS, QUADS // 2, 128), F32),
            pltpu.VMEM((PLACES, 5 * 128), F32),
            pltpu.VMEM((QUADS - 1, BACK, PLACES), F32),
            pltpu.VMEM((GS, QUADS // 2, 128), F32),
            pltpu.VMEM((4, G), F32),
            pltpu.SemaphoreType.DMA((4,)),
        ],
        limit=UNPACK_MIB,
        remote=1,
    )


def final(*ins):
    return call(final_kernel, ins, [(48, G), (1, G), (2, G), (3, QUADS, PIX)])


def local(sh_coef, opacity_logit, view_angle, mean_pos, conic, send_slot, depth_rank, target):
    arrived, angles, own, *prepared = pack(
        sh_coef,
        opacity_logit.reshape(1, G),
        view_angle[0],
        mean_pos[0],
        jnp.transpose(conic, (1, 0, 2)),
        send_slot,
        depth_rank,
        jnp.transpose(target[0], (1, 0, 2)),
    )
    images, *blended = render(arrived, *prepared)
    parts, move, basis = unpack(*blended, own, angles)
    sh_grad, logit_grad, mean_grad, images = final(parts, move, basis, own, images)
    return (sh_grad, logit_grad.reshape(G), mean_grad[None], jnp.transpose(images, (1, 0, 2))[None])


def solution(mesh):
    return jax.shard_map(
        local,
        mesh=mesh,
        in_specs=(
            P(None, "gs"),
            P("gs"),
            P("view", None, "gs"),
            P("view", None, "gs"),
            P("view", None, "gs"),
            P("view", "gs"),
            P("view", "gs"),
            P("view", "gs", None, None),
        ),
        out_specs=(P(None, "gs"), P("gs"), P("view", None, "gs"), P("view", "gs", None, None)),
        check_vma=False,
    )
```

```python
import jax
import jax.numpy as jnp
from jax import lax
from jax.experimental import pallas as pl
from jax.experimental.pallas import tpu as pltpu
from jax.sharding import PartitionSpec as P

F32 = jnp.float32
BF16 = jnp.bfloat16

SH_ZERO = 0.28209479177387814
SH_ONE = 0.4886025119029199
SH_TWO = (
    1.0925484305920792,
    -1.0925484305920792,
    0.31539156525252005,
    -1.0925484305920792,
    0.5462742152960396,
)
SH_THREE = (
    -0.5900435899266435,
    2.890611442640554,
    -0.4570457994644658,
    0.3731763325901154,
    -0.4570457994644658,
    1.445305721320277,
    -0.5900435899266435,
)
SSIM_MEAN = 0.0001
SSIM_SPREAD = 0.0009

GS = 64
VIEWS = 4
QUADS = 4
CAP = 8
G = 1024
PLACES = GS * CAP
PIX = 1024
TILES = PIX // 128
WIDE = 16
COL, KEY = 6, 9
SENT = 12
ROWS = QUADS * CAP * SENT // 128
BACK = 8
OWN = 7
SHIFT = 64.0
LOG2E = 1.4426950408889634
HALF = 8
PASSES = 8 // HALF
UNROLL = 8
RENDER_MIB = 36
UNPACK_MIB = 24
FORMS = 2 * PASSES + 4


def iota(shape, axis):
    return lax.broadcasted_iota(jnp.int32, shape, axis)


def sh_basis(polar, azimuth):
    across = jnp.sin(polar)
    x = across * jnp.cos(azimuth)
    y = across * jnp.sin(azimuth)
    z = jnp.cos(polar)
    xx, yy, zz = x * x, y * y, z * z
    return [
        jnp.full_like(x, SH_ZERO),
        -SH_ONE * y,
        SH_ONE * z,
        -SH_ONE * x,
        SH_TWO[0] * x * y,
        SH_TWO[1] * y * z,
        SH_TWO[2] * (2.0 * zz - xx - yy),
        SH_TWO[3] * x * z,
        SH_TWO[4] * (xx - yy),
        SH_THREE[0] * y * (3.0 * xx - yy),
        SH_THREE[1] * x * y * z,
        SH_THREE[2] * y * (4.0 * zz - xx - yy),
        SH_THREE[3] * z * (2.0 * zz - 3.0 * xx - 3.0 * yy),
        SH_THREE[4] * x * (4.0 * zz - xx - yy),
        SH_THREE[5] * z * (xx - yy),
        SH_THREE[6] * x * (xx - 3.0 * yy),
    ]


def three_parts(values):
    high = values.astype(BF16).astype(F32)
    rest = values - high
    middle = rest.astype(BF16).astype(F32)
    return high, middle, rest - middle


def centre(mean):
    return mean * 32.0 - 16.5


def peers():
    return lax.axis_index("gs"), lax.axis_index("view")


def far_first(me):
    across = [((me // 16 + d) % 4) * 16 for d in range(4)]
    along = [((me // 2 + d) % 8) * 2 for d in range(8)]
    core = [me % 2, 1 - me % 2]
    steps = [(x, z, c) for x in range(4) for z in range(8) for c in range(2)]
    steps.sort(key=lambda s: (-min(s[0], 4 - s[0]) - min(s[1], 8 - s[1]), -s[2]))
    return [across[x] + along[z] + core[c] for x, z, c in steps if (x, z, c) != (0, 0, 0)]


def greet(between=()):
    me, view = peers()
    barrier = pltpu.get_barrier_semaphore()
    for n, other in enumerate(far_first(me)):
        if n == 16:
            for copy in between:
                copy.start()
        pl.semaphore_signal(barrier, inc=1, device_id=(other, view), device_id_type=MESH)
    for d in range(1, VIEWS):
        pl.semaphore_signal(barrier, inc=1, device_id=(me, lax.rem(view + d, VIEWS)), device_id_type=MESH)


def greeted():
    pl.semaphore_wait(pltpu.get_barrier_semaphore(), GS - 1 + VIEWS - 1)


def deal(sent, got, send_sem, recv_sem):
    me, view = peers()
    for other in far_first(me):
        pltpu.make_async_remote_copy(
            src_ref=sent.at[other],
            dst_ref=got.at[me],
            send_sem=send_sem,
            recv_sem=recv_sem,
            device_id=(other, view),
            device_id_type=MESH,
        ).start()


def spread_views(mine, got, send_sem, recv_sem):
    me, view = peers()
    for d in (2, 1, 3):
        pltpu.make_async_remote_copy(
            src_ref=mine,
            dst_ref=got.at[view],
            send_sem=send_sem,
            recv_sem=recv_sem,
            device_id=(me, lax.rem(view + d, VIEWS)),
            device_id_type=MESH,
        ).start()


def settle(whole, count, sem):
    part = whole.at[pl.ds(0, count)]
    pltpu.make_async_copy(part, part, sem).wait()


def pack_kernel(*refs):
    far, outs, rest = refs[:8], refs[8:15], refs[15:]
    arr_ref, angles_ref, own_ref, tgt, mono, step_s, sub_s = outs
    near, (out_ref, pay, sems, load_sems) = rest[:8], rest[8:]
    loads = [
        pltpu.make_async_copy(src, dst, load_sems.at[k]) for k, (src, dst) in enumerate(zip(far, near))
    ]
    greet(loads)
    for load in loads:
        load.wait()
    sh_ref, logit_ref, angle_ref, mean_ref, conic_ref, slot_ref, rank_ref, tgt_ref = near
    me, view = peers()
    angles_ref[view] = angle_ref[...]
    basis = sh_basis(angle_ref[0:1, :], angle_ref[1:2, :])
    colour = jnp.full((3, G), 0.5, F32)
    for k in range(16):
        colour = colour + sh_ref[3 * k : 3 * k + 3, :] * basis[k]
    m, n = centre(mean_ref[0:1, :]), centre(mean_ref[1:2, :])
    kept = [slot_ref[...].astype(F32), m, n] + [conic_ref[k] * (1.0 / 32.0) for k in range(3)]
    for k, row in enumerate(kept + [logit_ref[...]]):
        own_ref[k : k + 1, :] = row
    scale = LOG2E / 1024.0
    opacity = 0.99 * jax.nn.sigmoid(logit_ref[...])
    a, b, c = (conic_ref[k] * scale for k in range(3))
    pay[...] = jnp.zeros((SENT, G), F32)
    away = 0.5 * (a * m * m + 2.0 * b * m * n + c * n * n)
    pay[0:1, :] = (jnp.log(opacity) * LOG2E + SHIFT) - away
    pay[1:2, :] = a * m + b * n
    pay[2:3, :] = b * m + c * n
    pay[3:4, :] = -0.5 * a
    pay[4:5, :] = -b
    pay[5:6, :] = -0.5 * c
    pay[COL : COL + 3, :] = colour
    pay[KEY : KEY + 1, :] = (rank_ref[...] + 1).astype(F32)
    parts = three_parts(pay[...])
    slot = slot_ref[...]
    owner = jnp.where(iota((GS, G), 0) == (slot >> 5), 1.0, 0.0).astype(BF16)
    place = (slot & 31) - jnp.where(iota((2 * SENT, G), 0) >= SENT, 1, 0)
    total = jnp.zeros((GS, ROWS * 128), F32)
    for part in parts[::-1]:
        pair = jnp.concatenate([part, part], axis=0)
        spread = jnp.concatenate(
            [jnp.where(place == i, pair, 0.0) for i in range(0, QUADS * CAP, 2)], axis=0
        ).astype(BF16)
        total = total + lax.dot_general(
            owner, spread, (((1,), (1,)), ((), ())), preferred_element_type=F32
        )
    for r in range(ROWS):
        out_ref[:, r, :] = total[:, tile(r)]
    arr_ref[me] = out_ref[me]
    mono[...] = monomials()
    at = iota((PLACES, 128), 0)
    step_s[...] = (at >> 3).astype(F32)
    sub_s[...] = (at & 7).astype(F32)
    for q in range(QUADS):
        for c in range(3):
            for t in range(TILES):
                tgt[q, c * 8 + t : c * 8 + t + 1, :] = tgt_ref[c, q : q + 1, tile(t)]
    for q in range(QUADS):
        y = tgt[q, 0:24, :]
        means = window_means(jnp.concatenate([y, y * y], axis=0))
        tgt[q, 24:48, :] = means[0:24]
        tgt[q, 48:72, :] = means[24:48] - means[0:24] * means[0:24]
    greeted()
    deal(out_ref, arr_ref, sems.at[0], sems.at[1])
    spread_views(angle_ref, angles_ref, sems.at[2], sems.at[3])
    settle(arr_ref, GS - 1, sems.at[1])
    settle(angles_ref, VIEWS - 1, sems.at[3])
    settle(arr_ref, GS - 1, sems.at[0])
    settle(angles_ref, VIEWS - 1, sems.at[2])


def monomials():
    lane = iota((WIDE, 128), 1)
    row = iota((WIDE, 128), 0)
    u = ((lane & 31) - 16).astype(F32)
    top = ((lane >> 5) - 16).astype(F32)

    def rows(entries):
        out = jnp.zeros((WIDE, 128), F32)
        for k, value in entries.items():
            out = jnp.where(row == k, value, out)
        return out

    def power(w):
        return rows({0: 1.0, 1: u, 2: w, 3: u * u, 4: u * w, 5: w * w})

    def first(w):
        return rows({2: 4.0, 4: 4.0 * u, 5: 8.0 * w + 16.0})

    tiles = []
    for h in range(PASSES):
        tiles += [power(top + 4.0 * HALF * h), first(top + 4.0 * HALF * h)]
    tiles.append(rows({5: 32.0}))
    tiles += [rows({COL + c: 1.0}) for c in range(3)]
    base = jnp.concatenate(tiles, axis=1)
    shift = jnp.where(
        (iota((WIDE, 128), 0) == 0) & (iota((WIDE, 128), 1) >= 0), -SHIFT, 0.0
    )
    none = jnp.zeros((WIDE, 128), F32)
    shift = jnp.concatenate([shift, none] * PASSES + [none] * 4, axis=1)
    return jnp.concatenate([base, base, base, shift], axis=0).astype(BF16)


def window_means(values):
    lane = iota((128, 128), 1)
    other = iota((128, 128), 0)
    same = ((lane & 31) >> 2) == ((other & 31) >> 2)
    pool = jnp.where(same, 1.0 / 16.0, 0.0).astype(BF16)
    rows = values.shape[0]
    sums = jnp.dot(
        jnp.concatenate(three_parts(values), axis=0).astype(BF16), pool, preferred_element_type=F32
    )
    return (sums[2 * rows :] + sums[rows : 2 * rows]) + sums[0:rows]


def loss_slope(x, y, my, vy):
    rows = x.shape[0]
    means = window_means(jnp.concatenate([x, x * x, x * y], axis=0))
    mx, exx, exy = (means[k * rows : (k + 1) * rows] for k in range(3))
    n1 = 2.0 * mx * my + SSIM_MEAN
    n2 = 2.0 * (exy - mx * my) + SSIM_SPREAD
    d1 = mx * mx + my * my + SSIM_MEAN
    d2 = (exx - mx * mx) + vy + SSIM_SPREAD
    i1, i2 = 1.0 / d1, 1.0 / d2
    both = i1 * i2
    ratio = n1 * n2 * both
    by_mean = 2.0 * my * (n2 - n1) * both + 2.0 * mx * ratio * (i2 - i1)
    by_square = -ratio * i2
    by_cross = 2.0 * n1 * both
    return 0.1 * (x - y) - (0.2 / 16.0) * (by_mean + 2.0 * x * by_square + y * by_cross)


def shifted(values, by, fill):
    sub = iota(values.shape, 0)
    keep = (sub >= by) if by > 0 else (sub < 8 + by)
    return jnp.where(keep, pltpu.roll(values, by % 8, 0), fill)


def order(blocks, arrived, perm, bc, mono, step_s, sub_s):
    pick = jnp.where((iota((3 * WIDE, 128), 0) & 15) == KEY, 1.0, 0.0).astype(BF16)
    turned = jnp.concatenate([arrived[:, r, :].T for r in range(ROWS)], axis=0)
    rest = jnp.zeros((WIDE - SENT, PLACES), F32)
    packed = []
    for q in blocks:
        places = [turned[i * SENT : (i + 1) * SENT, :] for i in range(q * CAP, (q + 1) * CAP)]
        packed.append(jnp.concatenate([jnp.concatenate(places, axis=1), rest], axis=0))
    parts = [jnp.concatenate(three_parts(p), axis=0).astype(BF16) for p in packed]
    keys = [p[KEY : KEY + 1, :] for p in packed]
    columns = [
        lax.dot_general(p, pick, (((0,), (0,)), ((), ())), preferred_element_type=F32) for p in parts
    ]
    filled = [jnp.sum(jnp.where(k > 0.0, 1.0, 0.0), axis=1, keepdims=True) for k in keys]
    turns = [jnp.floor((f + (8 * UNROLL - 1.0)) * (1.0 / (8 * UNROLL))) for f in filled]
    step, sub = step_s[...], sub_s[...]
    for q, key, column, turn, full in zip(blocks, keys, columns, turns, filled):
        span = turn * UNROLL
        wanted = jnp.where(step < span, sub * span + step + (PLACES - full), -1.0)
        for t in range(PLACES // 128):
            less = jnp.where(column < key[:, tile(t)], 1.0, 0.0)
            rank = jnp.sum(less, axis=0, keepdims=True)
            perm[q, :, tile(t)] = jnp.where(rank == wanted, 1.0, 0.0).astype(BF16)
    ordered = [
        lax.dot_general(p, perm[q], (((1,), (1,)), ((), ())), preferred_element_type=F32)
        for q, p in zip(blocks, parts)
    ]
    ones = jnp.ones((WIDE, PLACES), F32)
    ordered = [jnp.concatenate([o, ones], axis=0).astype(BF16) for o in ordered]
    for q, o in zip(blocks, ordered):
        bc[q] = lax.dot_general(o, mono[...], (((0,), (0,)), ((), ())), preferred_element_type=F32)
    return turns


def unroll_loop(run, body, start):
    def several(i, state):
        for k in range(UNROLL):
            state = body(i * UNROLL + k, state)
        return state

    return lax.fori_loop(0, run // UNROLL, several, start)


def tile(t):
    return slice(t * 128, (t + 1) * 128)


def blend(run, bc, a_s, w_s, col, left, seen):
    one = jnp.ones((8, 128), F32)
    zero = jnp.zeros((8, 128), F32)
    for h in range(PASSES):

        def ahead(i, state, h=h):
            passing, got = list(state[0]), [list(s) for s in state[1]]
            rows = pl.ds(pl.multiple_of(i * 8, 8), 8)
            power, first = bc[rows, tile(2 * h)], bc[rows, tile(2 * h + 1)]
            second = bc[rows, tile(2 * PASSES)]
            colours = [bc[rows, tile(2 * PASSES + 1 + c)] for c in range(3)]
            if h == 0 and col is not None:
                for c in range(3):
                    col[rows, tile(c)] = colours[c]
            for t in range(HALF):
                alpha = jnp.exp2(power)
                weight = passing[t] * alpha
                passing[t] = passing[t] - weight
                a_s[rows, tile(h * HALF + t)] = alpha
                w_s[rows, tile(h * HALF + t)] = weight
                for c in range(3):
                    got[c][t] = got[c][t] + colours[c] * weight
                if t < HALF - 1:
                    power = power + first
                    first = first + second
            return tuple(passing), tuple(tuple(s) for s in got)

        passing, got = unroll_loop(run, ahead, ((one,) * HALF, ((zero,) * HALF,) * 3))
        for t in range(HALF):
            left[:, tile(h * HALF + t)] = passing[t]
            for c in range(3):
                seen[c, :, tile(h * HALF + t)] = got[c][t]


def back_step(i, later, a_s, w_s, col, tg, red):
    zero = jnp.zeros((8, 128), F32)
    later = list(later)
    rows = pl.ds(pl.multiple_of(i * 8, 8), 8)
    c0, c1, c2 = (col[rows, tile(c)] for c in range(3))
    plain, graded = zero, zero
    sums = [zero, zero, zero]
    for t in range(TILES - 1, -1, -1):
        alpha, weight = a_s[rows, tile(t)], w_s[rows, tile(t)]
        g0, g1, g2 = (tg[c, :, tile(t)] for c in range(3))
        gap = c0 * g0 + c1 * g1 + c2 * g2 - later[t]
        later[t] = later[t] + alpha * gap
        plain = plain + weight * gap
        if t:
            graded = graded + plain
        sums = [sums[0] + weight * g0, sums[1] + weight * g1, sums[2] + weight * g2]
    for k, value in enumerate(sums + [plain, graded]):
        red[rows, tile(k)] = value
    return tuple(later)


def backward(run, a_s, w_s, col, tg, later, red):
    def back(i, state):
        return back_step(run - 1 - i, state, a_s, w_s, col, tg, red)

    unroll_loop(run, back, tuple(later[:, tile(t)] for t in range(TILES)))


def backward_whole(runs, a_s, w_s, col, tg, later, red):
    steps = PLACES // 8
    begin = tuple(later[:, tile(t)] for t in range(TILES))
    last = runs[...] * (1.0 / 8.0) - 1.0

    def several(n, state):
        for k in range(8):
            i = steps - 1 - (n * 8 + k)
            here = last == i.astype(F32)
            state = [jnp.where(here, b, v) for b, v in zip(begin, state)]
            state = back_step(i, state, a_s, w_s, col, tg, red)
        return tuple(state)

    lax.fori_loop(0, steps // 8, several, begin)


def join(left, seen, pic, slope, tgt, tg, later, image):
    before = shifted(left[...], 1, 1.0)
    for by in (1, 2, 4):
        before = before * shifted(before, by, 1.0)
    for c in range(3):
        row = jnp.sum(before * seen[c], axis=0, keepdims=True)
        image[c : c + 1, :] = row
        for t in range(TILES):
            pic[c * 8 + t : c * 8 + t + 1, :] = row[:, tile(t)]
    slope[...] = loss_slope(pic[...], *(tgt[24 * k : 24 * k + 24, :] for k in range(3)))
    behind = jnp.zeros((8, PIX), F32)
    for c in range(3):
        row = jnp.concatenate([slope[c * 8 + t : c * 8 + t + 1, :] for t in range(TILES)], axis=1)
        behind = behind + row * seen[c]
        tg[c] = before * row
    value, factor = shifted(behind, -1, 0.0), shifted(left[...], -1, 0.0)
    for by in (1, 2, 4):
        value = value + factor * shifted(value, -by, 0.0)
        factor = factor * shifted(factor, -by, 0.0)
    later[...] = before * value


def render_kernel(
    arr_ref, tgt, mono, step_s, sub_s,
    img_ref, red, perm, runs, largest, a_last, w_last, col_last, tg_last, later_last,
    bc, a_s, w_s, tg, later, left, seen, pic, slope, image, runs_s
):
    found = order(list(range(QUADS)), arr_ref, perm, bc, mono, step_s, sub_s)
    for q, turn in enumerate(found):
        runs_s[q] = jnp.sum(turn).astype(jnp.int32) * UNROLL
    best = jnp.int32(0)
    for q in range(1, QUADS):
        best = jnp.where(runs_s[q] > runs_s[best], q, best)
    last = QUADS - 1
    largest[...] = jnp.full((8, 128), best, jnp.int32).astype(F32)

    def block(at):
        return jnp.where(at == best, last, jnp.where(at == last, best, at))

    def first(at, carry):
        q = block(at)
        blend(runs_s[q], bc.at[q], a_s.at[at], w_s.at[at], None, left.at[at], seen.at[at])
        return carry

    def second(at, carry):
        q = block(at)
        col = bc.at[q, :, pl.ds((2 * PASSES + 1) * 128, 3 * 128)]
        backward(runs_s[q], a_s.at[at], w_s.at[at], col, tg.at[at], later.at[at], red.at[at])
        return carry

    lax.fori_loop(0, last, first, 0)
    blend(runs_s[best], bc.at[best], a_last, w_last, col_last, left.at[last], seen.at[last])
    for at in range(QUADS):
        q = block(at)
        runs[at] = jnp.full((8, 128), 8 * runs_s[q], jnp.int32).astype(F32)
        to = (tg_last, later_last) if at == last else (tg.at[at], later.at[at])
        join(left.at[at], seen.at[at], pic.at[at], slope.at[at], tgt.at[q], *to, image.at[q])
    lax.fori_loop(0, last, second, 0)
    for q in range(QUADS):
        for c in range(3):
            img_ref[c, q : q + 1, :] = image[q, c : c + 1, :]


def reduced(red, runs):
    pixel = iota((128, 128), 0)
    across = ((pixel & 31) - 16).astype(F32)
    down = ((pixel >> 5) - 16).astype(F32)
    row = iota((BACK, PLACES), 1).astype(F32)
    colour = red[:, 0 : 3 * 128]
    high = colour.astype(BF16)
    low = (colour - high.astype(F32)).astype(BF16)
    pick = jnp.where(iota((BACK, 3 * 128), 1) >> 7 == iota((BACK, 3 * 128), 0), 1.0, 0.0).astype(BF16)
    nt = (((1,), (1,)), ((), ()))
    sums = lax.dot_general(
        jnp.concatenate([pick, pick], axis=1),
        jnp.concatenate([low, high], axis=1),
        nt,
        preferred_element_type=F32,
    )
    groups = []
    for n in range(PLACES // 128):
        plain, graded = (red[tile(n), tile(k)].T for k in (3, 4))
        moved = (plain * across, plain * down + 4.0 * graded, plain)
        moved = [jnp.sum(value, axis=0, keepdims=True) for value in moved]
        groups.append(jnp.concatenate(moved, axis=0))
    sums = jnp.concatenate(
        [sums[0:3], jnp.concatenate(groups, axis=1), jnp.zeros((BACK - 6, PLACES), F32)], axis=0
    )
    return jnp.where(row < runs[0:1, 0:1], sums, 0.0)


def send_back(red, perm, runs, largest, a_s, w_s, col, tg, later, sent, red_last, sums_s):
    last = QUADS - 1
    for at in range(last):
        sums_s[at] = reduced(red.at[at], runs.at[at])
    backward_whole(
        runs.at[last], a_s, w_s, col, tg, later, red_last
    )
    sums = [sums_s[at] for at in range(last)] + [reduced(red_last, runs.at[last])]
    swap = [largest[:, 0:1] == float(q) for q in range(last)]
    moved = sums[last]
    for q in range(last):
        moved = jnp.where(swap[q], sums[q], moved)
    sums = [jnp.where(swap[q], sums[last], sums[q]) for q in range(last)] + [moved]
    parts = [jnp.concatenate(three_parts(p), axis=0).astype(BF16) for p in sums]
    placed = [jnp.dot(p, perm[q], preferred_element_type=F32) for q, p in enumerate(parts)]
    placed = [(p[2 * BACK :] + p[BACK : 2 * BACK]) + p[0:BACK] for p in placed]
    back = [jnp.concatenate([p[:, c * GS : (c + 1) * GS] for c in range(CAP)], axis=0).T for p in placed]
    for j in range(QUADS // 2):
        sent[:, j, :] = jnp.concatenate([back[2 * j], back[2 * j + 1]], axis=1)


def unpack_kernel(
    red, perm, runs, largest, a_s, w_s, col, tg, later, own_ref, angles_ref, parts_ref, move_ref, basis_ref,
    sent_ref, red_last, sums_s, ret_ref, part_ref, sems
):
    greet()
    me, view = peers()
    send_back(red, perm, runs, largest, a_s, w_s, col, tg, later, sent_ref, red_last, sums_s)
    ret_ref[me] = sent_ref[me]
    slot = own_ref[0:1, :].astype(jnp.int32)
    owner = jnp.where(iota((GS, G), 0) == (slot >> 5), 1.0, 0.0).astype(BF16)
    owner = jnp.concatenate([owner] * 3, axis=0)
    place = slot & 31
    greeted()
    deal(sent_ref, ret_ref, sems.at[0], sems.at[1])
    polar = jnp.concatenate([angles_ref[v, 0:1, :] for v in range(VIEWS)], axis=0)
    azimuth = jnp.concatenate([angles_ref[v, 1:2, :] for v in range(VIEWS)], axis=0)
    for k, values in enumerate(sh_basis(polar, azimuth)):
        for v in range(VIEWS):
            basis_ref[v, 3 * k : 3 * k + 3, :] = jnp.broadcast_to(values[v : v + 1, :], (3, G))
    settle(ret_ref, GS - 1, sems.at[1])
    both = jnp.concatenate([ret_ref[:, j, :] for j in range(QUADS // 2)], axis=1)
    parts = jnp.concatenate(three_parts(both), axis=0).astype(BF16)
    spread = lax.dot_general(parts, owner, (((0,), (0,)), ((), ())), preferred_element_type=F32)
    found = [spread[i * BACK : (i + 1) * BACK, :] for i in range(QUADS * CAP)]
    for bit in range(5):
        odd = ((place >> bit) & 1) == 1
        found = [jnp.where(odd, found[i + 1], found[i]) for i in range(0, len(found), 2)]
    total = found[0]
    m, n, a, b, c = (own_ref[k : k + 1, :] for k in range(1, 6))
    plain = total[5:6, :]
    du = total[3:4, :] - m * plain
    dw = total[4:5, :] - n * plain
    part_ref[0:3, :] = total[0:3, :]
    part_ref[3:4, :] = plain
    spread_views(part_ref, parts_ref, sems.at[2], sems.at[3])
    parts_ref[view] = part_ref[...]
    move_ref[0:1, :] = a * du + b * dw
    move_ref[1:2, :] = b * du + c * dw
    settle(parts_ref, VIEWS - 1, sems.at[3])
    settle(ret_ref, GS - 1, sems.at[0])
    settle(parts_ref, VIEWS - 1, sems.at[2])


def final_kernel(part_ref, move_ref, basis_ref, own_ref, image_ref, sh_ref, logit_grad_ref, mean_grad_ref, img_ref):
    mean_grad_ref[...] = move_ref[...]
    img_ref[...] = image_ref[...]
    plain = part_ref[0, 3:4, :]
    for v in range(1, VIEWS):
        plain = plain + part_ref[v, 3:4, :]
    logit_grad_ref[...] = plain * (1.0 - jax.nn.sigmoid(own_ref[6:7, :]))
    colours = [jnp.concatenate([part_ref[v, 0:3, :]] * 8, axis=0) for v in range(VIEWS)]
    for half in (slice(0, 24), slice(24, 48)):
        total = colours[0] * basis_ref[0, half, :]
        for v in range(1, VIEWS):
            total = total + colours[v] * basis_ref[v, half, :]
        sh_ref[half, :] = total


MESH = pl.DeviceIdType.MESH
VM = pl.BlockSpec(memory_space=pltpu.VMEM)


def call(kernel, ins, outs, scratch=(), limit=20, remote=None, far=False):
    extra = {} if remote is None else dict(collective_id=remote, has_side_effects=True)
    shapes = [o if isinstance(o, jax.ShapeDtypeStruct) else jax.ShapeDtypeStruct(o, F32) for o in outs]
    return pl.pallas_call(
        kernel,
        out_shape=shapes,
        in_specs=[pl.BlockSpec(memory_space=pltpu.HBM) if far else VM] * len(ins),
        out_specs=[VM] * len(shapes),
        scratch_shapes=list(scratch),
        compiler_params=pltpu.CompilerParams(vmem_limit_bytes=limit * 2**20, **extra),
    )(*ins)


def pack(*ins):
    return call(
        pack_kernel,
        [pltpu.with_memory_space_constraint(i, pltpu.HBM) for i in ins],
        [
            (GS, ROWS, 128),
            (VIEWS, 2, G),
            (OWN, G),
            (QUADS, 72, 128),
            jax.ShapeDtypeStruct((4 * WIDE, FORMS * 128), BF16),
            (PLACES, 128),
            (PLACES, 128),
        ],
        [pltpu.VMEM(i.shape, i.dtype) for i in ins]
        + [
            pltpu.VMEM((GS, ROWS, 128), F32),
            pltpu.VMEM((SENT, G), F32),
            pltpu.SemaphoreType.DMA((4,)),
            pltpu.SemaphoreType.DMA((len(ins),)),
        ],
        remote=0,
        far=True,
    )


def render(*ins):
    return call(
        render_kernel,
        ins,
        [
            (3, QUADS, PIX),
            (QUADS - 1, PLACES, 5 * 128),
            jax.ShapeDtypeStruct((QUADS, PLACES, PLACES), BF16),
            (QUADS, 8, 128),
            (8, 128),
            (PLACES, PIX),
            (PLACES, PIX),
            (PLACES, 3 * 128),
            (3, 8, PIX),
            (8, PIX),
        ],
        [
            pltpu.VMEM((QUADS, PLACES, FORMS * 128), F32),
            pltpu.VMEM((QUADS - 1, PLACES, PIX), F32),
            pltpu.VMEM((QUADS - 1, PLACES, PIX), F32),
            pltpu.VMEM((QUADS - 1, 3, 8, PIX), F32),
            pltpu.VMEM((QUADS - 1, 8, PIX), F32),
            pltpu.VMEM((QUADS, 8, PIX), F32),
            pltpu.VMEM((QUADS, 3, 8, PIX), F32),
            pltpu.VMEM((QUADS, 24, 128), F32),
            pltpu.VMEM((QUADS, 24, 128), F32),
            pltpu.VMEM((QUADS, 3, PIX), F32),
            pltpu.SMEM((QUADS,), jnp.int32),
        ],
        limit=RENDER_MIB,
    )


def unpack(*ins):
    return call(
        unpack_kernel,
        ins,
        [(VIEWS, 4, G), (2, G), (VIEWS, 48, G)],
        [
            pltpu.VMEM((GS, QUADS // 2, 128), F32),
            pltpu.VMEM((PLACES, 5 * 128), F32),
            pltpu.VMEM((QUADS - 1, BACK, PLACES), F32),
            pltpu.VMEM((GS, QUADS // 2, 128), F32),
            pltpu.VMEM((4, G), F32),
            pltpu.SemaphoreType.DMA((4,)),
        ],
        limit=UNPACK_MIB,
        remote=1,
    )


def final(*ins):
    return call(final_kernel, ins, [(48, G), (1, G), (2, G), (3, QUADS, PIX)])


def local(sh_coef, opacity_logit, view_angle, mean_pos, conic, send_slot, depth_rank, target):
    arrived, angles, own, *prepared = pack(
        sh_coef,
        opacity_logit.reshape(1, G),
        view_angle[0],
        mean_pos[0],
        jnp.transpose(conic, (1, 0, 2)),
        send_slot,
        depth_rank,
        jnp.transpose(target[0], (1, 0, 2)),
    )
    images, *blended = render(arrived, *prepared)
    parts, move, basis = unpack(*blended, own, angles)
    sh_grad, logit_grad, mean_grad, images = final(parts, move, basis, own, images)
    return (sh_grad, logit_grad.reshape(G), mean_grad[None], jnp.transpose(images, (1, 0, 2))[None])


def solution(mesh):
    return jax.shard_map(
        local,
        mesh=mesh,
        in_specs=(
            P(None, "gs"),
            P("gs"),
            P("view", None, "gs"),
            P("view", None, "gs"),
            P("view", None, "gs"),
            P("view", "gs"),
            P("view", "gs"),
            P("view", "gs", None, None),
        ),
        out_specs=(P(None, "gs"), P("gs"), P("view", None, "gs"), P("view", "gs", None, None)),
        check_vma=False,
    )
```
